32 devices in a mesh: dp: 4 (over x, core), expert: 8 (over z, y).
Axes of the slice: x: 2, y: 2, z: 4, core: 2. Of those that a mesh axis runs over, the one named last changes fastest.
Arguments:
- tokens: bfloat16 [4096, 1024], P(('dp', 'expert')), may hold values from -6 to 6
- context: bfloat16 [4096, 1024], P(('dp', 'expert')), may hold values from -6 to 6
- w_out: bfloat16 [1024, 1024], replicated, may hold values from -0.1875 to 0.1875
- w_router: bfloat16 [1024, 8], replicated, may hold values from -0.1875 to 0.1875
- expert_ids: int32 [4096, 2], P(('dp', 'expert')), may hold values from 0 to 7, as said below
- w_in: bfloat16 [8, 1024, 4096], P('expert', None, 'dp'), may hold values from -0.1875 to 0.1875
- w_down: bfloat16 [8, 4096, 1024], P('expert', 'dp'), may hold values from -0.09375 to 0.09375
- cotangent: bfloat16 [4096, 1024], P(('dp', 'expert')), may hold values from -6 to 6
Outputs:
- output: bfloat16 [4096, 1024], P(('dp', 'expert'))
- grad_tokens: bfloat16 [4096, 1024], P(('dp', 'expert'))
- grad_context: bfloat16 [4096, 1024], P(('dp', 'expert'))
- grad_w_out: float32 [1024, 1024], P('expert')
- grad_w_router: float32 [1024, 8], P(None, 'expert')
- grad_w_in: bfloat16 [8, 1024, 4096], P('expert', None, 'dp')
- grad_w_down: bfloat16 [8, 4096, 1024], P('expert', 'dp')
The draws below stay inside these ranges and needn't reach their ends.
Inputs may be any that keep to these rules, and one draw needn't show every extreme that they name: `expert_ids`: the two experts of a row differ; among the 128 rows of one device every expert is named exactly 32 times.
All inputs are finite; a program needn't handle non-finite values.
Results may differ from the reference program's by a relative error of at most 0.02.
Values may be sent and summed in bfloat16 or wider, within the bound.
No kernel may reach another device: no remote copies, remote signals or barrier semaphores. Data moves between devices by JAX's collectives and lax.ppermute only.
A program may use at most 128 MiB of HBM per device.

```python
import jax
import jax.numpy as jnp
from jax import lax

D = 1024
HID = 4096
TOK_DEV = 128
EXPERTS = 8
TOKENS = 4096


def draw_expert_ids(key, part):
    blocks = TOKENS // TOK_DEV
    rounds = TOK_DEV // EXPERTS
    key_tau, key_swap, key_place = jax.random.split(jax.random.fold_in(key, 7), 3)
    tau_keys = jax.random.split(key_tau, blocks * rounds)
    taus = jax.vmap(lambda single: jax.random.permutation(single, EXPERTS))(tau_keys).astype(jnp.int32)
    taus = taus.reshape(blocks, rounds, EXPERTS)
    first_ids = taus.reshape(blocks, TOK_DEV)
    second_ids = jnp.roll(taus, -1, axis=2).reshape(blocks, TOK_DEV)
    swapped = jax.random.randint(key_swap, (blocks, TOK_DEV), 0, 2).astype(jnp.int32)
    column_a = jnp.where(swapped == 1, second_ids, first_ids)
    column_b = jnp.where(swapped == 1, first_ids, second_ids)
    paired = jnp.stack([column_a, column_b], axis=2)
    place_keys = jax.random.split(key_place, blocks)
    placement = jax.vmap(lambda single: jax.random.permutation(single, TOK_DEV))(place_keys).astype(jnp.int32)
    inverse = jnp.argsort(placement, axis=1).astype(jnp.int32)
    placed = jnp.take_along_axis(paired, inverse[:, :, None], axis=1)
    return placed.reshape(TOKENS, 2).astype(jnp.int32)


def spiked(entries, key, source, target, parts, factor):
    def block_of(position):
        return (jnp.arange(entries.shape[position]) // (entries.shape[position] // parts)).reshape((-1,) + (1,) * (entries.ndim - 1 - position))

    first = jax.random.permutation(key, parts)[block_of(target)]
    second = (block_of(target) + parts // 2) % parts
    return jnp.where((block_of(source) == first) | (block_of(source) == second), factor * entries, entries)


def block_levels(key, dims, pieces, smallest, top_value):
    loudness, own = 1.0, jax.random.fold_in(key, 6)
    for dim, shards_of in pieces:
        draws = jnp.exp(jax.random.uniform(jax.random.fold_in(own, dim), (shards_of,), jnp.float32, smallest / len(pieces), top_value / len(pieces)))
        loudness = loudness * jnp.repeat(draws, dims[dim] // shards_of).reshape([-1 if axis == dim else 1 for axis in range(len(dims))])
    return loudness


def noise(rng, shape, deviation, limit, pieces=(), held_as=jnp.bfloat16):
    entries = deviation * jax.random.normal(rng, shape, jnp.float32)
    if pieces:
        entries = entries * block_levels(rng, shape, pieces, -0.22, 0.18)
    return jnp.clip(entries, -limit, limit).astype(held_as)


def heavy_noise(own_key, shape, scale, bound, cuts, heavy, held_as=jnp.bfloat16):
    drawn = scale * jax.random.normal(own_key, shape, jnp.float32)
    if cuts:
        drawn = drawn * block_levels(own_key, shape, cuts, -0.22, 0.18)
    return jnp.clip(spiked(drawn, jax.random.fold_in(own_key, 3), *heavy), -bound, bound).astype(held_as)


def setup_inputs(seed: int = 0) -> dict:
    seeds = jax.random.split(jax.random.key(seed), 9)
    tokens = noise(seeds[0], (TOKENS, D), 1.0, 6.0, ((0, 32),))
    context = heavy_noise(seeds[1], (TOKENS, D), 1.0, 6.0, ((0, 32),), (0, 1, 32, 2.75))
    w_out = noise(seeds[2], (D, D), D ** -0.5, 0.1875)
    w_router = noise(seeds[3], (D, EXPERTS), D ** -0.5, 0.1875)
    expert_ids = draw_expert_ids(jax.random.fold_in(seeds[8], 71), 0)
    w_in = noise(seeds[5], (EXPERTS, D, HID), D ** -0.5, 0.1875, ((0, 8), (2, 4)))
    w_down = noise(seeds[6], (EXPERTS, HID, D), HID ** -0.5, 0.09375, ((0, 8), (1, 4)))
    cotangent = noise(seeds[7], (TOKENS, D), 1.0, 6.0, ((0, 32),))
    return {"tokens": tokens, "context": context, "w_out": w_out, "w_router": w_router, "expert_ids": expert_ids, "w_in": w_in, "w_down": w_down, "cotangent": cotangent}


GELU_C = 0.7978845608028654
GELU_A = 0.044715
EPSILON = 1e-06

def gelu_pair(preact):
    cubed_in = preact * preact * preact
    tangent = jnp.tanh(GELU_C * (preact + GELU_A * cubed_in))
    gelu_value = 0.5 * preact * (1.0 + tangent)
    derivative = 0.5 * (1.0 + tangent) + 0.5 * preact * (1.0 - tangent * tangent) * GELU_C * (1.0 + 3.0 * GELU_A * preact * preact)
    return (gelu_value, derivative)

def reference(tokens, context, w_out, w_router, expert_ids, w_in, w_down, cotangent):
    attn_out = jnp.dot(context, w_out, preferred_element_type=jnp.float32)
    residual = (tokens.astype(jnp.float32) + attn_out).astype(jnp.bfloat16)
    resid_f = residual.astype(jnp.float32)
    inv_rms = lax.rsqrt(lax.optimization_barrier(jnp.mean(resid_f * resid_f, axis=1, keepdims=True)) + EPSILON)
    normed = (resid_f * inv_rms).astype(jnp.bfloat16)
    logits = jnp.dot(normed, w_router, preferred_element_type=jnp.float32)
    picked = jnp.take_along_axis(logits, expert_ids, axis=1)
    gates = jax.nn.sigmoid(picked)
    cot_f = cotangent.astype(jnp.float32)
    slot_grads = (gates[:, :, None] * cot_f[:, None, :]).astype(jnp.bfloat16).reshape(-1, D)
    flat_ids = expert_ids.reshape(-1)
    per_expert = 2 * TOKENS // EXPERTS

    def one_expert(expert):
        chosen = jnp.nonzero(flat_ids == expert, size=per_expert)[0].astype(jnp.int32)
        rows_in = normed[chosen // 2]
        rows_grad = slot_grads[chosen]
        weight_in = w_in[expert]
        weight_down = w_down[expert]
        preact = jnp.dot(rows_in, weight_in, preferred_element_type=jnp.float32)
        gelu_value, derivative = gelu_pair(preact)
        activated = gelu_value.astype(jnp.bfloat16)
        expert_out = jnp.dot(activated, weight_down, preferred_element_type=jnp.float32).astype(jnp.bfloat16)
        act_grad = jnp.dot(rows_grad, weight_down.T, preferred_element_type=jnp.float32)
        pre_grad = (act_grad * derivative).astype(jnp.bfloat16)
        grad_down = jnp.dot(activated.T, rows_grad, preferred_element_type=jnp.float32).astype(jnp.bfloat16)
        grad_in = jnp.dot(rows_in.T, pre_grad, preferred_element_type=jnp.float32).astype(jnp.bfloat16)
        input_grad = jnp.dot(pre_grad, weight_in.T, preferred_element_type=jnp.float32).astype(jnp.bfloat16)
        return (chosen, expert_out, input_grad, grad_in, grad_down)
    chosen, expert_out, input_grad, grad_w_in, grad_w_down = lax.map(one_expert, jnp.arange(EXPERTS, dtype=jnp.int32))
    order = chosen.reshape(-1)
    slot_out = jnp.zeros((2 * TOKENS, D), jnp.bfloat16).at[order].set(expert_out.reshape(-1, D)).reshape(TOKENS, 2, D)
    slot_in_grad = jnp.zeros((2 * TOKENS, D), jnp.bfloat16).at[order].set(input_grad.reshape(-1, D)).reshape(TOKENS, 2, D)
    slot_out_f = slot_out.astype(jnp.float32)
    combined = resid_f + lax.optimization_barrier(jnp.sum(gates[:, :, None] * slot_out_f, axis=1))
    output = combined.astype(jnp.bfloat16)
    gate_grad = lax.optimization_barrier(jnp.sum(cot_f[:, None, :] * slot_out_f, axis=2))
    logit_grad = gate_grad * gates * (1.0 - gates)
    onehot_ids = (expert_ids[:, :, None] == jnp.arange(EXPERTS, dtype=jnp.int32)[None, None, :]).astype(jnp.float32)
    logit_table = lax.optimization_barrier(jnp.sum(onehot_ids * logit_grad[:, :, None], axis=1)).astype(jnp.bfloat16)
    normed_grad = lax.optimization_barrier(jnp.sum(slot_in_grad.astype(jnp.float32), axis=1)) + jnp.dot(logit_table, w_router.T, preferred_element_type=jnp.float32)
    mean_term = lax.optimization_barrier(jnp.mean(normed_grad * resid_f, axis=1, keepdims=True))
    resid_grad = inv_rms * normed_grad - inv_rms * inv_rms * inv_rms * resid_f * mean_term
    grad_tokens = (cot_f + resid_grad).astype(jnp.bfloat16)
    grad_context = jnp.dot(grad_tokens, w_out.T, preferred_element_type=jnp.float32).astype(jnp.bfloat16)
    grad_w_out = jnp.dot(context.T, grad_tokens, preferred_element_type=jnp.float32)
    grad_w_router = jnp.dot(normed.T, logit_table, preferred_element_type=jnp.float32)
    return (output, grad_tokens, grad_context, grad_w_out, grad_w_router, grad_w_in, grad_w_down)
```

```python
import functools

import jax
import jax.numpy as jnp
from jax import lax
from jax.experimental import pallas as pl
from jax.experimental.pallas import tpu as pltpu
from jax.sharding import PartitionSpec as P

GELU_C = 0.7978845608028654
GELU_A = 0.044715
EPSILON = 1e-06
BF = jnp.bfloat16
F32 = jnp.float32
LANES = 128
VMEM_BYTES = 40 * 1024 * 1024

NN = (((1,), (0,)), ((), ()))
NT = (((1,), (1,)), ((), ()))
TN = (((0,), (0,)), ((), ()))


def mm(a, b, dims=NN):
    return lax.dot_general(a, b, dims, preferred_element_type=F32)


def gelu_pair(preact):
    square = preact * preact
    tangent = jnp.tanh(GELU_C * (preact + GELU_A * (square * preact)))
    half = 0.5 * (1.0 + tangent)
    derivative = half + (0.5 * GELU_C) * preact * (1.0 - tangent * tangent) * (
        1.0 + 3.0 * GELU_A * square
    )
    return preact * half, derivative


def call(body, outs, args, specs=None, out_specs=None, grid=(), scratch=(), flops=0, moved=0, name=None):
    whole = pl.BlockSpec(memory_space=pltpu.VMEM)
    return pl.pallas_call(
        body,
        out_shape=outs,
        grid=grid,
        in_specs=specs if specs is not None else [whole] * len(args),
        out_specs=out_specs if out_specs is not None else [whole] * len(outs),
        scratch_shapes=scratch,
        compiler_params=pltpu.CompilerParams(vmem_limit_bytes=VMEM_BYTES),
        cost_estimate=pl.CostEstimate(flops=flops, bytes_accessed=moved, transcendentals=0),
        name=name,
    )(*args)


def shape(dims, dtype=BF):
    return jax.ShapeDtypeStruct(dims, dtype)


def onehot(column, width):
    lanes = lax.broadcasted_iota(jnp.int32, (column.shape[0], width), 1)
    return (lanes == column).astype(F32)


def place_body(me_ref, ids_ref, cot_ref, placed_ref, send_ref, *, capacity):
    tok = ids_ref.shape[0]
    rows = lax.broadcasted_iota(jnp.int32, (tok, tok), 0)
    cols = lax.broadcasted_iota(jnp.int32, (tok, tok), 1)
    lower = (cols < rows).astype(BF)
    rel = [ids_ref[:, k : k + 1] ^ me_ref[0] for k in range(2)]
    hot = [onehot(r, LANES) for r in rel]
    before = [mm(lower, h.astype(BF)) for h in hot]
    rank_0 = jnp.sum(before[0] * hot[0], axis=1, keepdims=True)
    first = jnp.sum(hot[0], axis=0, keepdims=True)
    rank_1 = jnp.sum((before[1] + first) * hot[1], axis=1, keepdims=True)
    spot = [r * capacity + q.astype(jnp.int32) for r, q in zip(rel, (rank_0, rank_1))]
    for k in range(2):
        placed_ref[:, k : k + 1] = spot[k]
    where = onehot(spot[0], 2 * tok) + onehot(spot[1], 2 * tok)
    send_ref[...] = mm(where.astype(BF), cot_ref[...], TN).astype(BF)


def head_body(me_ref, tok_ref, ctx_ref, w_out_ref, router_ref, ids_ref, placed_ref,
              resid_ref, inv_ref, normed_ref, gates_ref, send_ref):
    tok = ids_ref.shape[0]
    resid = (tok_ref[...].astype(F32) + mm(ctx_ref[...], w_out_ref[...])).astype(BF)
    resid_ref[...] = resid
    resid_f = resid.astype(F32)
    inv = lax.rsqrt(jnp.mean(resid_f * resid_f, axis=1, keepdims=True) + EPSILON)
    inv_ref[...] = inv
    normed = (resid_f * inv).astype(BF)
    normed_ref[...] = normed
    where = onehot(placed_ref[:, 0:1], 2 * tok) + onehot(placed_ref[:, 1:2], 2 * tok)
    send_ref[...] = mm(where.astype(BF), normed, TN).astype(BF)
    logits = mm(normed, router_ref[...])
    for k in range(2):
        picked = jnp.sum(logits * onehot(ids_ref[:, k : k + 1], LANES), axis=1, keepdims=True)
        gates_ref[:, k : k + 1] = jax.nn.sigmoid(picked)


def forward_body(me_ref, *refs, pieces):
    parts, (router_ref, w_in_ref, w_down_ref, rows_ref, act_ref, der_ref, gate_ref, keep_ref, send_ref, total) = (
        refs[:pieces], refs[pieces:])
    step = pl.program_id(0)
    size = parts[0].shape[0]

    @pl.when(step == 0)
    def _():
        for i, part in enumerate(parts):
            rows_ref[pl.ds(i * size, size), :] = part[...]
        logits = mm(rows_ref[...], router_ref[...])
        lanes = lax.broadcasted_iota(jnp.int32, logits.shape, 1)
        picked = jnp.sum(jnp.where(lanes == me_ref[0], logits, 0.0), axis=1, keepdims=True)
        gate_ref[...] = jax.nn.sigmoid(picked)

    value, derivative = gelu_pair(mm(rows_ref[...], w_in_ref[...]))
    act = value.astype(BF)
    act_ref[...] = act
    der_ref[...] = derivative.astype(BF)
    term = mm(act, w_down_ref[...])

    @pl.when(step == 0)
    def _():
        total[...] = term

    @pl.when(step > 0)
    def _():
        total[...] += term

    @pl.when(step == pl.num_programs(0) - 1)
    def _():
        half = keep_ref.shape[0]
        keep_ref[...] = total[:half, :].astype(BF)
        send_ref[...] = total[half:, :].astype(BF)


def backward_body(*refs, pieces):
    parts, (gate_ref, der_ref, w_in_ref, w_down_ref, grads_ref, pre_ref, keep_ref, send_ref, total) = (
        refs[:pieces], refs[pieces:])
    step = pl.program_id(0)
    size = parts[0].shape[0]

    @pl.when(step == 0)
    def _():
        for i, part in enumerate(parts):
            at = pl.ds(i * size, size)
            grads_ref[at, :] = (gate_ref[at, :] * part[...].astype(F32)).astype(BF)

    act_grad = mm(grads_ref[...], w_down_ref[...], NT)
    pre = (act_grad * der_ref[...].astype(F32)).astype(BF)
    pre_ref[...] = pre
    term = mm(pre, w_in_ref[...], NT)

    @pl.when(step == 0)
    def _():
        total[...] = term

    @pl.when(step > 0)
    def _():
        total[...] += term

    @pl.when(step == pl.num_programs(0) - 1)
    def _():
        half = keep_ref.shape[0]
        keep_ref[...] = total[:half, :].astype(BF)
        send_ref[...] = total[half:, :].astype(BF)


def weight_body(left_a, left_b, right_a, right_b, out_ref):
    out_ref[...] = (mm(left_a[...], right_a[...], TN) + mm(left_b[...], right_b[...], TN)).astype(BF)


def combine_body(me_ref, *refs, pieces):
    backs, (ids_ref, placed_ref, gates_ref, resid_ref, cot_ref, normed_ref, out_ref, table_ref, router_ref, slots) = (
        refs[:pieces], refs[pieces:])
    size = backs[0].shape[0]
    for i, back in enumerate(backs):
        slots[pl.ds(i * size, size), :] = back[...]
    held = slots[...]
    cot_f = cot_ref[...].astype(F32)
    total = resid_ref[...].astype(F32)
    table = jnp.zeros((cot_f.shape[0], LANES), F32)
    table_rel = jnp.zeros((cot_f.shape[0], LANES), F32)
    for k in range(2):
        gate = gates_ref[:, k : k + 1]
        mine = mm(onehot(placed_ref[:, k : k + 1], held.shape[0]).astype(BF), held)
        total = total + gate * mine
        logit = jnp.sum(cot_f * mine, axis=1, keepdims=True) * gate * (1.0 - gate)
        ids = ids_ref[:, k : k + 1]
        table = table + onehot(ids, LANES) * logit
        table_rel = table_rel + onehot(ids ^ me_ref[0], LANES) * logit
    out_ref[...] = total.astype(BF)
    table_ref[...] = table.astype(BF)
    router_ref[...] = mm(table_rel.astype(BF), normed_ref[...], TN)


def tail_body(cols_ref, *refs, pieces):
    backs, (placed_ref, table_ref, router_t_ref, resid_ref, inv_ref, cot_ref, w_out_ref, ctx_t_ref,
            grad_ref, grad_ctx_ref, keep_ref, send_ref, slots) = (refs[:pieces], refs[pieces:])
    size = backs[0].shape[0]
    for i, back in enumerate(backs):
        slots[pl.ds(i * size, size), :] = back[...]
    total = slots.shape[0]
    where = onehot(placed_ref[:, 0:1], total) + onehot(placed_ref[:, 1:2], total)
    normed_grad = mm(where.astype(BF), slots[...]) + mm(table_ref[...], router_t_ref[...])
    resid_f = resid_ref[...].astype(F32)
    inv = inv_ref[...]
    mean_term = jnp.mean(normed_grad * resid_f, axis=1, keepdims=True)
    grad = (cot_ref[...].astype(F32) + inv * normed_grad - (inv * inv * inv * mean_term) * resid_f).astype(BF)
    grad_ref[...] = grad
    width = keep_ref.shape[2]
    for m in range(2 * keep_ref.shape[0]):
        part = grad_ref[:, pl.ds(pl.multiple_of(cols_ref[m] * width, LANES), width)]
        held = (send_ref if m % 2 else keep_ref).at[m // 2]
        held[...] = mm(ctx_t_ref[...], part).astype(BF)
    grad_ctx_ref[...] = mm(grad, w_out_ref[...], NT).astype(BF)


def swap(x, axis, mask):
    count = lax.axis_size(axis)
    return lax.ppermute(x, axis, [(i, i ^ mask) for i in range(count)])


def added(*terms):
    return functools.reduce(jnp.add, [t.astype(F32) for t in terms])


class Expert:
    def __init__(self, count, capacity):
        self.high = 4 if count % 4 == 0 else 1
        self.low = count // self.high
        self.capacity = capacity
        self.chunks = [list(range(self.high))[: self.high // 2], list(range(self.high))[self.high // 2 :]]
        self.chunks = [c for c in self.chunks if c]

    def out(self, send):
        size, cap = self.low * self.capacity, self.capacity
        held = [send[k * size : (k + 1) * size] for k in range(self.high)]
        held = [held[0]] + [swap(held[k], "expert", k * self.low) for k in range(1, self.high)]
        groups = []
        for ks in self.chunks:
            rows = [jnp.concatenate([held[k][:cap] for k in ks])]
            for m in range(1, self.low):
                rows.append(swap(jnp.concatenate([held[k][m * cap : (m + 1) * cap] for k in ks]), "expert", m))
            groups.append(jnp.concatenate(rows))
        return groups

    def back(self, groups):
        cap = self.capacity
        blocks = {}
        for ks, rows in zip(self.chunks, groups):
            size = len(ks) * cap
            parts = [rows[:size]] + [swap(rows[m * size : (m + 1) * size], "expert", m) for m in range(1, self.low)]
            for i, k in enumerate(ks):
                block = jnp.concatenate([part[i * cap : (i + 1) * cap] for part in parts])
                blocks[k] = swap(block, "expert", k * self.low) if k else block
        return [blocks[k] for k in range(self.high)]


def on_device(tokens, context, w_out, w_router, expert_ids, w_in, w_down, cotangent):
    tok, width = tokens.shape
    experts = lax.axis_size("expert")
    dp = lax.axis_size("dp")
    far = dp // 2
    capacity = 2 * tok // experts
    slots = 2 * tok
    me = lax.axis_index("expert").astype(jnp.int32)
    mine = lax.axis_index("dp").astype(jnp.int32)
    me_1 = me.reshape(1)
    cols = mine ^ jnp.arange(dp, dtype=jnp.int32)
    weight_in, weight_down = w_in[0], w_down[0]
    hidden = weight_in.shape[1]
    router = jnp.pad(w_router, ((0, 0), (0, LANES - experts)))
    router_t = router.T
    per = width // experts
    ctx_t = jnp.take(context.T.reshape(experts, per, tok), me ^ jnp.arange(experts, dtype=jnp.int32), axis=0)
    ctx_t = ctx_t.reshape(width, tok)
    net = Expert(experts, capacity)
    smem = pl.BlockSpec(memory_space=pltpu.SMEM)
    vmem = pl.BlockSpec(memory_space=pltpu.VMEM)

    placed, cot_send = call(
        functools.partial(place_body, capacity=capacity),
        [shape((tok, 2), jnp.int32), shape((slots, width))],
        (me_1, expert_ids, cotangent), specs=[smem, vmem, vmem], moved=1 << 20, name="place")
    resid, inv, normed, gates, normed_send = call(
        head_body,
        [shape((tok, width)), shape((tok, 1), F32), shape((tok, width)), shape((tok, 2), F32), shape((slots, width))],
        (me_1, tokens, context, w_out, router, expert_ids, placed), specs=[smem] + [vmem] * 6,
        flops=2 * tok * width * width, moved=4 << 20, name="head")

    def spread(send):
        own = net.out(send)
        across = [swap(g, "dp", far) for g in own]
        return own + [swap(g, "dp", 1) for g in own], across + [swap(g, "dp", 1) for g in across]

    rows = spread(normed_send)
    grads = spread(cot_send)
    half = 2 * slots
    block = 256 if hidden % 256 == 0 else hidden
    steps = hidden // block

    def held(dims):
        return pl.BlockSpec(dims, lambda j: (0,) * len(dims))

    in_spec = pl.BlockSpec((width, block), lambda j: (0, j))
    down_spec = pl.BlockSpec((block, width), lambda j: (j, 0))
    hid_spec = pl.BlockSpec((half, block), lambda j: (0, j))

    def forward(parts):
        size = parts[0].shape[0]
        return call(
            functools.partial(forward_body, pieces=len(parts)),
            [shape((half, width)), shape((half, hidden)), shape((half, hidden)), shape((half, 1), F32),
             shape((slots, width)), shape((slots, width))],
            (me_1, *parts, router, weight_in, weight_down),
            specs=[smem] + [held((size, width))] * len(parts) + [held((width, LANES)), in_spec, down_spec],
            out_specs=[held((half, width)), hid_spec, hid_spec, held((half, 1)), held((slots, width)), held((slots, width))],
            grid=(steps,), scratch=[pltpu.VMEM((half, width), F32)],
            flops=4 * half * width * hidden, moved=8 << 20, name="forward")

    def backward(parts, gate, der):
        size = parts[0].shape[0]
        return call(
            functools.partial(backward_body, pieces=len(parts)),
            [shape((half, width)), shape((half, hidden)), shape((slots, width)), shape((slots, width))],
            (*parts, gate, der, weight_in, weight_down),
            specs=[held((size, width))] * len(parts) + [held((half, 1)), hid_spec, in_spec, down_spec],
            out_specs=[held((half, width)), hid_spec, held((slots, width)), held((slots, width))],
            grid=(steps,), scratch=[pltpu.VMEM((half, width), F32)],
            flops=4 * half * width * hidden, moved=8 << 20, name="backward")

    def gather_back(near, away):
        pick = [slice(i * slots // len(net.chunks), (i + 1) * slots // len(net.chunks)) for i in range(len(net.chunks))]
        away_in = swap(away[1], "dp", 1)
        near_in = swap(near[1], "dp", 1)
        crossing = [swap(added(away[0][p], away_in[p]).astype(BF), "dp", far) for p in pick]
        sums = [added(near[0][p], near_in[p], c).astype(BF) for p, c in zip(pick, crossing)]
        return net.back(sums)

    rows_a, act_a, der_a, gate_a, keep_a, send_a = forward(rows[0])
    rows_b, act_b, der_b, gate_b, keep_b, send_b = forward(rows[1])
    back_out = gather_back((keep_a, send_a), (keep_b, send_b))
    grads_a, pre_a, ikeep_a, isend_a = backward(grads[0], gate_a, der_a)
    grads_b, pre_b, ikeep_b, isend_b = backward(grads[1], gate_b, der_b)
    back_in = gather_back((ikeep_a, isend_a), (ikeep_b, isend_b))

    def weight_grad(left_a, left_b, right_a, right_b):
        left, right = left_a.shape[1], right_a.shape[1]
        tile = 256 if left % 256 == 0 else left
        left_spec = pl.BlockSpec((half, tile), lambda i: (0, i))
        return call(
            weight_body, [shape((left, right))], (left_a, left_b, right_a, right_b),
            specs=[left_spec, left_spec, held((half, right)), held((half, right))],
            out_specs=[pl.BlockSpec((tile, right), lambda i: (i, 0))], grid=(left // tile,),
            flops=4 * half * left * right, moved=6 << 20, name="weights")[0]

    grad_w_down = weight_grad(act_a, act_b, grads_a, grads_b)
    grad_w_in = weight_grad(rows_a, rows_b, pre_a, pre_b)

    output, table, local_router = call(
        functools.partial(combine_body, pieces=net.high),
        [shape((tok, width)), shape((tok, LANES)), shape((LANES, width), F32)],
        (me_1, *back_out, expert_ids, placed, gates, resid, cotangent, normed),
        specs=[smem] + [vmem] * (net.high + 6), scratch=[pltpu.VMEM((slots, width), BF)],
        flops=8 * tok * slots * width, moved=2 << 20, name="combine")

    part = width // dp
    grad_tokens, grad_context, keep, send = call(
        functools.partial(tail_body, pieces=net.high),
        [shape((tok, width)), shape((tok, width)), shape((dp // 2, width, part)), shape((dp // 2, width, part))],
        (cols, *back_in, placed, table, router_t, resid, inv, cotangent, w_out, ctx_t),
        specs=[smem] + [vmem] * (net.high + 8), scratch=[pltpu.VMEM((slots, width), BF)],
        flops=6 * tok * width * width, moved=6 << 20, name="tail")

    high, low = net.high, net.low
    summed = added(keep, swap(send, "dp", 1)).astype(BF).reshape(dp // 2, high, low, per, part)
    first, second = summed[:, : high // 2], summed[:, high // 2 :]
    first = added(first[0], swap(first[1], "dp", far)).astype(BF)
    first = added(first[:, 0], *[swap(first[:, m], "expert", m) for m in range(1, low)]).astype(BF)
    second = added(second[:, :, 0], *[swap(second[:, :, m], "expert", m) for m in range(1, low)]).astype(BF)
    second = added(second[0], swap(second[1], "dp", far)).astype(BF)
    blocks = [first[k] for k in range(high // 2)] + [second[k] for k in range(high - high // 2)]
    own = added(blocks[0], *[swap(blocks[k], "expert", k * low) for k in range(1, high)]).astype(BF)
    pair = jnp.stack([own, swap(own, "dp", far)])
    other = swap(pair, "dp", 1)
    quarters = jnp.stack([pair, other], axis=1).reshape(dp, per, part)
    grad_w_out = jnp.take(quarters, cols, axis=0).transpose(1, 0, 2).reshape(per, width).astype(F32)

    table_sum = local_router[:experts]
    table_sum = table_sum + swap(table_sum, "dp", 1)
    table_sum = table_sum + swap(table_sum, "dp", far)
    table_sum = table_sum.reshape(high, low, width)
    table_sum = added(table_sum[:, 0], *[swap(table_sum[:, m], "expert", m) for m in range(1, low)])
    table_sum = added(table_sum[0], *[swap(table_sum[k], "expert", k * low) for k in range(1, high)])
    grad_w_router = table_sum.reshape(width, 1)

    return (
        output,
        grad_tokens,
        grad_context,
        grad_w_out,
        grad_w_router,
        grad_w_in.reshape(1, width, hidden),
        grad_w_down.reshape(1, hidden, width),
    )


def solution(mesh):
    split = P(("dp", "expert"), None)
    return jax.shard_map(
        on_device,
        mesh=mesh,
        in_specs=(split, split, P(), P(), split, P("expert", None, "dp"), P("expert", "dp", None), split),
        out_specs=(split, split, split, P("expert", None), P(None, "expert"), P("expert", None, "dp"),
                   P("expert", "dp", None)),
        check_vma=False,
    )
```

```python
import functools

import jax
import jax.numpy as jnp
from jax import lax
from jax.experimental import pallas as pl
from jax.experimental.pallas import tpu as pltpu
from jax.sharding import PartitionSpec as P

GELU_C = 0.7978845608028654
GELU_A = 0.044715
EPSILON = 1e-06
BF = jnp.bfloat16
F32 = jnp.float32
LANES = 128
TILE = 16
MIB = 1024 * 1024

NN = (((1,), (0,)), ((), ()))
NT = (((1,), (1,)), ((), ()))
TN = (((0,), (0,)), ((), ()))

VMEM = pl.BlockSpec(memory_space=pltpu.VMEM)
SMEM = pl.BlockSpec(memory_space=pltpu.SMEM)
ANY = pl.BlockSpec(memory_space=pl.ANY)
HBM = pl.BlockSpec(memory_space=pltpu.HBM)
DMA = pltpu.SemaphoreType.DMA


def mm(a, b, dims=NN):
    return lax.dot_general(a, b, dims, preferred_element_type=F32)


def shape(dims, dtype=BF):
    return jax.ShapeDtypeStruct(dims, dtype)


def gelu_pair(preact):
    square = preact * preact
    tangent = jnp.tanh(GELU_C * (preact + GELU_A * (square * preact)))
    half = 0.5 * (1.0 + tangent)
    derivative = half + (0.5 * GELU_C) * preact * (1.0 - tangent * tangent) * (
        1.0 + 3.0 * GELU_A * square
    )
    return preact * half, derivative


class Line:
    def __init__(self):
        self.last = None

    def call(self, body, outs, args, specs=None, out_specs=None, scratch=(), flops=0, moved=MIB, vmem=8 * MIB, name=None):
        args, specs = list(args), list(specs) if specs is not None else [VMEM] * len(args)
        out_specs = list(out_specs) if out_specs is not None else [VMEM] * len(outs)
        count, given = len(args), len(outs)
        if self.last is not None:
            args.append(self.last)
            specs.append(ANY)

        def kernel(*refs):
            results = refs[len(args) :]
            results[given][...] = jnp.zeros((8, LANES), F32)
            body(*refs[:count], *results[:given], *results[given + 1 :])

        *results, self.last = pl.pallas_call(
            kernel,
            out_shape=[*outs, shape((8, LANES), F32)],
            in_specs=specs,
            out_specs=[*out_specs, VMEM],
            scratch_shapes=scratch,
            compiler_params=pltpu.CompilerParams(vmem_limit_bytes=vmem),
            cost_estimate=pl.CostEstimate(flops=flops, bytes_accessed=moved, transcendentals=0),
            name=name,
        )(*args)
        return results

    def move(self, *outputs, name="move"):
        arrays, places = [], {}
        aligned = True
        for pieces in outputs:
            for rows, terms in pieces:
                aligned = aligned and rows % TILE == 0
                for array, first in terms:
                    aligned = aligned and first % TILE == 0
                    if id(array) not in places:
                        places[id(array)] = len(arrays)
                        arrays.append(array)
        width = arrays[0].shape[1]
        if not aligned:
            return [
                jnp.concatenate([
                    added(*[a[f : f + rows] for a, f in terms]) if len(terms) > 1 else terms[0][0][terms[0][1] : terms[0][1] + rows]
                    for rows, terms in pieces
                ])
                for pieces in outputs
            ]

        def body(*refs):
            for pieces, out in zip(outputs, refs[len(arrays) :]):
                at = 0
                for rows, terms in pieces:
                    parts = [refs[places[id(a)]][f : f + rows, :] for a, f in terms]
                    if len(parts) > 1:
                        parts = [functools.reduce(jnp.add, [p.astype(F32) for p in parts]).astype(BF)]
                    out[at : at + rows, :] = parts[0]
                    at += rows

        outs = [shape((sum(rows for rows, _ in pieces), width)) for pieces in outputs]
        return self.call(body, outs, arrays, name=name)


def added(*terms):
    return functools.reduce(jnp.add, [t.astype(F32) for t in terms]).astype(BF)


def swap(x, axis, mask):
    return lax.ppermute(x, axis, [(i, i ^ mask) for i in range(lax.axis_size(axis))])


def hot_rows(ids_ref, rel_to, count):
    tok = ids_ref.shape[1]
    rows = lax.broadcasted_iota(jnp.int32, (count, tok), 0)
    return [(rows == (ids_ref[k : k + 1, :] ^ rel_to)).astype(F32) for k in range(2)]


def at_rows(places, total):
    tok = places[0].shape[1]
    rows = lax.broadcasted_iota(jnp.int32, (total, tok), 0)
    return functools.reduce(jnp.add, [(rows == p).astype(F32) for p in places]).astype(BF)


def onehot(column, width):
    lanes = lax.broadcasted_iota(jnp.int32, (column.shape[0], width), 1)
    return (lanes == column).astype(F32)


def on_device(tokens, context, w_out, w_router, expert_ids, w_in, w_down, cotangent):
    tok, width = tokens.shape
    experts = lax.axis_size("expert")
    dp = lax.axis_size("dp")
    far = dp // 2
    cap = 2 * tok // experts
    slots = 2 * tok
    hidden = w_in.shape[2]
    masks = [0, 2, 1, 3]
    low = experts // len(masks)
    shift = low.bit_length() - 1
    chunks = [[0, 1], [2, 3]]
    size = low * cap
    me = lax.axis_index("expert").astype(jnp.int32)
    mine = lax.axis_index("dp").astype(jnp.int32)
    info = jnp.concatenate([me.reshape(1), mine ^ jnp.arange(dp, dtype=jnp.int32)])
    ids_t = expert_ids.T
    router_t = w_router.T
    weight_in, weight_down = w_in[0], w_down[0]
    per = width // experts
    part = width // dp
    line = Line()

    def order(rel):
        high = rel >> shift
        return (high >> 1) | ((high & 1) << 1), rel & (low - 1)

    def head_body(info_ref, ids_hbm, cot_hbm, tok_hbm, ctx_hbm, router_hbm, w_out_hbm, *refs):
        outs, copies = refs[: low + 9], refs[low + 9 :]
        lows, (placed_ref, resid_ref, inv_ref, normed_ref, cols_ref), sends = outs[:low], outs[low : low + 5], outs[low + 5 :]
        held, sems = copies[:6], copies[6]
        loads = [pltpu.make_async_copy(src, dst, sems.at[i]) for i, (src, dst) in enumerate(
            zip((ids_hbm, ctx_hbm, w_out_hbm, tok_hbm, cot_hbm, router_hbm), held))]
        for load in loads:
            load.start()
        ids_ref, ctx_ref, w_out_ref, tok_ref, cot_ref, router_ref = held
        loads[0].wait()
        rows = lax.broadcasted_iota(jnp.int32, (tok, tok), 0)
        cols = lax.broadcasted_iota(jnp.int32, (tok, tok), 1)
        upper = (rows < cols).astype(BF)
        hot = hot_rows(ids_ref, info_ref[0], experts)
        before = [mm(h.astype(BF), upper) for h in hot]
        first = jnp.sum(hot[0], axis=1, keepdims=True)
        rank = [jnp.sum(before[0] * hot[0], axis=0, keepdims=True),
                jnp.sum((before[1] + first) * hot[1], axis=0, keepdims=True)]
        places, spots = [], []
        for k in range(2):
            block, lower = order(ids_ref[k : k + 1, :] ^ info_ref[0])
            places.append((block * low + lower) * cap + rank[k].astype(jnp.int32))
            placed_ref[k : k + 1, :] = places[k]
            spots.append((lower * len(masks) + block) * cap + rank[k].astype(jnp.int32))
        loads[1].wait()
        loads[2].wait()
        attn = mm(ctx_ref[...], w_out_ref[...])
        loads[3].wait()
        resid = (tok_ref[...].astype(F32) + attn).astype(BF)
        resid_ref[...] = resid
        resid_f = resid.astype(F32)
        inv = lax.rsqrt(jnp.mean(resid_f * resid_f, axis=1, keepdims=True) + EPSILON)
        inv_ref[...] = inv
        normed = (resid_f * inv).astype(BF)
        normed_ref[...] = normed
        moved = mm(at_rows(places, slots), normed).astype(BF)
        for c in range(len(masks)):
            sends[c][...] = moved[c * size : (c + 1) * size, :]
        loads[4].wait()
        moved = mm(at_rows(spots, slots), cot_ref[...]).astype(BF)
        each = slots // low
        for m in range(low):
            lows[m][...] = moved[m * each : (m + 1) * each, :]
        loads[5].wait()
        logits = mm(router_ref[...], normed, NT)
        hot = hot_rows(ids_ref, 0, experts)
        gates = [jax.nn.sigmoid(jnp.sum(logits * h, axis=0, keepdims=True)) for h in hot]
        ids_f = ids_ref[...].astype(F32)
        table = jnp.concatenate(gates + [ids_f, placed_ref[...].astype(F32), ids_f], axis=0)
        cols_ref[...] = table.T

    outs = line.call(
        head_body,
        [shape((slots // low, width))] * low + [shape((2, tok), jnp.int32)]
        + [shape((tok, width)), shape((tok, 1), F32), shape((tok, width)), shape((tok, 8), F32)] + [shape((size, width))] * 4,
        (info, ids_t, cotangent, tokens, context, router_t, w_out), specs=[SMEM] + [HBM] * 6,
        scratch=[pltpu.VMEM((2, tok), jnp.int32), pltpu.VMEM((tok, width), BF), pltpu.VMEM((width, width), BF),
                 pltpu.VMEM((tok, width), BF), pltpu.VMEM((tok, width), BF), pltpu.VMEM((experts, width), BF), DMA((6,))],
        flops=2 * tok * width * width, moved=4 * MIB, vmem=12 * MIB, name="head")
    cot_low, (placed, resid, inv, normed, cols), sends = outs[:low], outs[low : low + 5], outs[low + 5 :]
    cot_low = [cot_low[0]] + [swap(cot_low[m], "expert", m) for m in range(1, low)]
    norm_high = [sends[0]] + [swap(sends[c], "expert", masks[c] * low) for c in (1, 2, 3)]

    cot_high = line.move(*[[(cap, [(cot_low[m], c * cap)]) for m in range(low)] for c in range(4)], name="pack_cot_z")
    cot_high = [cot_high[0]] + [swap(cot_high[c], "expert", masks[c] * low) for c in (1, 2, 3)]

    def norm_chunk(chunk):
        lows = []
        if low > 1:
            lows = line.move(*[[(cap, [(norm_high[c], m * cap)]) for c in chunk] for m in range(1, low)], name="pack_norm_y")
            lows = [swap(x, "expert", m + 1) for m, x in enumerate(lows)]
        pieces = []
        for i, c in enumerate(chunk):
            pieces.append((cap, [(norm_high[c], 0)]))
            pieces += [(cap, [(x, i * cap)]) for x in lows]
        own = line.move(pieces, name="pack_norm_x")[0]
        across = swap(own, "dp", far)
        return own, swap(own, "dp", 1), across, swap(across, "dp", 1)

    def cot_chunk(chunk):
        own = line.move([(size, [(cot_high[c], 0)]) for c in chunk], name="pack_cot_x")[0]
        across = swap(own, "dp", far)
        return own, swap(own, "dp", 1), across, swap(across, "dp", 1)

    block = 256 if hidden % 256 == 0 else hidden

    def forward(parts):
        each = parts[0].shape[0]
        rows = each * len(parts)

        def body(info_ref, *refs):
            ins = refs[: len(parts)]
            (router_ref, in_ref, down_ref, rows_hbm, act_hbm, der_ref, gate_ref, keep_ref, send_ref,
             rows_ref, act_ref, total, sems) = refs[len(parts) :]
            for i, ref in enumerate(ins):
                rows_ref[i * each : (i + 1) * each, :] = ref[...]
            stores = [pltpu.make_async_copy(rows_ref, rows_hbm, sems.at[0]), pltpu.make_async_copy(act_ref, act_hbm, sems.at[1])]
            stores[0].start()
            for j in range(hidden // block):
                at = slice(j * block, (j + 1) * block)
                value, derivative = gelu_pair(mm(rows_ref[...], in_ref[:, at]))
                act = value.astype(BF)
                act_ref[:, at] = act
                der_ref[:, at] = derivative.astype(BF)
                term = mm(act, down_ref[at, :])
                total[...] = term if j == 0 else total[...] + term
            stores[1].start()
            keep_ref[...] = total[: rows // 2, :].astype(BF)
            send_ref[...] = total[rows // 2 :, :].astype(BF)
            logits = mm(rows_ref[...], router_ref[...], NT)
            lanes = lax.broadcasted_iota(jnp.int32, logits.shape, 1)
            picked = jnp.sum(jnp.where(lanes == info_ref[0], logits, 0.0), axis=1, keepdims=True)
            gate_ref[...] = jax.nn.sigmoid(picked)
            for store in stores:
                store.wait()

        return line.call(
            body,
            [shape((rows, width)), shape((rows, hidden)), shape((rows, hidden)), shape((rows, 1), F32),
             shape((rows // 2, width)), shape((rows // 2, width))],
            (info, *parts, router_t, weight_in, weight_down), specs=[SMEM] + [VMEM] * (len(parts) + 3),
            out_specs=[HBM] * 2 + [VMEM] * 4,
            scratch=[pltpu.VMEM((rows, width), BF), pltpu.VMEM((rows, hidden), BF), pltpu.VMEM((rows, width), F32), DMA((2,))],
            flops=4 * rows * width * hidden, moved=8 * MIB, vmem=20 * MIB, name="forward")

    def backward(parts, gate, der):
        each = parts[0].shape[0]
        rows = each * len(parts)

        def body(*refs):
            ins = refs[: len(parts)]
            (gate_ref, der_ref, in_ref, down_ref, grads_hbm, pre_hbm, keep_ref, send_ref,
             grads_ref, pre_ref, total, sems) = refs[len(parts) :]
            for i, ref in enumerate(ins):
                at = slice(i * each, (i + 1) * each)
                grads_ref[at, :] = (gate_ref[at, :] * ref[...].astype(F32)).astype(BF)
            stores = [pltpu.make_async_copy(grads_ref, grads_hbm, sems.at[0]), pltpu.make_async_copy(pre_ref, pre_hbm, sems.at[1])]
            stores[0].start()
            for j in range(hidden // block):
                at = slice(j * block, (j + 1) * block)
                act_grad = mm(grads_ref[...], down_ref[at, :], NT)
                pre = (act_grad * der_ref[:, at].astype(F32)).astype(BF)
                pre_ref[:, at] = pre
                term = mm(pre, in_ref[:, at], NT)
                total[...] = term if j == 0 else total[...] + term
            stores[1].start()
            keep_ref[...] = total[: rows // 2, :].astype(BF)
            send_ref[...] = total[rows // 2 :, :].astype(BF)
            for store in stores:
                store.wait()

        return line.call(
            body,
            [shape((rows, width)), shape((rows, hidden)), shape((rows // 2, width)), shape((rows // 2, width))],
            (*parts, gate, der, weight_in, weight_down), out_specs=[HBM] * 2 + [VMEM] * 2,
            scratch=[pltpu.VMEM((rows, width), BF), pltpu.VMEM((rows, hidden), BF), pltpu.VMEM((rows, width), F32), DMA((2,))],
            flops=4 * rows * width * hidden, moved=8 * MIB, vmem=20 * MIB, name="backward")

    half = slots // 2

    def cross(keep, send_in):
        both = line.move([(half, [(keep, 0), (send_in, 0)])], name="sum_core")[0]
        return swap(both, "dp", far)

    def gather(i, near_keep, near_in, crossing):
        terms = lambda at, rows: (rows, [(near_keep, i * half + at), (near_in, i * half + at), (crossing, at)])
        total, *lows = line.move(
            [terms(0, half)], *[[terms(j * size + m * cap, cap) for j in range(2)] for m in range(1, low)], name="sum_x")
        return total, [swap(x, "expert", m + 1) for m, x in enumerate(lows)]

    def send_back(i, total, lows):
        blocks = line.move(
            *[[(cap, [(total, j * size)])] + [(cap, [(x, j * cap)]) for x in lows] for j in range(2)], name="pack_back_z")
        return [swap(b, "expert", masks[c] * low) if masks[c] else b for c, b in zip(chunks[i], blocks)]

    norm_a = norm_chunk(chunks[0])
    norm_b = norm_chunk(chunks[1])
    cot_a = cot_chunk(chunks[0])
    rows_n, act_n, der_n, gate_n, keep_n, send_n = forward([norm_a[0], norm_b[0], norm_a[1], norm_b[1]])
    near_out = swap(send_n, "dp", 1)
    cot_b = cot_chunk(chunks[1])
    rows_a, act_a, der_a, gate_a, keep_a, send_a = forward([norm_a[2], norm_a[3]])
    core_a = swap(send_a, "dp", 1)
    rows_b, act_b, der_b, gate_b, keep_b, send_b = forward([norm_b[2], norm_b[3]])
    core_b = swap(send_b, "dp", 1)
    out_a = cross(keep_a, core_a)
    out_b = cross(keep_b, core_b)
    grads_n, pre_n, ikeep_n, isend_n = backward([cot_a[0], cot_b[0], cot_a[1], cot_b[1]], gate_n, der_n)
    near_in = swap(isend_n, "dp", 1)
    grads_a, pre_a, ikeep_a, isend_a = backward([cot_a[2], cot_a[3]], gate_a, der_a)
    icore_a = swap(isend_a, "dp", 1)
    grads_b, pre_b, ikeep_b, isend_b = backward([cot_b[2], cot_b[3]], gate_b, der_b)
    icore_b = swap(isend_b, "dp", 1)
    in_a = cross(ikeep_a, icore_a)
    in_b = cross(ikeep_b, icore_b)
    total_oa = gather(0, keep_n, near_out, out_a)
    total_ob = gather(1, keep_n, near_out, out_b)
    back_out = send_back(0, *total_oa)
    back_out += send_back(1, *total_ob)

    def weight_grad(lefts, rights):
        left, right = lefts[0].shape[1], rights[0].shape[1]
        tile = 256 if left % 256 == 0 else left

        def body(*refs):
            count = 2 * len(lefts)
            out_hbm, held, result, sems = refs[count], refs[count + 1 : 2 * count + 1], refs[2 * count + 1], refs[2 * count + 2]
            loads = [pltpu.make_async_copy(src, dst, sems.at[i]) for i, (src, dst) in enumerate(zip(refs[:count], held))]
            for load in loads:
                load.start()
            for load in loads:
                load.wait()
            stores = []
            for i in range(left // tile):
                at = slice(i * tile, (i + 1) * tile)
                result[at, :] = functools.reduce(
                    jnp.add, [mm(a[:, at], b[...], TN) for a, b in zip(held[: len(lefts)], held[len(lefts) :])]).astype(BF)
                stores.append(pltpu.make_async_copy(result.at[at, :], out_hbm.at[at, :], sems.at[count + i]))
                stores[-1].start()
            for store in stores:
                store.wait()

        return line.call(
            body, [shape((left, right))], (*lefts, *rights), specs=[HBM] * (2 * len(lefts)), out_specs=[HBM],
            scratch=[pltpu.VMEM(x.shape, BF) for x in (*lefts, *rights)]
            + [pltpu.VMEM((left, right), BF), DMA((2 * len(lefts) + left // tile,))],
            flops=4 * slots * 2 * left * right, moved=6 * MIB, vmem=20 * MIB, name="weights")[0]

    grad_w_down = weight_grad((act_n, act_a, act_b), (grads_n, grads_a, grads_b))
    total_ia = gather(0, ikeep_n, near_in, in_a)
    grad_w_in = weight_grad((rows_n, rows_a, rows_b), (pre_n, pre_a, pre_b))
    back_in = send_back(0, *total_ia)
    total_ib = gather(1, ikeep_n, near_in, in_b)
    back_in += send_back(1, *total_ib)

    spare = -(-experts // TILE) * TILE
    span = width + spare

    def combine_body(*refs):
        backs = refs[:4]
        placed_ref, cols_ref, resid_ref, cot_ref, normed_ref, out_ref, table_ref, router_ref = refs[4:]
        held = jnp.concatenate([b[...] for b in backs], axis=0)
        cot_f = cot_ref[...].astype(F32)
        total = resid_ref[...].astype(F32)
        table = jnp.zeros((tok, LANES), F32)
        for k in range(2):
            gate = cols_ref[:, k : k + 1]
            taken = mm(at_rows([placed_ref[k : k + 1, :]], slots), held, TN)
            total = total + gate * taken
            logit = jnp.sum(cot_f * taken, axis=1, keepdims=True) * gate * (1.0 - gate)
            table = table + onehot(cols_ref[:, 2 + k : 3 + k].astype(jnp.int32), LANES) * logit
        out_ref[...] = total.astype(BF)
        table = table.astype(BF)
        table_ref[...] = table
        router_ref[...] = mm(table, normed_ref[...], TN)[:spare, :].astype(BF)

    output, table, local_router = line.call(
        combine_body, [shape((tok, width)), shape((tok, LANES)), shape((spare, width))],
        (*back_out, placed, cols, resid, cotangent, normed),
        flops=8 * tok * slots * width, moved=2 * MIB, name="combine")

    def tail_body(info_ref, *refs):
        backs = refs[:4]
        (placed_ref, table_ref, router_ref, resid_ref, inv_ref, local_ref, cot_hbm, w_out_hbm, ctx_hbm,
         grad_ref, grad_ctx_ref, keep_ref, send_ref, cot_ref, w_out_ref, ctx_ref, turned, sems) = refs[4:]
        loads = [pltpu.make_async_copy(src, dst, sems.at[i]) for i, (src, dst) in enumerate(
            ((cot_hbm, cot_ref), (ctx_hbm, ctx_ref), (w_out_hbm, w_out_ref)))]
        for load in loads:
            load.start()
        held = jnp.concatenate([b[...] for b in backs], axis=0)
        where = at_rows([placed_ref[k : k + 1, :] for k in range(2)], slots)
        normed_grad = mm(where, held, TN) + mm(table_ref[:, :experts], router_ref[...])
        resid_f = resid_ref[...].astype(F32)
        inv_col = inv_ref[...]
        mean_term = jnp.mean(normed_grad * resid_f, axis=1, keepdims=True)
        loads[0].wait()
        grad = (cot_ref[...].astype(F32) + inv_col * normed_grad
                - (inv_col * inv_col * inv_col * mean_term) * resid_f).astype(BF)
        grad_ref[...] = grad
        outs = [(send_ref if m % 2 else keep_ref, (m // 2) * span) for m in range(dp)]
        for m, (out, base) in enumerate(outs):
            at = pl.ds(pl.multiple_of(info_ref[1 + m] * part, LANES), part)
            turned[:, m * part : (m + 1) * part] = grad_ref[:, at]
            out[base + width : base + span, :] = local_ref[:, at]
        loads[1].wait()
        tile = max(per, LANES)
        for i in range(width // tile):
            block = mm(ctx_ref[:, i * tile : (i + 1) * tile], turned[...], TN).astype(BF)
            for j in range(tile // per):
                spot, lower = order((i * (tile // per) + j) ^ info_ref[0])
                to = (spot * low + lower) * per
                for m, (out, base) in enumerate(outs):
                    out[pl.ds(pl.multiple_of(base + to, TILE), per), :] = (
                        block[j * per : (j + 1) * per, m * part : (m + 1) * part])
        loads[2].wait()
        grad_ctx_ref[...] = mm(grad, w_out_ref[...], NT).astype(BF)

    grad_tokens, grad_context, keep, send = line.call(
        tail_body,
        [shape((tok, width)), shape((tok, width)), shape((far * span, part)), shape((far * span, part))],
        (info, *back_in, placed, table, router_t, resid, inv, local_router, cotangent, w_out, context),
        specs=[SMEM] + [VMEM] * 10 + [HBM] * 3,
        scratch=[pltpu.VMEM((tok, width), BF), pltpu.VMEM((width, width), BF), pltpu.VMEM((tok, width), BF),
                 pltpu.VMEM((tok, width), BF), DMA((3,))],
        flops=6 * tok * width * width, moved=6 * MIB, vmem=16 * MIB, name="tail")

    core = swap(send, "dp", 1)
    spot = lambda d, c, m: d * span + (c * low + m) * per
    two = lambda first: [(keep, first), (core, first)]
    group = [(spare, two(width))]
    sum_x = line.move(
        [(2 * low * per, two(span)), (spare, two(span + width))],
        *[[(per, two(spot(d, c, m))) for d in range(2) for c in (2, 3)] for m in range(1, low)], name="reduce_core")
    first_x = swap(sum_x[0], "dp", far)
    second_low = [swap(x, "expert", m + 1) for m, x in enumerate(sum_x[1:])]
    first = line.move(
        *[[(per, two(spot(0, c, m)) + [(first_x, (c * low + m) * per)]) for c in (0, 1)]
          + [(spare, two(width) + [(first_x, 2 * low * per)])] for m in range(low)], name="reduce_x")
    first_low = [swap(x, "expert", m) for m, x in enumerate(first) if m]
    second = line.move(
        *[[(per, two(spot(d, c, 0)) + [(x, (d * 2 + i) * per) for x in second_low]) for i, c in enumerate((2, 3))]
          for d in (1, 0)], name="reduce_y")
    second_x = swap(second[0], "dp", far)
    router_terms = [(x, 2 * per) for x in [first[0], *first_low]]
    blocks = line.move(
        *[[(per, [(x, c * per) for x in [first[0], *first_low]]), (spare, router_terms)] for c in (0, 1)],
        *[[(per, [(second[1], c * per), (second_x, c * per)]), (spare, router_terms)] for c in (0, 1)], name="reduce_xy")
    blocks = [blocks[0]] + [swap(blocks[c], "expert", masks[c] * low) for c in (1, 2, 3)]
    own = line.move([(per + spare, [(b, 0) for b in blocks])], name="reduce_z")[0]
    quarters = [own] + [swap(own, "dp", m) for m in range(1, dp)]

    def final_body(info_ref, *refs):
        out_ref, router_ref = refs[dp:]
        for m in range(dp):
            at = pl.ds(pl.multiple_of(info_ref[1 + m] * part, LANES), part)
            out_ref[:, at] = refs[m][:per, :].astype(F32)
            table = refs[m][per:, :].astype(F32)
            rows = lax.broadcasted_iota(jnp.int32, table.shape, 0)
            router_ref[:, at] = jnp.sum(jnp.where(rows == info_ref[0], table, 0.0), axis=0, keepdims=True)

    grad_w_out, grad_w_router = line.call(
        final_body, [shape((per, width), F32), shape((1, width), F32)], (info, *quarters),
        specs=[SMEM] + [VMEM] * dp, name="final")

    return (
        output,
        grad_tokens,
        grad_context,
        grad_w_out,
        grad_w_router.reshape(width, 1),
        grad_w_in.reshape(1, width, hidden),
        grad_w_down.reshape(1, hidden, width),
    )


def solution(mesh):
    split = P(("dp", "expert"), None)
    return jax.shard_map(
        on_device,
        mesh=mesh,
        in_specs=(split, split, P(), P(), split, P("expert", None, "dp"), P("expert", "dp", None), split),
        out_specs=(split, split, split, P("expert", None), P(None, "expert"), P("expert", None, "dp"),
                   P("expert", "dp", None)),
        check_vma=False,
    )
```

```python
import functools

import jax
import jax.numpy as jnp
from jax import lax
from jax.experimental import pallas as pl
from jax.experimental.pallas import tpu as pltpu
from jax.sharding import PartitionSpec as P

GELU_C = 0.7978845608028654
GELU_A = 0.044715
EPSILON = 1e-06
BF = jnp.bfloat16
F32 = jnp.float32
LANES = 128
TILE = 16
MIB = 1024 * 1024
WAIT = 20 * 10**9

NN = (((1,), (0,)), ((), ()))
NT = (((1,), (1,)), ((), ()))
TN = (((0,), (0,)), ((), ()))

VMEM = pl.BlockSpec(memory_space=pltpu.VMEM)
ANY = pl.BlockSpec(memory_space=pl.ANY)
HBM = pl.BlockSpec(memory_space=pltpu.HBM)
DMA = pltpu.SemaphoreType.DMA


def mm(a, b, dims=NN):
    return lax.dot_general(a, b, dims, preferred_element_type=F32)


def shape(dims, dtype=BF):
    return jax.ShapeDtypeStruct(dims, dtype)


def gelu_pair(preact):
    square = preact * preact
    tangent = jnp.tanh(GELU_C * (preact + GELU_A * (square * preact)))
    half = 0.5 * (1.0 + tangent)
    derivative = half + (0.5 * GELU_C) * preact * (1.0 - tangent * tangent) * (
        1.0 + 3.0 * GELU_A * square
    )
    return preact * half, derivative


class Line:
    def __init__(self):
        self.last = None

    def call(self, body, outs, args, specs=None, out_specs=None, scratch=(), flops=0, vmem=8 * MIB, name=None):
        args, specs = list(args), list(specs) if specs is not None else [VMEM] * len(args)
        out_specs = list(out_specs) if out_specs is not None else [VMEM] * len(outs)
        count, given = len(args), len(outs)
        if self.last is not None:
            args.append(self.last)
            specs.append(ANY)

        def kernel(*refs):
            results = refs[len(args) :]
            results[given][...] = jnp.zeros((8, LANES), F32)
            body(*refs[:count], *results[:given], *results[given + 1 :])

        *results, self.last = pl.pallas_call(
            kernel,
            out_shape=[*outs, shape((8, LANES), F32)],
            in_specs=specs,
            out_specs=[*out_specs, VMEM],
            scratch_shapes=scratch,
            compiler_params=pltpu.CompilerParams(vmem_limit_bytes=vmem),
            cost_estimate=pl.CostEstimate(flops=flops, bytes_accessed=0, transcendentals=0),
            name=name,
        )(*args)
        return results

    def move(self, *outputs, flops=0, name="move"):
        arrays, places = [], {}
        aligned = True
        for pieces in outputs:
            for rows, terms in pieces:
                aligned = aligned and rows % TILE == 0
                for array, first in terms:
                    aligned = aligned and first % TILE == 0
                    if id(array) not in places:
                        places[id(array)] = len(arrays)
                        arrays.append(array)
        width = arrays[0].shape[1]
        if not aligned:
            return [
                jnp.concatenate([
                    added(*[a[f : f + rows] for a, f in terms]) if len(terms) > 1 else terms[0][0][terms[0][1] : terms[0][1] + rows]
                    for rows, terms in pieces
                ])
                for pieces in outputs
            ]

        def body(*refs):
            for pieces, out in zip(outputs, refs[len(arrays) :]):
                at = 0
                for rows, terms in pieces:
                    parts = [refs[places[id(a)]][f : f + rows, :] for a, f in terms]
                    if len(parts) > 1:
                        parts = [functools.reduce(jnp.add, [p.astype(F32) for p in parts]).astype(BF)]
                    out[at : at + rows, :] = parts[0]
                    at += rows

        outs = [shape((sum(rows for rows, _ in pieces), width)) for pieces in outputs]
        return self.call(body, outs, arrays, flops=flops, name=name)


def added(*terms):
    return functools.reduce(jnp.add, [t.astype(F32) for t in terms]).astype(BF)


def swap(x, axis, mask):
    return lax.ppermute(x, axis, [(i, i ^ mask) for i in range(lax.axis_size(axis))])


def hot_rows(ids_ref, rel_to, count):
    tok = ids_ref.shape[1]
    rows = lax.broadcasted_iota(jnp.int32, (count, tok), 0)
    return [(rows == (ids_ref[k : k + 1, :] ^ rel_to)).astype(F32) for k in range(2)]


def at_rows(places, total):
    tok = places[0].shape[1]
    rows = lax.broadcasted_iota(jnp.int32, (total, tok), 0)
    return functools.reduce(jnp.add, [(rows == p).astype(F32) for p in places]).astype(BF)


def onehot(column, width):
    lanes = lax.broadcasted_iota(jnp.int32, (column.shape[0], width), 1)
    return (lanes == column).astype(F32)


def on_device(tokens, context, w_out, w_router, expert_ids, w_in, w_down, cotangent):
    tok, width = tokens.shape
    experts = lax.axis_size("expert")
    dp = lax.axis_size("dp")
    far = dp // 2
    cap = 2 * tok // experts
    slots = 2 * tok
    hidden = w_in.shape[2]
    masks = [0, 2, 1, 3]
    low = experts // len(masks)
    shift = low.bit_length() - 1
    chunks = [[0, 1], [2, 3]]
    size = low * cap
    ids_t = expert_ids.T
    router_t = w_router.T
    weight_in, weight_down = w_in[0], w_down[0]
    per = width // experts
    part = width // dp
    line = Line()

    def order(rel):
        high = rel >> shift
        return (high >> 1) | ((high & 1) << 1), rel & (low - 1)

    def head_body(ids_hbm, cot_hbm, tok_hbm, ctx_hbm, w_out_hbm, *refs):
        outs, copies = refs[: low + 8], refs[low + 8 :]
        lows, (placed_ref, resid_ref, inv_ref, normed_ref), sends = outs[:low], outs[low : low + 4], outs[low + 4 :]
        held, sems = copies[:5], copies[5]
        me = lax.axis_index("expert")
        loads = [pltpu.make_async_copy(src, dst, sems.at[i]) for i, (src, dst) in enumerate(
            zip((ids_hbm, ctx_hbm, w_out_hbm, tok_hbm, cot_hbm), held))]
        for load in loads:
            load.start()
        ids_ref, ctx_ref, w_out_ref, tok_ref, cot_ref = held
        loads[0].wait()
        rows = lax.broadcasted_iota(jnp.int32, (tok, tok), 0)
        cols = lax.broadcasted_iota(jnp.int32, (tok, tok), 1)
        upper = (rows < cols).astype(BF)
        hot = hot_rows(ids_ref, me, experts)
        before = [mm(h.astype(BF), upper) for h in hot]
        first = jnp.sum(hot[0], axis=1, keepdims=True)
        rank = [jnp.sum(before[0] * hot[0], axis=0, keepdims=True),
                jnp.sum((before[1] + first) * hot[1], axis=0, keepdims=True)]
        places, spots = [], []
        for k in range(2):
            block, lower = order(ids_ref[k : k + 1, :] ^ me)
            places.append((block * low + lower) * cap + rank[k].astype(jnp.int32))
            placed_ref[k : k + 1, :] = places[k]
            spots.append((lower * len(masks) + block) * cap + rank[k].astype(jnp.int32))
        loads[1].wait()
        loads[2].wait()
        attn = mm(ctx_ref[...], w_out_ref[...])
        loads[3].wait()
        resid = (tok_ref[...].astype(F32) + attn).astype(BF)
        resid_ref[...] = resid
        resid_f = resid.astype(F32)
        inv = lax.rsqrt(jnp.mean(resid_f * resid_f, axis=1, keepdims=True) + EPSILON)
        inv_ref[...] = inv
        normed = (resid_f * inv).astype(BF)
        normed_ref[...] = normed
        moved = mm(at_rows(places, slots), normed).astype(BF)
        for c in range(len(masks)):
            sends[c][...] = moved[c * size : (c + 1) * size, :]
        loads[4].wait()
        moved = mm(at_rows(spots, slots), cot_ref[...]).astype(BF)
        each = slots // low
        for m in range(low):
            lows[m][...] = moved[m * each : (m + 1) * each, :]

    outs = line.call(
        head_body,
        [shape((slots // low, width))] * low + [shape((2, tok), jnp.int32)]
        + [shape((tok, width)), shape((tok, 1), F32), shape((tok, width))] + [shape((size, width))] * 4,
        (ids_t, cotangent, tokens, context, w_out), specs=[HBM] * 5,
        scratch=[pltpu.VMEM((2, tok), jnp.int32), pltpu.VMEM((tok, width), BF), pltpu.VMEM((width, width), BF),
                 pltpu.VMEM((tok, width), BF), pltpu.VMEM((tok, width), BF), DMA((5,))],
        vmem=53 * MIB, name="head")
    cot_low, (placed, resid, inv, normed), sends = outs[:low], outs[low : low + 4], outs[low + 4 :]
    cot_low = [cot_low[0]] + [swap(cot_low[m], "expert", m) for m in range(1, low)]
    norm_high = [sends[0]] + [swap(sends[c], "expert", masks[c] * low) for c in (1, 2, 3)]

    cot_high = line.move(*[[(cap, [(cot_low[m], c * cap)]) for m in range(low)] for c in range(4)], name="pack_cot_z")
    cot_high = [cot_high[0]] + [swap(cot_high[c], "expert", masks[c] * low) for c in (1, 2, 3)]

    norm_low = []
    if low > 1:
        lows = line.move(*[[(cap, [(norm_high[c], m * cap)]) for c in range(4)] for m in range(1, low)], name="pack_norm_y")
        norm_low = [swap(x, "expert", m + 1) for m, x in enumerate(lows)]
    norm_own = line.move(
        [(cap, [piece]) for c in range(4) for piece in [(norm_high[c], 0)] + [(x, c * cap) for x in norm_low]],
        name="pack_norm_x")[0]
    norm_far = swap(norm_own, "dp", far)
    norm_core = swap(norm_own, "dp", 1)
    cot_own = line.move([(size, [(x, 0)]) for x in cot_high], flops=WAIT, name="pack_cot_x")[0]
    cot_far = swap(cot_own, "dp", far)
    cot_core = swap(cot_own, "dp", 1)

    block = 256 if hidden % 256 == 0 else hidden

    def forward(parts, pieces):
        rows = sum(x.shape[0] for x in parts)
        piece = rows // 2 // pieces

        def body(*refs):
            ins = refs[: len(parts)]
            router_ref, in_ref, down_ref, rows_hbm, act_hbm, der_ref, gate_ref, keep_ref = refs[len(parts) : len(parts) + 8]
            sends, (rows_ref, act_ref, total, sems) = refs[len(parts) + 8 : -4], refs[-4:]
            at = 0
            for ref in ins:
                rows_ref[at : at + ref.shape[0], :] = ref[...]
                at += ref.shape[0]
            stores = [pltpu.make_async_copy(rows_ref, rows_hbm, sems.at[0]), pltpu.make_async_copy(act_ref, act_hbm, sems.at[1])]
            stores[0].start()
            for j in range(hidden // block):
                at = slice(j * block, (j + 1) * block)
                value, derivative = gelu_pair(mm(rows_ref[...], in_ref[:, at]))
                act = value.astype(BF)
                act_ref[:, at] = act
                der_ref[:, at] = derivative.astype(BF)
                term = mm(act, down_ref[at, :])
                total[...] = term if j == 0 else total[...] + term
            stores[1].start()
            keep_ref[...] = total[: rows // 2, :].astype(BF)
            for i in range(pieces):
                sends[i][...] = total[rows // 2 + i * piece : rows // 2 + (i + 1) * piece, :].astype(BF)
            logits = mm(rows_ref[...], router_ref[...], NT)
            lanes = lax.broadcasted_iota(jnp.int32, logits.shape, 1)
            picked = jnp.sum(jnp.where(lanes == lax.axis_index("expert"), logits, 0.0), axis=1, keepdims=True)
            gate_ref[...] = jax.nn.sigmoid(picked)
            for store in stores:
                store.wait()

        *results, = line.call(
            body,
            [shape((rows, width)), shape((rows, hidden)), shape((rows, hidden)), shape((rows, 1), F32),
             shape((rows // 2, width))] + [shape((piece, width))] * pieces,
            (*parts, router_t, weight_in, weight_down),
            out_specs=[HBM] * 2 + [VMEM] * (3 + pieces),
            scratch=[pltpu.VMEM((rows, width), BF), pltpu.VMEM((rows, hidden), BF), pltpu.VMEM((rows, width), F32), DMA((2,))],
            vmem=20 * MIB, name="forward")
        return (*results[:5], results[5:])

    def backward(parts, gate, der, pieces):
        rows = sum(x.shape[0] for x in parts)
        piece = rows // 2 // pieces

        def body(*refs):
            ins, refs = refs[: len(parts)], refs[len(parts) :]
            gate_ref, der_ref, in_ref, down_ref, grads_hbm, pre_hbm, keep_ref = refs[:7]
            sends, (grads_ref, pre_ref, total, sems) = refs[7 : 7 + pieces], refs[7 + pieces :]
            first = 0
            for ref in ins:
                at = slice(first, first + ref.shape[0])
                first += ref.shape[0]
                grads_ref[at, :] = (gate_ref[at, :] * ref[...].astype(F32)).astype(BF)
            stores = [pltpu.make_async_copy(grads_ref, grads_hbm, sems.at[0]), pltpu.make_async_copy(pre_ref, pre_hbm, sems.at[1])]
            stores[0].start()
            for j in range(hidden // block):
                at = slice(j * block, (j + 1) * block)
                act_grad = mm(grads_ref[...], down_ref[at, :], NT)
                pre = (act_grad * der_ref[:, at].astype(F32)).astype(BF)
                pre_ref[:, at] = pre
                term = mm(pre, in_ref[:, at], NT)
                total[...] = term if j == 0 else total[...] + term
            stores[1].start()
            keep_ref[...] = total[: rows // 2, :].astype(BF)
            for i in range(pieces):
                sends[i][...] = total[rows // 2 + i * piece : rows // 2 + (i + 1) * piece, :].astype(BF)
            for store in stores:
                store.wait()

        grads, pre, keep, *sends = line.call(
            body,
            [shape((rows, width)), shape((rows, hidden)), shape((rows // 2, width))] + [shape((piece, width))] * pieces,
            (*parts, gate, der, weight_in, weight_down),
            out_specs=[HBM] * 2 + [VMEM] * (1 + pieces),
            scratch=[pltpu.VMEM((rows, width), BF), pltpu.VMEM((rows, hidden), BF), pltpu.VMEM((rows, width), F32), DMA((2,))],
            vmem=20 * MIB, name="backward")
        return grads, pre, keep, sends

    half = slots // 2

    def relay(x):
        whole, *halves = line.move([(slots, [(x, 0)])], *[[(half, [(x, i * half)])] for i in range(2)], name="relay")
        return [whole] + [swap(h, "dp", 1) for h in halves]

    rows_n, act_n, der_n, gate_n, keep_n, send_n = forward([norm_own, norm_core], 1)
    near_out = swap(send_n[0], "dp", 1)
    rows_f, act_f, der_f, gate_f, keep_f, send_f = forward(relay(norm_far), 2)
    core_out = [swap(x, "dp", 1) for x in send_f]
    grads_n, pre_n, ikeep_n, isend_n = backward([cot_own, cot_core], gate_n, der_n, 1)
    near_in = swap(isend_n[0], "dp", 1)
    far_out = line.move([(half, [(keep_f, i * half), (core_out[i], 0)]) for i in range(2)], name="sum_core_out")[0]
    far_out = swap(far_out, "dp", far)
    grads_f, pre_f, ikeep_f, isend_f = backward(relay(cot_far), gate_f, der_f, 2)
    core_in = [swap(x, "dp", 1) for x in isend_f]
    far_in = line.move(*[[(half, [(ikeep_f, i * half), (core_in[i], 0)])] for i in range(2)], name="sum_core_in")
    far_in = [swap(x, "dp", far) for x in far_in]

    def weight_grad(lefts, rights):
        left, right = lefts[0].shape[1], rights[0].shape[1]
        tile = 256 if left % 256 == 0 else left

        def body(*refs):
            count = len(lefts) + len(rights)
            out_hbm, left_ref, right_ref, result, sems = refs[count:]
            loads = []
            for group, ref in ((refs[: len(lefts)], left_ref), (refs[len(lefts) : count], right_ref)):
                at = 0
                for src in group:
                    loads.append(pltpu.make_async_copy(src, ref.at[at : at + src.shape[0], :], sems.at[len(loads)]))
                    loads[-1].start()
                    at += src.shape[0]
            for load in loads:
                load.wait()
            stores = []
            for i in range(left // tile):
                at = slice(i * tile, (i + 1) * tile)
                result[at, :] = mm(left_ref[:, at], right_ref[...], TN).astype(BF)
                stores.append(pltpu.make_async_copy(result.at[at, :], out_hbm.at[at, :], sems.at[count + i]))
                stores[-1].start()
            for store in stores:
                store.wait()

        return line.call(
            body, [shape((left, right))], (*lefts, *rights), specs=[HBM] * (len(lefts) + len(rights)), out_specs=[HBM],
            scratch=[pltpu.VMEM((4 * slots, left), BF), pltpu.VMEM((4 * slots, right), BF), pltpu.VMEM((left, right), BF),
                     DMA((len(lefts) + len(rights) + left // tile,))],
            vmem=20 * MIB, name="weights")[0]

    grad_w_down = weight_grad((act_n, act_f), (grads_n, grads_f))

    quarter = slots // 4
    sums = line.move(
        *[[(quarter, [(x, c * quarter) for x in (keep_n, near_out, far_out)])] for c in range(4)], name="sum_x_out")
    out_high = [swap(x, "expert", masks[c] * low) if masks[c] else x for c, x in enumerate(sums)]

    def gather_in(i):
        terms = lambda at, rows: (rows, [(ikeep_n, i * half + at), (near_in, i * half + at), (far_in[i], at)])
        total, *lows = line.move(
            [terms(0, half)], *[[terms(j * size + m * cap, cap) for j in range(2)] for m in range(1, low)], name="sum_x_in")
        return total, [swap(x, "expert", m + 1) for m, x in enumerate(lows)]

    def send_back(i, total, lows):
        blocks = line.move(
            *[[(cap, [(total, j * size)])] + [(cap, [(x, j * cap)]) for x in lows] for j in range(2)], name="pack_back_z")
        return [swap(b, "expert", masks[c] * low) if masks[c] else b for c, b in zip(chunks[i], blocks)]

    total_a = gather_in(0)
    total_b = gather_in(1)
    out_low = []
    if low > 1:
        out_low = line.move(*[[(cap, [(x, m * cap)]) for x in out_high] for m in range(1, low)], name="pack_out_y")
    back_in = send_back(0, *total_a)
    back_in += send_back(1, *total_b)
    if low > 1:
        out_low = line.move(*[[(4 * cap, [(x, 0)])] for x in out_low], name="pass_out_y")
        out_low = [swap(x, "expert", m + 1) for m, x in enumerate(out_low)]
    grad_w_in = weight_grad((rows_n, rows_f), (pre_n, pre_f))
    back_out = line.move(
        [(cap, [piece]) for c in range(4) for piece in [(out_high[c], 0)] + [(x, c * cap) for x in out_low]],
        name="pack_out")

    spare = -(-experts // TILE) * TILE
    span = width + spare

    def combine_body(*refs):
        back_ref, placed_ref, ids_ref, router_ref, resid_ref, cot_ref, normed_ref, out_ref, table_ref, local_ref = refs
        logits = mm(router_ref[...], normed_ref[...], NT)
        gates = [jax.nn.sigmoid(jnp.sum(logits * h, axis=0, keepdims=True)) for h in hot_rows(ids_ref, 0, experts)]
        ids_f = ids_ref[...].astype(F32)
        cols = jnp.concatenate(gates + [ids_f] * 3, axis=0).T
        held = back_ref[...]
        cot_f = cot_ref[...].astype(F32)
        total = resid_ref[...].astype(F32)
        table = jnp.zeros((tok, LANES), F32)
        for k in range(2):
            gate = cols[:, k : k + 1]
            taken = mm(at_rows([placed_ref[k : k + 1, :]], slots), held, TN)
            total = total + gate * taken
            logit = jnp.sum(cot_f * taken, axis=1, keepdims=True) * gate * (1.0 - gate)
            table = table + onehot(cols[:, 2 + k : 3 + k].astype(jnp.int32), LANES) * logit
        out_ref[...] = total.astype(BF)
        table = table.astype(BF)
        table_ref[...] = table
        local_ref[...] = mm(table, normed_ref[...], TN)[:spare, :].astype(BF)

    output, table, local_router = line.call(
        combine_body, [shape((tok, width)), shape((tok, LANES)), shape((spare, width))],
        (*back_out, placed, ids_t, router_t, resid, cotangent, normed),
        name="combine")

    def tail_body(*refs):
        me, mine = lax.axis_index("expert"), lax.axis_index("dp")
        backs = refs[:4]
        (placed_ref, table_ref, router_ref, resid_ref, inv_ref, local_ref, cot_hbm, w_out_hbm, ctx_hbm,
         grad_ref, grad_ctx_ref, keep_ref, send_ref, cot_ref, w_out_ref, ctx_ref, turned, sems) = refs[4:]
        loads = [pltpu.make_async_copy(src, dst, sems.at[i]) for i, (src, dst) in enumerate(
            ((cot_hbm, cot_ref), (ctx_hbm, ctx_ref), (w_out_hbm, w_out_ref)))]
        for load in loads:
            load.start()
        held = jnp.concatenate([b[...] for b in backs], axis=0)
        where = at_rows([placed_ref[k : k + 1, :] for k in range(2)], slots)
        normed_grad = mm(where, held, TN) + mm(table_ref[:, :experts], router_ref[...])
        resid_f = resid_ref[...].astype(F32)
        inv_col = inv_ref[...]
        mean_term = jnp.mean(normed_grad * resid_f, axis=1, keepdims=True)
        loads[0].wait()
        grad = (cot_ref[...].astype(F32) + inv_col * normed_grad
                - (inv_col * inv_col * inv_col * mean_term) * resid_f).astype(BF)
        grad_ref[...] = grad
        outs = [(send_ref if m % 2 else keep_ref, (m // 2) * span) for m in range(dp)]
        for m, (out, base) in enumerate(outs):
            at = pl.ds(pl.multiple_of((mine ^ m) * part, LANES), part)
            turned[:, m * part : (m + 1) * part] = grad_ref[:, at]
            out[base + width : base + span, :] = local_ref[:, at]
        loads[1].wait()
        tile = max(per, LANES)
        for i in range(width // tile):
            block = mm(ctx_ref[:, i * tile : (i + 1) * tile], turned[...], TN).astype(BF)
            for j in range(tile // per):
                spot, lower = order((i * (tile // per) + j) ^ me)
                to = (spot * low + lower) * per
                for m, (out, base) in enumerate(outs):
                    out[pl.ds(pl.multiple_of(base + to, TILE), per), :] = (
                        block[j * per : (j + 1) * per, m * part : (m + 1) * part])
        loads[2].wait()
        grad_ctx_ref[...] = mm(grad, w_out_ref[...], NT).astype(BF)

    grad_tokens, grad_context, keep, send = line.call(
        tail_body,
        [shape((tok, width)), shape((tok, width)), shape((far * span, part)), shape((far * span, part))],
        (*back_in, placed, table, router_t, resid, inv, local_router, cotangent, w_out, context),
        specs=[VMEM] * 10 + [HBM] * 3,
        scratch=[pltpu.VMEM((tok, width), BF), pltpu.VMEM((width, width), BF), pltpu.VMEM((tok, width), BF),
                 pltpu.VMEM((tok, width), BF), DMA((3,))],
        vmem=16 * MIB, name="tail")

    core = swap(send, "dp", 1)
    spot = lambda d, c, m: d * span + (c * low + m) * per
    two = lambda first: [(keep, first), (core, first)]
    group = [(spare, two(width))]
    sum_x = line.move(
        [(2 * low * per, two(span)), (spare, two(span + width))],
        *[[(per, two(spot(d, c, m))) for d in range(2) for c in (2, 3)] for m in range(1, low)], name="reduce_core")
    first_x = swap(sum_x[0], "dp", far)
    second_low = [swap(x, "expert", m + 1) for m, x in enumerate(sum_x[1:])]
    first = line.move(
        *[[(per, two(spot(0, c, m)) + [(first_x, (c * low + m) * per)]) for c in (0, 1)]
          + [(spare, two(width) + [(first_x, 2 * low * per)])] for m in range(low)], name="reduce_x")
    first_low = [swap(x, "expert", m) for m, x in enumerate(first) if m]
    second = line.move(
        *[[(per, two(spot(d, c, 0)) + [(x, (d * 2 + i) * per) for x in second_low]) for i, c in enumerate((2, 3))]
          for d in (1, 0)], name="reduce_y")
    second_x = swap(second[0], "dp", far)
    router_terms = [(x, 2 * per) for x in [first[0], *first_low]]
    blocks = line.move(
        *[[(per, [(x, c * per) for x in [first[0], *first_low]]), (spare, router_terms)] for c in (0, 1)],
        *[[(per, [(second[1], c * per), (second_x, c * per)]), (spare, router_terms)] for c in (0, 1)], name="reduce_xy")
    blocks = [blocks[0]] + [swap(blocks[c], "expert", masks[c] * low) for c in (1, 2, 3)]
    own = line.move([(per + spare, [(b, 0) for b in blocks])], name="reduce_z")[0]
    quarters = [own] + [swap(own, "dp", m) for m in range(1, dp)]

    def final_body(*refs):
        me, mine = lax.axis_index("expert"), lax.axis_index("dp")
        out_ref, router_ref = refs[dp:]
        for m in range(dp):
            at = pl.ds(pl.multiple_of((mine ^ m) * part, LANES), part)
            out_ref[:, at] = refs[m][:per, :].astype(F32)
            table = refs[m][per:, :].astype(F32)
            rows = lax.broadcasted_iota(jnp.int32, table.shape, 0)
            router_ref[:, at] = jnp.sum(jnp.where(rows == me, table, 0.0), axis=0, keepdims=True)

    grad_w_out, grad_w_router = line.call(
        final_body, [shape((per, width), F32), shape((1, width), F32)], quarters, name="final")

    return (
        output,
        grad_tokens,
        grad_context,
        grad_w_out,
        grad_w_router.reshape(width, 1),
        grad_w_in.reshape(1, width, hidden),
        grad_w_down.reshape(1, hidden, width),
    )


def solution(mesh):
    split = P(("dp", "expert"), None)
    return jax.shard_map(
        on_device,
        mesh=mesh,
        in_specs=(split, split, P(), P(), split, P("expert", None, "dp"), P("expert", "dp", None), split),
        out_specs=(split, split, split, P("expert", None), P(None, "expert"), P("expert", None, "dp"),
                   P("expert", "dp", None)),
        check_vma=False,
    )
```

```python
import functools

import jax
import jax.numpy as jnp
from jax import lax
from jax.experimental import pallas as pl
from jax.experimental.pallas import tpu as pltpu
from jax.sharding import PartitionSpec as P

GELU_C = 0.7978845608028654
GELU_A = 0.044715
EPSILON = 1e-06
BF = jnp.bfloat16
F32 = jnp.float32
LANES = 128
TILE = 16
MIB = 1024 * 1024
WAIT = 20 * 10**9
PIECES = 4

NN = (((1,), (0,)), ((), ()))
NT = (((1,), (1,)), ((), ()))
TN = (((0,), (0,)), ((), ()))

VMEM = pl.BlockSpec(memory_space=pltpu.VMEM)
ANY = pl.BlockSpec(memory_space=pl.ANY)
HBM = pl.BlockSpec(memory_space=pltpu.HBM)
DMA = pltpu.SemaphoreType.DMA


def mm(a, b, dims=NN):
    return lax.dot_general(a, b, dims, preferred_element_type=F32)


def shape(dims, dtype=BF):
    return jax.ShapeDtypeStruct(dims, dtype)


def gelu_pair(preact):
    square = preact * preact
    tangent = jnp.tanh(GELU_C * (preact + GELU_A * (square * preact)))
    half = 0.5 * (1.0 + tangent)
    derivative = half + (0.5 * GELU_C) * preact * (1.0 - tangent * tangent) * (
        1.0 + 3.0 * GELU_A * square
    )
    return preact * half, derivative


class Line:
    def __init__(self):
        self.last = None

    def call(self, body, outs, args, specs=None, out_specs=None, scratch=(), flops=0, vmem=8 * MIB, name=None):
        args, specs = list(args), list(specs) if specs is not None else [VMEM] * len(args)
        out_specs = list(out_specs) if out_specs is not None else [VMEM] * len(outs)
        count, given = len(args), len(outs)
        if self.last is not None:
            args.append(self.last)
            specs.append(ANY)

        def kernel(*refs):
            results = refs[len(args) :]
            results[given][...] = jnp.zeros((8, LANES), F32)
            body(*refs[:count], *results[:given], *results[given + 1 :])

        *results, self.last = pl.pallas_call(
            kernel,
            out_shape=[*outs, shape((8, LANES), F32)],
            in_specs=specs,
            out_specs=[*out_specs, VMEM],
            scratch_shapes=scratch,
            compiler_params=pltpu.CompilerParams(vmem_limit_bytes=vmem),
            cost_estimate=pl.CostEstimate(flops=flops, bytes_accessed=0, transcendentals=0),
            name=name,
        )(*args)
        return results

    def move(self, *outputs, flops=0, hold=(), name="move"):
        arrays, places = [], {}
        aligned = True
        for pieces in outputs:
            for rows, terms in pieces:
                aligned = aligned and rows % TILE == 0
                for array, first in terms:
                    aligned = aligned and first % TILE == 0
                    if id(array) not in places:
                        places[id(array)] = len(arrays)
                        arrays.append(array)
        width = arrays[0].shape[1]
        if not aligned:
            return [
                jnp.concatenate([
                    added(*[a[f : f + rows] for a, f in terms]) if len(terms) > 1 else terms[0][0][terms[0][1] : terms[0][1] + rows]
                    for rows, terms in pieces
                ])
                for pieces in outputs
            ]

        def body(*refs):
            for pieces, out in zip(outputs, refs[len(arrays) + len(hold) :]):
                at = 0
                for rows, terms in pieces:
                    parts = [refs[places[id(a)]][f : f + rows, :] for a, f in terms]
                    if len(parts) > 1:
                        parts = [functools.reduce(jnp.add, [p.astype(F32) for p in parts]).astype(BF)]
                    out[at : at + rows, :] = parts[0]
                    at += rows

        outs = [shape((sum(rows for rows, _ in pieces), width)) for pieces in outputs]
        return self.call(body, outs, arrays + list(hold), flops=flops, name=name)


def added(*terms):
    return functools.reduce(jnp.add, [t.astype(F32) for t in terms]).astype(BF)


def swap(x, axis, mask):
    return lax.ppermute(x, axis, [(i, i ^ mask) for i in range(lax.axis_size(axis))])


def hot_rows(ids_ref, rel_to, count):
    tok = ids_ref.shape[1]
    rows = lax.broadcasted_iota(jnp.int32, (count, tok), 0)
    return [(rows == (ids_ref[k : k + 1, :] ^ rel_to)).astype(F32) for k in range(2)]


def at_rows(places, total):
    tok = places[0].shape[1]
    rows = lax.broadcasted_iota(jnp.int32, (total, tok), 0)
    return functools.reduce(jnp.add, [(rows == p).astype(F32) for p in places]).astype(BF)


def onehot(column, width):
    lanes = lax.broadcasted_iota(jnp.int32, (column.shape[0], width), 1)
    return (lanes == column).astype(F32)


def on_device(tokens, context, w_out, w_router, expert_ids, w_in, w_down, cotangent):
    tok, width = tokens.shape
    experts = lax.axis_size("expert")
    dp = lax.axis_size("dp")
    far = dp // 2
    cap = 2 * tok // experts
    slots = 2 * tok
    hidden = w_in.shape[2]
    masks = [0, 2, 1, 3]
    low = experts // len(masks)
    shift = low.bit_length() - 1
    chunks = [[0, 1], [2, 3]]
    size = low * cap
    ids_t = expert_ids.T
    router_t = w_router.T
    weight_in, weight_down = w_in[0], w_down[0]
    per = width // experts
    part = width // dp
    line = Line()

    def order(rel):
        high = rel >> shift
        return (high >> 1) | ((high & 1) << 1), rel & (low - 1)

    def head_body(ids_hbm, cot_hbm, tok_hbm, ctx_hbm, w_out_hbm, *refs):
        outs, copies = refs[: 2 * low + 7], refs[2 * low + 7 :]
        lows, (placed_ref, resid_ref, inv_ref, normed_ref), sends = outs[:low], outs[low : low + 4], outs[low + 4 :]
        held, sems = copies[:5], copies[5]
        me = lax.axis_index("expert")
        loads = [pltpu.make_async_copy(src, dst, sems.at[i]) for i, (src, dst) in enumerate(
            zip((ids_hbm, ctx_hbm, w_out_hbm, tok_hbm, cot_hbm), held))]
        for load in loads:
            load.start()
        ids_ref, ctx_ref, w_out_ref, tok_ref, cot_ref = held
        loads[0].wait()
        rows = lax.broadcasted_iota(jnp.int32, (tok, tok), 0)
        cols = lax.broadcasted_iota(jnp.int32, (tok, tok), 1)
        upper = (rows < cols).astype(BF)
        hot = hot_rows(ids_ref, me, experts)
        before = [mm(h.astype(BF), upper) for h in hot]
        first = jnp.sum(hot[0], axis=1, keepdims=True)
        rank = [jnp.sum(before[0] * hot[0], axis=0, keepdims=True),
                jnp.sum((before[1] + first) * hot[1], axis=0, keepdims=True)]
        places, spots = [], []
        for k in range(2):
            block, lower = order(ids_ref[k : k + 1, :] ^ me)
            places.append((block * low + lower) * cap + rank[k].astype(jnp.int32))
            placed_ref[k : k + 1, :] = places[k]
            spots.append((lower * len(masks) + block) * cap + rank[k].astype(jnp.int32))
        loads[1].wait()
        loads[2].wait()
        attn = mm(ctx_ref[...], w_out_ref[...])
        loads[3].wait()
        resid = (tok_ref[...].astype(F32) + attn).astype(BF)
        resid_ref[...] = resid
        resid_f = resid.astype(F32)
        inv = lax.rsqrt(jnp.mean(resid_f * resid_f, axis=1, keepdims=True) + EPSILON)
        inv_ref[...] = inv
        normed = (resid_f * inv).astype(BF)
        normed_ref[...] = normed
        moved = mm(at_rows(places, slots), normed).astype(BF)
        for m in range(low):
            sends[m][...] = moved[m * cap : (m + 1) * cap, :]
        for c in range(1, 4):
            sends[low + c - 1][...] = moved[c * size : (c + 1) * size, :]
        loads[4].wait()
        moved = mm(at_rows(spots, slots), cot_ref[...]).astype(BF)
        each = slots // low
        for m in range(low):
            lows[m][...] = moved[m * each : (m + 1) * each, :]

    outs = line.call(
        head_body,
        [shape((slots // low, width))] * low + [shape((2, tok), jnp.int32)]
        + [shape((tok, width)), shape((tok, 1), F32), shape((tok, width))] + [shape((cap, width))] * low + [shape((size, width))] * 3,
        (ids_t, cotangent, tokens, context, w_out), specs=[HBM] * 5,
        scratch=[pltpu.VMEM((2, tok), jnp.int32), pltpu.VMEM((tok, width), BF), pltpu.VMEM((width, width), BF),
                 pltpu.VMEM((tok, width), BF), pltpu.VMEM((tok, width), BF), DMA((5,))],
        vmem=53 * MIB, name="head")
    cot_low, (placed, resid, inv, normed), sends = outs[:low], outs[low : low + 4], outs[low + 4 :]
    cot_low = [cot_low[0]] + [swap(cot_low[m], "expert", m) for m in range(1, low)]
    norm_zero = [sends[0]] + [swap(sends[m], "expert", m) for m in range(1, low)]
    norm_high = [None] + [swap(sends[low + c - 1], "expert", masks[c] * low) for c in (1, 2, 3)]
    halves = [range(low)[: low // 2], range(low)[low // 2 :]]
    early = line.move(
        *[[(cap, [(norm_zero[m], 0)]) for m in part] for part in halves],
        *[[(cap, [(cot_low[m], c * cap)]) for m in range(low)] for c in range(4)], hold=(weight_in, weight_down), name="pack_zero")
    early, cot_high = early[:2], [swap(x, "expert", masks[c] * low) if masks[c] else x for c, x in enumerate(early[2:])]
    early_far = [swap(x, "dp", far) for x in early]

    whole = lambda *arrays: [(x.shape[0], [(x, 0)]) for x in arrays]
    norm_far, *lows = line.move(
        whole(*early_far),
        *[[(cap, [(norm_high[c], m * cap)]) for c in (1, 2, 3)] for m in range(1, low)], name="pack_norm_y")
    lows = [swap(x, "expert", m + 1) for m, x in enumerate(lows)]
    rest = [(cap, [piece]) for c in (1, 2, 3) for piece in [(norm_high[c], 0)] + [(x, (c - 1) * cap) for x in lows]]
    norm_own, norm_rest = line.move(whole(*early) + rest, rest, name="pack_norm_x")
    norm_far = [norm_far, swap(norm_rest, "dp", far)]
    norm_core = swap(norm_own, "dp", 1)
    cot_own = line.move(whole(*cot_high), flops=WAIT, name="pack_cot_x")[0]
    cot_far = [swap(cot_own, "dp", far)]
    cot_core = swap(cot_own, "dp", 1)

    block = 256 if hidden % 256 == 0 else hidden

    def forward(parts, pieces):
        rows = sum(x.shape[0] for x in parts)
        piece = rows // 2 // pieces

        def body(*refs):
            ins = refs[: len(parts)]
            router_ref, in_ref, down_ref, rows_hbm, act_hbm, der_ref, gate_ref, keep_ref = refs[len(parts) : len(parts) + 8]
            sends, (rows_ref, act_ref, total, sems) = refs[len(parts) + 8 : -4], refs[-4:]
            at = 0
            for ref in ins:
                rows_ref[at : at + ref.shape[0], :] = ref[...]
                at += ref.shape[0]
            stores = [pltpu.make_async_copy(rows_ref, rows_hbm, sems.at[0]), pltpu.make_async_copy(act_ref, act_hbm, sems.at[1])]
            stores[0].start()
            for j in range(hidden // block):
                at = slice(j * block, (j + 1) * block)
                value, derivative = gelu_pair(mm(rows_ref[...], in_ref[:, at]))
                act = value.astype(BF)
                act_ref[:, at] = act
                der_ref[:, at] = derivative.astype(BF)
                term = mm(act, down_ref[at, :])
                total[...] = term if j == 0 else total[...] + term
            stores[1].start()
            keep_ref[...] = total[: rows // 2, :].astype(BF)
            for i in range(pieces):
                sends[i][...] = total[rows // 2 + i * piece : rows // 2 + (i + 1) * piece, :].astype(BF)
            logits = mm(rows_ref[...], router_ref[...], NT)
            lanes = lax.broadcasted_iota(jnp.int32, logits.shape, 1)
            picked = jnp.sum(jnp.where(lanes == lax.axis_index("expert"), logits, 0.0), axis=1, keepdims=True)
            gate_ref[...] = jax.nn.sigmoid(picked)
            for store in stores:
                store.wait()

        *results, = line.call(
            body,
            [shape((rows, width)), shape((rows, hidden)), shape((rows, hidden)), shape((rows, 1), F32),
             shape((rows // 2, width))] + [shape((piece, width))] * pieces,
            (*parts, router_t, weight_in, weight_down),
            out_specs=[HBM] * 2 + [VMEM] * (3 + pieces),
            scratch=[pltpu.VMEM((rows, width), BF), pltpu.VMEM((rows, hidden), BF), pltpu.VMEM((rows, width), F32), DMA((2,))],
            vmem=20 * MIB, name="forward")
        return (*results[:5], results[5:])

    def backward(parts, gate, der, pieces):
        rows = sum(x.shape[0] for x in parts)
        piece = rows // 2 // pieces

        def body(*refs):
            ins, refs = refs[: len(parts)], refs[len(parts) :]
            gate_ref, der_ref, in_ref, down_ref, grads_hbm, pre_hbm, keep_ref = refs[:7]
            sends, (grads_ref, pre_ref, total, sems) = refs[7 : 7 + pieces], refs[7 + pieces :]
            first = 0
            for ref in ins:
                at = slice(first, first + ref.shape[0])
                first += ref.shape[0]
                grads_ref[at, :] = (gate_ref[at, :] * ref[...].astype(F32)).astype(BF)
            stores = [pltpu.make_async_copy(grads_ref, grads_hbm, sems.at[0]), pltpu.make_async_copy(pre_ref, pre_hbm, sems.at[1])]
            stores[0].start()
            for j in range(hidden // block):
                at = slice(j * block, (j + 1) * block)
                act_grad = mm(grads_ref[...], down_ref[at, :], NT)
                pre = (act_grad * der_ref[:, at].astype(F32)).astype(BF)
                pre_ref[:, at] = pre
                term = mm(pre, in_ref[:, at], NT)
                total[...] = term if j == 0 else total[...] + term
            stores[1].start()
            keep_ref[...] = total[: rows // 2, :].astype(BF)
            for i in range(pieces):
                sends[i][...] = total[rows // 2 + i * piece : rows // 2 + (i + 1) * piece, :].astype(BF)
            for store in stores:
                store.wait()

        grads, pre, keep, *sends = line.call(
            body,
            [shape((rows, width)), shape((rows, hidden)), shape((rows // 2, width))] + [shape((piece, width))] * pieces,
            (*parts, gate, der, weight_in, weight_down),
            out_specs=[HBM] * 2 + [VMEM] * (1 + pieces),
            scratch=[pltpu.VMEM((rows, width), BF), pltpu.VMEM((rows, hidden), BF), pltpu.VMEM((rows, width), F32), DMA((2,))],
            vmem=20 * MIB, name="backward")
        return grads, pre, keep, sends

    half = slots // 2

    def relay(x, pieces):
        each = slots // pieces
        first, second = x[0], x[-1]
        cut = first.shape[0]
        spans = [[(lo, hi) for lo, hi in ((i * each, min((i + 1) * each, cut)), (max(i * each, cut), (i + 1) * each)) if lo < hi]
                 for i in range(pieces)]
        taken = [[(hi - lo, [(first, lo) if hi <= cut else (second, lo - cut)]) for lo, hi in span] for span in spans]
        joined, *parts = line.move(whole(*x), *taken, name="relay")
        return [joined] + [swap(part, "dp", 1) for part in parts]

    rows_n, act_n, der_n, gate_n, keep_n, send_n = forward([norm_own, norm_core], 1)
    near_out = swap(send_n[0], "dp", 1)
    rows_f, act_f, der_f, gate_f, keep_f, send_f = forward(relay(norm_far, PIECES), PIECES)
    core_out = [swap(x, "dp", 1) for x in send_f]
    far_out = line.move([(x.shape[0], [(keep_f, i * x.shape[0]), (x, 0)]) for i, x in enumerate(core_out)], name="sum_core_out")[0]
    far_out = swap(far_out, "dp", far)
    cot_far = relay(cot_far, 2)
    grads_n, pre_n, ikeep_n, isend_n = backward([cot_own, cot_core], gate_n, der_n, 1)
    near_in = swap(isend_n[0], "dp", 1)
    grads_f, pre_f, ikeep_f, isend_f = backward(cot_far, gate_f, der_f, 2)
    core_in = [swap(x, "dp", 1) for x in isend_f]
    far_in = [swap(line.move([(half, [(ikeep_f, 0), (core_in[0], 0)])], name="sum_core_in")[0], "dp", far)]

    def weight_grad(lefts, rights):
        left, right = lefts[0].shape[1], rights[0].shape[1]
        tile = 256 if left % 256 == 0 else left

        def body(*refs):
            count = len(lefts) + len(rights)
            out_hbm, left_ref, right_ref, result, sems = refs[count:]
            loads = []
            for group, ref in ((refs[: len(lefts)], left_ref), (refs[len(lefts) : count], right_ref)):
                at = 0
                for src in group:
                    loads.append(pltpu.make_async_copy(src, ref.at[at : at + src.shape[0], :], sems.at[len(loads)]))
                    loads[-1].start()
                    at += src.shape[0]
            for load in loads:
                load.wait()
            stores = []
            for i in range(left // tile):
                at = slice(i * tile, (i + 1) * tile)
                result[at, :] = mm(left_ref[:, at], right_ref[...], TN).astype(BF)
                stores.append(pltpu.make_async_copy(result.at[at, :], out_hbm.at[at, :], sems.at[count + i]))
                stores[-1].start()
            for store in stores:
                store.wait()

        return line.call(
            body, [shape((left, right))], (*lefts, *rights), specs=[HBM] * (len(lefts) + len(rights)), out_specs=[HBM],
            scratch=[pltpu.VMEM((4 * slots, left), BF), pltpu.VMEM((4 * slots, right), BF), pltpu.VMEM((left, right), BF),
                     DMA((len(lefts) + len(rights) + left // tile,))],
            vmem=20 * MIB, name="weights")[0]

    grad_w_down = weight_grad((act_n, act_f), (grads_n, grads_f))
    far_in.append(swap(line.move([(half, [(ikeep_f, half), (core_in[1], 0)])], name="sum_core_in")[0], "dp", far))

    quarter = slots // 4
    sums = line.move(
        *[[(quarter, [(x, c * quarter) for x in (keep_n, near_out, far_out)])] for c in range(4)], name="sum_x_out")
    out_high = [swap(x, "expert", masks[c] * low) if masks[c] else x for c, x in enumerate(sums)]

    def gather_in(i):
        terms = lambda at, rows: (rows, [(ikeep_n, i * half + at), (near_in, i * half + at), (far_in[i], at)])
        total, *lows = line.move(
            [terms(0, half)], *[[terms(j * size + m * cap, cap) for j in range(2)] for m in range(1, low)], name="sum_x_in")
        return total, [swap(x, "expert", m + 1) for m, x in enumerate(lows)]

    def send_back(i, total, lows):
        blocks = line.move(
            *[[(cap, [(total, j * size)])] + [(cap, [(x, j * cap)]) for x in lows] for j in range(2)], name="pack_back_z")
        return [swap(b, "expert", masks[c] * low) if masks[c] else b for c, b in zip(chunks[i], blocks)]

    total_a = gather_in(0)
    total_b = gather_in(1)
    out_low = []
    if low > 1:
        out_low = line.move(*[[(cap, [(x, m * cap)]) for x in out_high] for m in range(1, low)], name="pack_out_y")
    back_in = send_back(0, *total_a)
    back_in += send_back(1, *total_b)
    if low > 1:
        out_low = line.move(*[[(2 * cap, [(x, i * 2 * cap)])] for x in out_low for i in range(2)], name="pass_out_y")
        out_low = [swap(x, "expert", i // 2 + 1) for i, x in enumerate(out_low)]
    back_a = line.move([(x.shape[0], [(x, 0)]) for x in back_in[:2]], name="pack_back")[0]
    back_out = line.move(
        [(cap, [piece]) for c in range(4) for piece in [(out_high[c], 0)] + [(out_low[2 * m + c // 2], c % 2 * cap) for m in range(low - 1)]],
        name="pack_out")

    spare = -(-experts // TILE) * TILE
    span = width + spare

    def combine_body(*refs):
        back_ref, placed_ref, ids_ref, router_ref, resid_ref, cot_ref, normed_ref, out_ref, table_ref, local_ref = refs
        logits = mm(router_ref[...], normed_ref[...], NT)
        gates = [jax.nn.sigmoid(jnp.sum(logits * h, axis=0, keepdims=True)) for h in hot_rows(ids_ref, 0, experts)]
        ids_f = ids_ref[...].astype(F32)
        cols = jnp.concatenate(gates + [ids_f] * 3, axis=0).T
        held = back_ref[...]
        cot_f = cot_ref[...].astype(F32)
        total = resid_ref[...].astype(F32)
        table = jnp.zeros((tok, LANES), F32)
        for k in range(2):
            gate = cols[:, k : k + 1]
            taken = mm(at_rows([placed_ref[k : k + 1, :]], slots), held, TN)
            total = total + gate * taken
            logit = jnp.sum(cot_f * taken, axis=1, keepdims=True) * gate * (1.0 - gate)
            table = table + onehot(cols[:, 2 + k : 3 + k].astype(jnp.int32), LANES) * logit
        out_ref[...] = total.astype(BF)
        table = table.astype(BF)
        table_ref[...] = table
        local_ref[...] = mm(table, normed_ref[...], TN)[:spare, :].astype(BF)

    output, table, local_router = line.call(
        combine_body, [shape((tok, width)), shape((tok, LANES)), shape((spare, width))],
        (*back_out, placed, ids_t, router_t, resid, cotangent, normed),
        name="combine")

    tile = max(per, LANES)

    def products(odd, ctx_ref, grad_ref, local_ref, turned, out):
        me, mine = lax.axis_index("expert"), lax.axis_index("dp")
        for d in range(far):
            at = pl.ds(pl.multiple_of((mine ^ (2 * d + odd)) * part, LANES), part)
            turned[:, d * part : (d + 1) * part] = grad_ref[:, at]
            out[d * span + width : (d + 1) * span, :] = local_ref[:, at]
        for i in range(width // tile):
            block = mm(ctx_ref[:, i * tile : (i + 1) * tile], turned[...], TN).astype(BF)
            for j in range(tile // per):
                spot, lower = order((i * (tile // per) + j) ^ me)
                to = (spot * low + lower) * per
                for d in range(far):
                    out[pl.ds(pl.multiple_of(d * span + to, TILE), per), :] = (
                        block[j * per : (j + 1) * per, d * part : (d + 1) * part])

    def tail_body(*refs):
        backs = refs[:3]
        (placed_ref, table_ref, router_ref, resid_ref, inv_ref, local_ref, cot_hbm, ctx_hbm,
         grad_out, grad_ref, ctx_ref, send_ref, cot_ref, turned, sems) = refs[3:]
        loads = [pltpu.make_async_copy(src, dst, sems.at[i]) for i, (src, dst) in enumerate(
            ((cot_hbm, cot_ref), (ctx_hbm, ctx_ref)))]
        for load in loads:
            load.start()
        held = jnp.concatenate([b[...] for b in backs], axis=0)
        where = at_rows([placed_ref[k : k + 1, :] for k in range(2)], slots)
        normed_grad = mm(where, held, TN) + mm(table_ref[:, :experts], router_ref[...])
        resid_f = resid_ref[...].astype(F32)
        inv_col = inv_ref[...]
        mean_term = jnp.mean(normed_grad * resid_f, axis=1, keepdims=True)
        loads[0].wait()
        grad_ref[...] = (cot_ref[...].astype(F32) + inv_col * normed_grad
                         - (inv_col * inv_col * inv_col * mean_term) * resid_f).astype(BF)
        loads[1].wait()
        grad_out[...] = grad_ref[...]
        products(1, ctx_ref, grad_ref, local_ref, turned, send_ref)

    grad_tokens, grad_near, ctx_near, send = line.call(
        tail_body, [shape((tok, width))] * 3 + [ shape((far * span, part))],
        (back_a, *back_in[2:], placed, table, router_t, resid, inv, local_router, cotangent, context),
        specs=[VMEM] * 9 + [HBM] * 2,
        scratch=[pltpu.VMEM((tok, width), BF), pltpu.VMEM((tok, far * part), BF), DMA((2,))],
        vmem=16 * MIB, name="tail")
    core = swap(send, "dp", 1)

    def keep_body(ctx_ref, grad_ref, local_ref, w_out_ref, grad_ctx_ref, keep_ref, turned):
        products(0, ctx_ref, grad_ref, local_ref, turned, keep_ref)
        grad_ctx_ref[...] = mm(grad_ref[...], w_out_ref[...], NT).astype(BF)

    grad_context, keep = line.call(
        keep_body, [shape((tok, width)), shape((far * span, part))], (ctx_near, grad_near, local_router, w_out),
        scratch=[pltpu.VMEM((tok, far * part), BF)], vmem=16 * MIB, name="keep")

    spot = lambda d, c, m: d * span + (c * low + m) * per
    two = lambda first: [(keep, first), (core, first)]
    group = [(spare, two(width))]
    sum_x = line.move(
        [(2 * low * per, two(span)), (spare, two(span + width))],
        *[[(per, two(spot(d, c, m))) for d in range(2) for c in (2, 3)] for m in range(1, low)], name="reduce_core")
    grad_w_in = weight_grad((rows_n, rows_f), (pre_n, pre_f))
    first_x = swap(sum_x[0], "dp", far)
    second_low = [swap(x, "expert", m + 1) for m, x in enumerate(sum_x[1:])]
    first = line.move(
        *[[(per, two(spot(0, c, m)) + [(first_x, (c * low + m) * per)]) for c in (0, 1)]
          + [(spare, two(width) + [(first_x, 2 * low * per)])] for m in range(low)], name="reduce_x")
    first_low = [swap(x, "expert", m) for m, x in enumerate(first) if m]
    second = line.move(
        *[[(per, two(spot(d, c, 0)) + [(x, (d * 2 + i) * per) for x in second_low]) for i, c in enumerate((2, 3))]
          for d in (1, 0)], name="reduce_y")
    second_x = swap(second[0], "dp", far)
    router_terms = [(x, 2 * per) for x in [first[0], *first_low]]
    blocks = line.move(
        *[[(per, [(x, c * per) for x in [first[0], *first_low]]), (spare, router_terms)] for c in (0, 1)],
        *[[(per, [(second[1], c * per), (second_x, c * per)]), (spare, router_terms)] for c in (0, 1)], name="reduce_xy")
    blocks = [blocks[0]] + [swap(blocks[c], "expert", masks[c] * low) for c in (1, 2, 3)]
    own = line.move([(per + spare, [(b, 0) for b in blocks])], name="reduce_z")[0]
    quarters = [own] + [swap(own, "dp", m) for m in range(1, dp)]

    def final_body(*refs):
        me, mine = lax.axis_index("expert"), lax.axis_index("dp")
        out_ref, router_ref = refs[dp:]
        for m in range(dp):
            at = pl.ds(pl.multiple_of((mine ^ m) * part, LANES), part)
            out_ref[:, at] = refs[m][:per, :].astype(F32)
            table = refs[m][per:, :].astype(F32)
            rows = lax.broadcasted_iota(jnp.int32, table.shape, 0)
            router_ref[:, at] = jnp.sum(jnp.where(rows == me, table, 0.0), axis=0, keepdims=True)

    grad_w_out, grad_w_router = line.call(
        final_body, [shape((per, width), F32), shape((1, width), F32)], quarters, name="final")

    return (
        output,
        grad_tokens,
        grad_context,
        grad_w_out,
        grad_w_router.reshape(width, 1),
        grad_w_in.reshape(1, width, hidden),
        grad_w_down.reshape(1, hidden, width),
    )


def solution(mesh):
    split = P(("dp", "expert"), None)
    return jax.shard_map(
        on_device,
        mesh=mesh,
        in_specs=(split, split, P(), P(), split, P("expert", None, "dp"), P("expert", "dp", None), split),
        out_specs=(split, split, split, P("expert", None), P(None, "expert"), P("expert", None, "dp"),
                   P("expert", "dp", None)),
        check_vma=False,
    )
```

```python
import functools

import jax
import jax.numpy as jnp
from jax import lax
from jax.experimental import pallas as pl
from jax.experimental.pallas import tpu as pltpu
from jax.sharding import PartitionSpec as P

GELU_C = 0.7978845608028654
GELU_A = 0.044715
EPSILON = 1e-06
BF = jnp.bfloat16
F32 = jnp.float32
LANES = 128
TILE = 16
MIB = 1024 * 1024
WAIT = 20 * 10**9
PIECES = 4

NN = (((1,), (0,)), ((), ()))
NT = (((1,), (1,)), ((), ()))
TN = (((0,), (0,)), ((), ()))

VMEM = pl.BlockSpec(memory_space=pltpu.VMEM)
ANY = pl.BlockSpec(memory_space=pl.ANY)
HBM = pl.BlockSpec(memory_space=pltpu.HBM)
DMA = pltpu.SemaphoreType.DMA


def mm(a, b, dims=NN):
    return lax.dot_general(a, b, dims, preferred_element_type=F32)


def shape(dims, dtype=BF):
    return jax.ShapeDtypeStruct(dims, dtype)


def gelu_pair(preact):
    square = preact * preact
    tangent = jnp.tanh(GELU_C * (preact + GELU_A * (square * preact)))
    half = 0.5 * (1.0 + tangent)
    derivative = half + (0.5 * GELU_C) * preact * (1.0 - tangent * tangent) * (
        1.0 + 3.0 * GELU_A * square
    )
    return preact * half, derivative


class Line:
    def __init__(self):
        self.last = None

    def call(self, body, outs, args, specs=None, out_specs=None, scratch=(), flops=0, vmem=8 * MIB, name=None):
        args, specs = list(args), list(specs) if specs is not None else [VMEM] * len(args)
        out_specs = list(out_specs) if out_specs is not None else [VMEM] * len(outs)
        count, given = len(args), len(outs)
        if self.last is not None:
            args.append(self.last)
            specs.append(ANY)

        def kernel(*refs):
            results = refs[len(args) :]
            results[given][...] = jnp.zeros((8, LANES), F32)
            body(*refs[:count], *results[:given], *results[given + 1 :])

        *results, self.last = pl.pallas_call(
            kernel,
            out_shape=[*outs, shape((8, LANES), F32)],
            in_specs=specs,
            out_specs=[*out_specs, VMEM],
            scratch_shapes=scratch,
            compiler_params=pltpu.CompilerParams(vmem_limit_bytes=vmem),
            cost_estimate=pl.CostEstimate(flops=flops, bytes_accessed=0, transcendentals=0),
            name=name,
        )(*args)
        return results

    def move(self, *outputs, flops=0, hold=(), name="move"):
        arrays, places = [], {}
        aligned = True
        for pieces in outputs:
            for rows, terms in pieces:
                aligned = aligned and rows % TILE == 0
                for array, first in terms:
                    aligned = aligned and first % TILE == 0
                    if id(array) not in places:
                        places[id(array)] = len(arrays)
                        arrays.append(array)
        width = arrays[0].shape[1]
        if not aligned:
            return [
                jnp.concatenate([
                    added(*[a[f : f + rows] for a, f in terms]) if len(terms) > 1 else terms[0][0][terms[0][1] : terms[0][1] + rows]
                    for rows, terms in pieces
                ])
                for pieces in outputs
            ]

        def body(*refs):
            for pieces, out in zip(outputs, refs[len(arrays) + len(hold) :]):
                at = 0
                for rows, terms in pieces:
                    parts = [refs[places[id(a)]][f : f + rows, :] for a, f in terms]
                    if len(parts) > 1:
                        parts = [functools.reduce(jnp.add, [p.astype(F32) for p in parts]).astype(BF)]
                    out[at : at + rows, :] = parts[0]
                    at += rows

        outs = [shape((sum(rows for rows, _ in pieces), width)) for pieces in outputs]
        return self.call(body, outs, arrays + list(hold), flops=flops, name=name)


def added(*terms):
    return functools.reduce(jnp.add, [t.astype(F32) for t in terms]).astype(BF)


def swap(x, axis, mask):
    return lax.ppermute(x, axis, [(i, i ^ mask) for i in range(lax.axis_size(axis))])


def hot_rows(ids_ref, rel_to, count):
    tok = ids_ref.shape[1]
    rows = lax.broadcasted_iota(jnp.int32, (count, tok), 0)
    return [(rows == (ids_ref[k : k + 1, :] ^ rel_to)).astype(F32) for k in range(2)]


def at_rows(places, total):
    tok = places[0].shape[1]
    rows = lax.broadcasted_iota(jnp.int32, (total, tok), 0)
    return functools.reduce(jnp.add, [(rows == p).astype(F32) for p in places]).astype(BF)


def onehot(column, width):
    lanes = lax.broadcasted_iota(jnp.int32, (column.shape[0], width), 1)
    return (lanes == column).astype(F32)


def on_device(tokens, context, w_out, w_router, expert_ids, w_in, w_down, cotangent):
    tok, width = tokens.shape
    experts = lax.axis_size("expert")
    dp = lax.axis_size("dp")
    far = dp // 2
    cap = 2 * tok // experts
    slots = 2 * tok
    hidden = w_in.shape[2]
    masks = [0, 2, 1, 3]
    low = experts // len(masks)
    shift = low.bit_length() - 1
    chunks = [[0, 1], [2, 3]]
    size = low * cap
    ids_t = expert_ids.T
    router_t = w_router.T
    weight_in, weight_down = w_in[0], w_down[0]
    per = width // experts
    part = width // dp
    line = Line()

    def order(rel):
        high = rel >> shift
        return (high >> 1) | ((high & 1) << 1), rel & (low - 1)

    def head_body(ids_hbm, cot_hbm, tok_hbm, ctx_hbm, w_out_hbm, *refs):
        outs, copies = refs[: 2 * low + 7], refs[2 * low + 7 :]
        lows, (placed_ref, resid_ref, inv_ref, normed_ref), sends = outs[:low], outs[low : low + 4], outs[low + 4 :]
        held, sems = copies[:5], copies[5]
        me = lax.axis_index("expert")
        loads = [pltpu.make_async_copy(src, dst, sems.at[i]) for i, (src, dst) in enumerate(
            zip((ids_hbm, ctx_hbm, w_out_hbm, tok_hbm, cot_hbm), held))]
        for load in loads:
            load.start()
        ids_ref, ctx_ref, w_out_ref, tok_ref, cot_ref = held
        loads[0].wait()
        rows = lax.broadcasted_iota(jnp.int32, (tok, tok), 0)
        cols = lax.broadcasted_iota(jnp.int32, (tok, tok), 1)
        upper = (rows < cols).astype(BF)
        hot = hot_rows(ids_ref, me, experts)
        before = [mm(h.astype(BF), upper) for h in hot]
        first = jnp.sum(hot[0], axis=1, keepdims=True)
        rank = [jnp.sum(before[0] * hot[0], axis=0, keepdims=True),
                jnp.sum((before[1] + first) * hot[1], axis=0, keepdims=True)]
        places, spots = [], []
        for k in range(2):
            block, lower = order(ids_ref[k : k + 1, :] ^ me)
            places.append((block * low + lower) * cap + rank[k].astype(jnp.int32))
            placed_ref[k : k + 1, :] = places[k]
            spots.append((lower * len(masks) + block) * cap + rank[k].astype(jnp.int32))
        loads[1].wait()
        loads[2].wait()
        attn = mm(ctx_ref[...], w_out_ref[...])
        loads[3].wait()
        resid = (tok_ref[...].astype(F32) + attn).astype(BF)
        resid_ref[...] = resid
        resid_f = resid.astype(F32)
        inv = lax.rsqrt(jnp.mean(resid_f * resid_f, axis=1, keepdims=True) + EPSILON)
        inv_ref[...] = inv
        normed = (resid_f * inv).astype(BF)
        normed_ref[...] = normed
        moved = mm(at_rows(places, slots), normed).astype(BF)
        for m in range(low):
            sends[m][...] = moved[m * cap : (m + 1) * cap, :]
        for c in range(1, 4):
            sends[low + c - 1][...] = moved[c * size : (c + 1) * size, :]
        loads[4].wait()
        moved = mm(at_rows(spots, slots), cot_ref[...]).astype(BF)
        each = slots // low
        for m in range(low):
            lows[m][...] = moved[m * each : (m + 1) * each, :]

    outs = line.call(
        head_body,
        [shape((slots // low, width))] * low + [shape((2, tok), jnp.int32)]
        + [shape((tok, width)), shape((tok, 1), F32), shape((tok, width))] + [shape((cap, width))] * low + [shape((size, width))] * 3,
        (ids_t, cotangent, tokens, context, w_out), specs=[HBM] * 5,
        scratch=[pltpu.VMEM((2, tok), jnp.int32), pltpu.VMEM((tok, width), BF), pltpu.VMEM((width, width), BF),
                 pltpu.VMEM((tok, width), BF), pltpu.VMEM((tok, width), BF), DMA((5,))],
        vmem=53 * MIB, name="head")
    cot_low, (placed, resid, inv, normed), sends = outs[:low], outs[low : low + 4], outs[low + 4 :]
    cot_low = [cot_low[0]] + [swap(cot_low[m], "expert", m) for m in range(1, low)]
    norm_zero = [sends[0]] + [swap(sends[m], "expert", m) for m in range(1, low)]
    norm_high = [None] + [swap(sends[low + c - 1], "expert", masks[c] * low) for c in (1, 2, 3)]
    halves = [range(low)[: low // 2], range(low)[low // 2 :]]
    early = line.move(
        *[[(cap, [(norm_zero[m], 0)]) for m in part] for part in halves],
        *[[(cap, [(cot_low[m], c * cap)]) for m in range(low)] for c in range(4)], hold=(weight_in, weight_down), name="pack_zero")
    early, cot_high = early[:2], [swap(x, "expert", masks[c] * low) if masks[c] else x for c, x in enumerate(early[2:])]
    early_far = [swap(x, "dp", far) for x in early]

    whole = lambda *arrays: [(x.shape[0], [(x, 0)]) for x in arrays]
    norm_far, *lows = line.move(
        whole(*early_far),
        *[[(cap, [(norm_high[c], m * cap)]) for c in (1, 2, 3)] for m in range(1, low)], name="pack_norm_y")
    lows = [swap(x, "expert", m + 1) for m, x in enumerate(lows)]
    rest = [(cap, [piece]) for c in (1, 2, 3) for piece in [(norm_high[c], 0)] + [(x, (c - 1) * cap) for x in lows]]
    norm_own, norm_rest = line.move(whole(*early) + rest, rest, name="pack_norm_x")
    norm_far = [norm_far, swap(norm_rest, "dp", far)]
    norm_core = swap(norm_own, "dp", 1)
    block = 256 if hidden % 256 == 0 else hidden

    def forward(parts, pieces):
        rows = sum(x.shape[0] for x in parts)
        piece = rows // pieces

        def body(*refs):
            ins = refs[: len(parts)]
            router_ref, in_ref, down_ref, rows_hbm, act_hbm, der_ref, gate_ref = refs[len(parts) : len(parts) + 7]
            sums, (rows_ref, act_ref, total, sems) = refs[len(parts) + 7 : -4], refs[-4:]
            at = 0
            for ref in ins:
                rows_ref[at : at + ref.shape[0], :] = ref[...]
                at += ref.shape[0]
            stores = [pltpu.make_async_copy(rows_ref, rows_hbm, sems.at[0]), pltpu.make_async_copy(act_ref, act_hbm, sems.at[1])]
            stores[0].start()
            for j in range(hidden // block):
                at = slice(j * block, (j + 1) * block)
                value, derivative = gelu_pair(mm(rows_ref[...], in_ref[:, at]))
                act = value.astype(BF)
                act_ref[:, at] = act
                der_ref[:, at] = derivative.astype(BF)
                term = mm(act, down_ref[at, :])
                total[...] = term if j == 0 else total[...] + term
            stores[1].start()
            for i in range(pieces):
                sums[i][...] = total[i * piece : (i + 1) * piece, :].astype(BF)
            logits = mm(rows_ref[...], router_ref[...], NT)
            lanes = lax.broadcasted_iota(jnp.int32, logits.shape, 1)
            picked = jnp.sum(jnp.where(lanes == lax.axis_index("expert"), logits, 0.0), axis=1, keepdims=True)
            gate_ref[...] = jax.nn.sigmoid(picked)
            for store in stores:
                store.wait()

        *results, = line.call(
            body,
            [shape((rows, width)), shape((rows, hidden)), shape((rows, hidden)), shape((rows, 1), F32)]
            + [shape((piece, width))] * pieces,
            (*parts, router_t, weight_in, weight_down),
            out_specs=[HBM] * 2 + [VMEM] * (2 + pieces),
            scratch=[pltpu.VMEM((rows, width), BF), pltpu.VMEM((rows, hidden), BF), pltpu.VMEM((rows, width), F32), DMA((2,))],
            vmem=20 * MIB, name="forward")
        return (*results[:4], results[4:])

    def backward(parts, gate, der, pieces):
        rows = sum(x.shape[0] for x in parts)
        piece = rows // pieces

        def body(*refs):
            ins, refs = refs[: len(parts)], refs[len(parts) :]
            gate_ref, der_ref, in_ref, down_ref, grads_hbm, pre_hbm = refs[:6]
            sums, (grads_ref, pre_ref, total, sems) = refs[6 : 6 + pieces], refs[6 + pieces :]
            first = 0
            for ref in ins:
                at = slice(first, first + ref.shape[0])
                first += ref.shape[0]
                grads_ref[at, :] = (gate_ref[at, :] * ref[...].astype(F32)).astype(BF)
            stores = [pltpu.make_async_copy(grads_ref, grads_hbm, sems.at[0]), pltpu.make_async_copy(pre_ref, pre_hbm, sems.at[1])]
            stores[0].start()
            for j in range(hidden // block):
                at = slice(j * block, (j + 1) * block)
                act_grad = mm(grads_ref[...], down_ref[at, :], NT)
                pre = (act_grad * der_ref[:, at].astype(F32)).astype(BF)
                pre_ref[:, at] = pre
                term = mm(pre, in_ref[:, at], NT)
                total[...] = term if j == 0 else total[...] + term
            stores[1].start()
            for i in range(pieces):
                sums[i][...] = total[i * piece : (i + 1) * piece, :].astype(BF)
            for store in stores:
                store.wait()

        grads, pre, *sums = line.call(
            body,
            [shape((rows, width)), shape((rows, hidden))] + [shape((piece, width))] * pieces,
            (*parts, gate, der, weight_in, weight_down),
            out_specs=[HBM] * 2 + [VMEM] * pieces,
            scratch=[pltpu.VMEM((rows, width), BF), pltpu.VMEM((rows, hidden), BF), pltpu.VMEM((rows, width), F32), DMA((2,))],
            vmem=20 * MIB, name="backward")
        return grads, pre, sums

    half = slots // 2

    def relay(x, pieces):
        each = slots // pieces
        first, second = x[0], x[-1]
        cut = first.shape[0]
        spans = [[(lo, hi) for lo, hi in ((i * each, min((i + 1) * each, cut)), (max(i * each, cut), (i + 1) * each)) if lo < hi]
                 for i in range(pieces)]
        taken = [[(hi - lo, [(first, lo) if hi <= cut else (second, lo - cut)]) for lo, hi in span] for span in spans]
        joined, *parts = line.move(whole(*x), *taken, name="relay")
        return [joined] + [swap(part, "dp", 1) for part in parts]

    own = forward([norm_own], 1)
    cot_own = line.move(whole(*cot_high), flops=WAIT, name="pack_cot_x")[0]
    cot_far = [swap(cot_own, "dp", far)]
    cot_core = swap(cot_own, "dp", 1)
    near = forward([norm_core], 1)
    near_out = swap(near[4][0], "dp", 1)
    whole_far, *pieces_far = relay(norm_far, PIECES)
    away = forward([whole_far], 1)
    cross = forward(pieces_far, PIECES)
    core_out = [swap(x, "dp", 1) for x in cross[4]]
    own_in = backward([cot_own], gate=own[3], der=own[2], pieces=1)
    far_out = line.move([(x.shape[0], [(away[4][0], i * x.shape[0]), (x, 0)]) for i, x in enumerate(core_out)], name="sum_core_out")[0]
    far_out = swap(far_out, "dp", far)
    whole_far, *pieces_far = relay(cot_far, 2)
    near_back = backward([cot_core], gate=near[3], der=near[2], pieces=1)
    near_in = swap(near_back[2][0], "dp", 1)
    away_in = backward([whole_far], gate=away[3], der=away[2], pieces=1)
    cross_back = backward(pieces_far, gate=cross[3], der=cross[2], pieces=2)
    core_in = [swap(x, "dp", 1) for x in cross_back[2]]
    fronts, backs = (own, near, away, cross), (own_in, near_back, away_in, cross_back)
    keep_n, ikeep_n, ikeep_f = own[4][0], own_in[2][0], away_in[2][0]
    far_in = [swap(line.move([(half, [(ikeep_f, 0), (core_in[0], 0)])], name="sum_core_in")[0], "dp", far)]

    def weight_grad(lefts, rights):
        left, right = lefts[0].shape[1], rights[0].shape[1]
        tile = 256 if left % 256 == 0 else left

        def body(*refs):
            count = len(lefts) + len(rights)
            out_hbm, left_ref, right_ref, result, sems = refs[count:]
            loads = []
            for group, ref in ((refs[: len(lefts)], left_ref), (refs[len(lefts) : count], right_ref)):
                at = 0
                for src in group:
                    loads.append(pltpu.make_async_copy(src, ref.at[at : at + src.shape[0], :], sems.at[len(loads)]))
                    loads[-1].start()
                    at += src.shape[0]
            for load in loads:
                load.wait()
            stores = []
            for i in range(left // tile):
                at = slice(i * tile, (i + 1) * tile)
                result[at, :] = mm(left_ref[:, at], right_ref[...], TN).astype(BF)
                stores.append(pltpu.make_async_copy(result.at[at, :], out_hbm.at[at, :], sems.at[count + i]))
                stores[-1].start()
            for store in stores:
                store.wait()

        return line.call(
            body, [shape((left, right))], (*lefts, *rights), specs=[HBM] * (len(lefts) + len(rights)), out_specs=[HBM],
            scratch=[pltpu.VMEM((4 * slots, left), BF), pltpu.VMEM((4 * slots, right), BF), pltpu.VMEM((left, right), BF),
                     DMA((len(lefts) + len(rights) + left // tile,))],
            vmem=20 * MIB, name="weights")[0]

    quarter = slots // 4
    sums = line.move(
        *[[(quarter, [(x, c * quarter) for x in (keep_n, near_out, far_out)])] for c in range(4)], name="sum_x_out")
    out_high = [swap(x, "expert", masks[c] * low) if masks[c] else x for c, x in enumerate(sums)]

    far_in.append(swap(line.move([(half, [(ikeep_f, half), (core_in[1], 0)])], name="sum_core_in")[0], "dp", far))

    def gather_in(i):
        terms = lambda at, rows: (rows, [(ikeep_n, i * half + at), (near_in, i * half + at), (far_in[i], at)])
        total, *lows = line.move(
            [terms(0, half)], *[[terms(j * size + m * cap, cap) for j in range(2)] for m in range(1, low)], name="sum_x_in")
        return total, [swap(x, "expert", m + 1) for m, x in enumerate(lows)]

    def send_back(i, total, lows):
        blocks = line.move(
            *[[(cap, [(total, j * size)])] + [(cap, [(x, j * cap)]) for x in lows] for j in range(2)], name="pack_back_z")
        return [swap(b, "expert", masks[c] * low) if masks[c] else b for c, b in zip(chunks[i], blocks)]

    total_a = gather_in(0)
    grad_w_down = weight_grad([f[1] for f in fronts], [b[0] for b in backs])
    total_b = gather_in(1)
    out_low = []
    if low > 1:
        out_low = line.move(*[[(cap, [(x, m * cap)]) for x in out_high] for m in range(1, low)], name="pack_out_y")
    back_in = send_back(0, *total_a)
    back_in += send_back(1, *total_b)
    if low > 1:
        out_low = line.move(*[[(2 * cap, [(x, i * 2 * cap)])] for x in out_low for i in range(2)], name="pass_out_y")
        out_low = [swap(x, "expert", i // 2 + 1) for i, x in enumerate(out_low)]
    back_a = line.move([(x.shape[0], [(x, 0)]) for x in back_in[:2]], name="pack_back")[0]
    back_out = line.move(
        [(cap, [piece]) for c in range(4) for piece in [(out_high[c], 0)] + [(out_low[2 * m + c // 2], c % 2 * cap) for m in range(low - 1)]],
        name="pack_out")

    spare = -(-experts // TILE) * TILE
    span = width + spare

    def combine_body(*refs):
        back_ref, placed_ref, ids_ref, router_ref, resid_ref, cot_ref, normed_ref, out_ref, table_ref, local_ref = refs
        logits = mm(router_ref[...], normed_ref[...], NT)
        gates = [jax.nn.sigmoid(jnp.sum(logits * h, axis=0, keepdims=True)) for h in hot_rows(ids_ref, 0, experts)]
        ids_f = ids_ref[...].astype(F32)
        cols = jnp.concatenate(gates + [ids_f] * 3, axis=0).T
        held = back_ref[...]
        cot_f = cot_ref[...].astype(F32)
        total = resid_ref[...].astype(F32)
        table = jnp.zeros((tok, LANES), F32)
        for k in range(2):
            gate = cols[:, k : k + 1]
            taken = mm(at_rows([placed_ref[k : k + 1, :]], slots), held, TN)
            total = total + gate * taken
            logit = jnp.sum(cot_f * taken, axis=1, keepdims=True) * gate * (1.0 - gate)
            table = table + onehot(cols[:, 2 + k : 3 + k].astype(jnp.int32), LANES) * logit
        out_ref[...] = total.astype(BF)
        table = table.astype(BF)
        table_ref[...] = table
        local_ref[...] = mm(table, normed_ref[...], TN)[:spare, :].astype(BF)

    output, table, local_router = line.call(
        combine_body, [shape((tok, width)), shape((tok, LANES)), shape((spare, width))],
        (*back_out, placed, ids_t, router_t, resid, cotangent, normed),
        name="combine")

    tile = max(per, LANES)

    def products(odd, ctx_ref, grad_ref, local_ref, turned, out):
        me, mine = lax.axis_index("expert"), lax.axis_index("dp")
        for d in range(far):
            at = pl.ds(pl.multiple_of((mine ^ (2 * d + odd)) * part, LANES), part)
            turned[:, d * part : (d + 1) * part] = grad_ref[:, at]
            out[d * span + width : (d + 1) * span, :] = local_ref[:, at]
        for i in range(width // tile):
            block = mm(ctx_ref[:, i * tile : (i + 1) * tile], turned[...], TN).astype(BF)
            for j in range(tile // per):
                spot, lower = order((i * (tile // per) + j) ^ me)
                to = (spot * low + lower) * per
                for d in range(far):
                    out[pl.ds(pl.multiple_of(d * span + to, TILE), per), :] = (
                        block[j * per : (j + 1) * per, d * part : (d + 1) * part])

    def tail_body(*refs):
        backs = refs[:3]
        (placed_ref, table_ref, router_ref, resid_ref, inv_ref, local_ref, cot_hbm, ctx_hbm,
         grad_out, grad_ref, ctx_ref, send_ref, cot_ref, turned, sems) = refs[3:]
        loads = [pltpu.make_async_copy(src, dst, sems.at[i]) for i, (src, dst) in enumerate(
            ((cot_hbm, cot_ref), (ctx_hbm, ctx_ref)))]
        for load in loads:
            load.start()
        held = jnp.concatenate([b[...] for b in backs], axis=0)
        where = at_rows([placed_ref[k : k + 1, :] for k in range(2)], slots)
        normed_grad = mm(where, held, TN) + mm(table_ref[:, :experts], router_ref[...])
        resid_f = resid_ref[...].astype(F32)
        inv_col = inv_ref[...]
        mean_term = jnp.mean(normed_grad * resid_f, axis=1, keepdims=True)
        loads[0].wait()
        grad_ref[...] = (cot_ref[...].astype(F32) + inv_col * normed_grad
                         - (inv_col * inv_col * inv_col * mean_term) * resid_f).astype(BF)
        loads[1].wait()
        grad_out[...] = grad_ref[...]
        products(1, ctx_ref, grad_ref, local_ref, turned, send_ref)

    grad_tokens, grad_near, ctx_near, send = line.call(
        tail_body, [shape((tok, width))] * 3 + [ shape((far * span, part))],
        (back_a, *back_in[2:], placed, table, router_t, resid, inv, local_router, cotangent, context),
        specs=[VMEM] * 9 + [HBM] * 2,
        scratch=[pltpu.VMEM((tok, width), BF), pltpu.VMEM((tok, far * part), BF), DMA((2,))],
        vmem=16 * MIB, name="tail")
    core = swap(send, "dp", 1)

    def keep_body(ctx_ref, grad_ref, local_ref, w_out_ref, grad_ctx_ref, keep_ref, turned):
        products(0, ctx_ref, grad_ref, local_ref, turned, keep_ref)
        grad_ctx_ref[...] = mm(grad_ref[...], w_out_ref[...], NT).astype(BF)

    grad_context, keep = line.call(
        keep_body, [shape((tok, width)), shape((far * span, part))], (ctx_near, grad_near, local_router, w_out),
        scratch=[pltpu.VMEM((tok, far * part), BF)], vmem=16 * MIB, name="keep")

    spot = lambda d, c, m: d * span + (c * low + m) * per
    two = lambda first: [(keep, first), (core, first)]
    group = [(spare, two(width))]
    sum_x = line.move(
        [(2 * low * per, two(span)), (spare, two(span + width))],
        *[[(per, two(spot(d, c, m))) for d in range(2) for c in (2, 3)] for m in range(1, low)], name="reduce_core")
    grad_w_in = weight_grad([f[0] for f in fronts], [b[1] for b in backs])
    first_x = swap(sum_x[0], "dp", far)
    second_low = [swap(x, "expert", m + 1) for m, x in enumerate(sum_x[1:])]
    first = line.move(
        *[[(per, two(spot(0, c, m)) + [(first_x, (c * low + m) * per)]) for c in (0, 1)]
          + [(spare, two(width) + [(first_x, 2 * low * per)])] for m in range(low)], name="reduce_x")
    first_low = [swap(x, "expert", m) for m, x in enumerate(first) if m]
    second = line.move(
        *[[(per, two(spot(d, c, 0)) + [(x, (d * 2 + i) * per) for x in second_low]) for i, c in enumerate((2, 3))]
          for d in (1, 0)], name="reduce_y")
    second_x = swap(second[0], "dp", far)
    router_terms = [(x, 2 * per) for x in [first[0], *first_low]]
    blocks = line.move(
        *[[(per, [(x, c * per) for x in [first[0], *first_low]]), (spare, router_terms)] for c in (0, 1)],
        *[[(per, [(second[1], c * per), (second_x, c * per)]), (spare, router_terms)] for c in (0, 1)], name="reduce_xy")
    blocks = [blocks[0]] + [swap(blocks[c], "expert", masks[c] * low) for c in (1, 2, 3)]
    own = line.move([(per + spare, [(b, 0) for b in blocks])], name="reduce_z")[0]
    quarters = [own] + [swap(own, "dp", m) for m in range(1, dp)]

    def final_body(*refs):
        me, mine = lax.axis_index("expert"), lax.axis_index("dp")
        out_ref, router_ref = refs[dp:]
        for m in range(dp):
            at = pl.ds(pl.multiple_of((mine ^ m) * part, LANES), part)
            out_ref[:, at] = refs[m][:per, :].astype(F32)
            table = refs[m][per:, :].astype(F32)
            rows = lax.broadcasted_iota(jnp.int32, table.shape, 0)
            router_ref[:, at] = jnp.sum(jnp.where(rows == me, table, 0.0), axis=0, keepdims=True)

    grad_w_out, grad_w_router = line.call(
        final_body, [shape((per, width), F32), shape((1, width), F32)], quarters, name="final")

    return (
        output,
        grad_tokens,
        grad_context,
        grad_w_out,
        grad_w_router.reshape(width, 1),
        grad_w_in.reshape(1, width, hidden),
        grad_w_down.reshape(1, hidden, width),
    )


def solution(mesh):
    split = P(("dp", "expert"), None)
    return jax.shard_map(
        on_device,
        mesh=mesh,
        in_specs=(split, split, P(), P(), split, P("expert", None, "dp"), P("expert", "dp", None), split),
        out_specs=(split, split, split, P("expert", None), P(None, "expert"), P("expert", None, "dp"),
                   P("expert", "dp", None)),
        check_vma=False,
    )
```

```python
import functools

import jax
import jax.numpy as jnp
from jax import lax
from jax.experimental import pallas as pl
from jax.experimental.pallas import tpu as pltpu
from jax.sharding import PartitionSpec as P

GELU_C = 0.7978845608028654
GELU_A = 0.044715
EPSILON = 1e-06
BF = jnp.bfloat16
F32 = jnp.float32
LANES = 128
TILE = 16
MIB = 1024 * 1024
WAIT = 20 * 10**9
PIECES = 4

NN = (((1,), (0,)), ((), ()))
NT = (((1,), (1,)), ((), ()))
TN = (((0,), (0,)), ((), ()))

VMEM = pl.BlockSpec(memory_space=pltpu.VMEM)
ANY = pl.BlockSpec(memory_space=pl.ANY)
HBM = pl.BlockSpec(memory_space=pltpu.HBM)
DMA = pltpu.SemaphoreType.DMA


def mm(a, b, dims=NN):
    return lax.dot_general(a, b, dims, preferred_element_type=F32)


def shape(dims, dtype=BF):
    return jax.ShapeDtypeStruct(dims, dtype)


def gelu_pair(preact):
    square = preact * preact
    tangent = jnp.tanh(GELU_C * (preact + GELU_A * (square * preact)))
    half = 0.5 * (1.0 + tangent)
    derivative = half + (0.5 * GELU_C) * preact * (1.0 - tangent * tangent) * (
        1.0 + 3.0 * GELU_A * square
    )
    return preact * half, derivative


class Line:
    def __init__(self):
        self.last = None

    def call(self, body, outs, args, specs=None, out_specs=None, scratch=(), flops=0, vmem=8 * MIB, name=None):
        args, specs = list(args), list(specs) if specs is not None else [VMEM] * len(args)
        out_specs = list(out_specs) if out_specs is not None else [VMEM] * len(outs)
        count, given = len(args), len(outs)
        if self.last is not None:
            args.append(self.last)
            specs.append(ANY)

        def kernel(*refs):
            results = refs[len(args) :]
            results[given][...] = jnp.zeros((8, LANES), F32)
            body(*refs[:count], *results[:given], *results[given + 1 :])

        *results, self.last = pl.pallas_call(
            kernel,
            out_shape=[*outs, shape((8, LANES), F32)],
            in_specs=specs,
            out_specs=[*out_specs, VMEM],
            scratch_shapes=scratch,
            compiler_params=pltpu.CompilerParams(vmem_limit_bytes=vmem),
            cost_estimate=pl.CostEstimate(flops=flops, bytes_accessed=0, transcendentals=0),
            name=name,
        )(*args)
        return results

    def move(self, *outputs, flops=0, hold=(), name="move"):
        arrays, places = [], {}
        aligned = True
        for pieces in outputs:
            for rows, terms in pieces:
                aligned = aligned and rows % TILE == 0
                for array, first in terms:
                    aligned = aligned and first % TILE == 0
                    if id(array) not in places:
                        places[id(array)] = len(arrays)
                        arrays.append(array)
        width = arrays[0].shape[1]
        if not aligned:
            return [
                jnp.concatenate([
                    added(*[a[f : f + rows] for a, f in terms]) if len(terms) > 1 else terms[0][0][terms[0][1] : terms[0][1] + rows]
                    for rows, terms in pieces
                ])
                for pieces in outputs
            ]

        def body(*refs):
            for pieces, out in zip(outputs, refs[len(arrays) + len(hold) :]):
                at = 0
                for rows, terms in pieces:
                    parts = [refs[places[id(a)]][f : f + rows, :] for a, f in terms]
                    if len(parts) > 1:
                        parts = [functools.reduce(jnp.add, [p.astype(F32) for p in parts]).astype(BF)]
                    out[at : at + rows, :] = parts[0]
                    at += rows

        outs = [shape((sum(rows for rows, _ in pieces), width)) for pieces in outputs]
        return self.call(body, outs, arrays + list(hold), flops=flops, name=name)


def added(*terms):
    return functools.reduce(jnp.add, [t.astype(F32) for t in terms]).astype(BF)


def swap(x, axis, mask):
    return lax.ppermute(x, axis, [(i, i ^ mask) for i in range(lax.axis_size(axis))])


def hot_rows(ids_ref, rel_to, count):
    tok = ids_ref.shape[1]
    rows = lax.broadcasted_iota(jnp.int32, (count, tok), 0)
    return [(rows == (ids_ref[k : k + 1, :] ^ rel_to)).astype(F32) for k in range(2)]


def at_rows(places, total):
    tok = places[0].shape[1]
    rows = lax.broadcasted_iota(jnp.int32, (total, tok), 0)
    return functools.reduce(jnp.add, [(rows == p).astype(F32) for p in places]).astype(BF)


def onehot(column, width):
    lanes = lax.broadcasted_iota(jnp.int32, (column.shape[0], width), 1)
    return (lanes == column).astype(F32)


def on_device(tokens, context, w_out, w_router, expert_ids, w_in, w_down, cotangent):
    tok, width = tokens.shape
    experts = lax.axis_size("expert")
    dp = lax.axis_size("dp")
    far = dp // 2
    cap = 2 * tok // experts
    slots = 2 * tok
    hidden = w_in.shape[2]
    masks = [0, 2, 1, 3]
    low = experts // len(masks)
    shift = low.bit_length() - 1
    chunks = [[0, 1], [2, 3]]
    size = low * cap
    ids_t = expert_ids.T
    router_t = w_router.T
    weight_in, weight_down = w_in[0], w_down[0]
    per = width // experts
    part = width // dp
    line = Line()

    def order(rel):
        high = rel >> shift
        return (high >> 1) | ((high & 1) << 1), rel & (low - 1)

    def head_body(ids_hbm, cot_hbm, tok_hbm, ctx_hbm, w_out_hbm, *refs):
        outs, copies = refs[: 2 * low + 7], refs[2 * low + 7 :]
        lows, (placed_ref, resid_ref, inv_ref, normed_ref), sends = outs[:low], outs[low : low + 4], outs[low + 4 :]
        held, sems = copies[:5], copies[5]
        me = lax.axis_index("expert")
        ids_ref, ctx_ref, w_out_ref, tok_ref, cot_ref = held
        quarter = width // 4
        rows_of = [slice(i * quarter, (i + 1) * quarter) for i in range(4)]
        pairs = [(ids_hbm, ids_ref), (ctx_hbm, ctx_ref)] + [(w_out_hbm.at[r, :], w_out_ref.at[r, :]) for r in rows_of]
        pairs += [(tok_hbm, tok_ref), (cot_hbm, cot_ref)]
        loads = [pltpu.make_async_copy(src, dst, sems.at[i]) for i, (src, dst) in enumerate(pairs)]
        for load in loads:
            load.start()
        loads[0].wait()
        rows = lax.broadcasted_iota(jnp.int32, (tok, tok), 0)
        cols = lax.broadcasted_iota(jnp.int32, (tok, tok), 1)
        upper = (rows < cols).astype(BF)
        hot = hot_rows(ids_ref, me, experts)
        before = [mm(h.astype(BF), upper) for h in hot]
        first = jnp.sum(hot[0], axis=1, keepdims=True)
        rank = [jnp.sum(before[0] * hot[0], axis=0, keepdims=True),
                jnp.sum((before[1] + first) * hot[1], axis=0, keepdims=True)]
        places, spots = [], []
        for k in range(2):
            block, lower = order(ids_ref[k : k + 1, :] ^ me)
            places.append((block * low + lower) * cap + rank[k].astype(jnp.int32))
            placed_ref[k : k + 1, :] = places[k]
            spots.append((lower * len(masks) + block) * cap + rank[k].astype(jnp.int32))
        loads[1].wait()
        attn = None
        for i, r in enumerate(rows_of):
            loads[2 + i].wait()
            term = mm(ctx_ref[:, r], w_out_ref[r, :])
            attn = term if attn is None else attn + term
        loads[6].wait()
        resid = (tok_ref[...].astype(F32) + attn).astype(BF)
        resid_ref[...] = resid
        resid_f = resid.astype(F32)
        inv = lax.rsqrt(jnp.mean(resid_f * resid_f, axis=1, keepdims=True) + EPSILON)
        inv_ref[...] = inv
        normed = (resid_f * inv).astype(BF)
        normed_ref[...] = normed
        moved = mm(at_rows(places, slots), normed).astype(BF)
        for m in range(low):
            sends[m][...] = moved[m * cap : (m + 1) * cap, :]
        for c in range(1, 4):
            sends[low + c - 1][...] = moved[c * size : (c + 1) * size, :]
        loads[7].wait()
        moved = mm(at_rows(spots, slots), cot_ref[...]).astype(BF)
        each = slots // low
        for m in range(low):
            lows[m][...] = moved[m * each : (m + 1) * each, :]

    outs = line.call(
        head_body,
        [shape((slots // low, width))] * low + [shape((2, tok), jnp.int32)]
        + [shape((tok, width)), shape((tok, 1), F32), shape((tok, width))] + [shape((cap, width))] * low + [shape((size, width))] * 3,
        (ids_t, cotangent, tokens, context, w_out), specs=[HBM] * 5,
        scratch=[pltpu.VMEM((2, tok), jnp.int32), pltpu.VMEM((tok, width), BF), pltpu.VMEM((width, width), BF),
                 pltpu.VMEM((tok, width), BF), pltpu.VMEM((tok, width), BF), DMA((8,))],
        vmem=53 * MIB, name="head")
    cot_low, (placed, resid, inv, normed), sends = outs[:low], outs[low : low + 4], outs[low + 4 :]
    cot_low = [cot_low[0]] + [swap(cot_low[m], "expert", m) for m in range(1, low)]
    norm_zero = [sends[0]] + [swap(sends[m], "expert", m) for m in range(1, low)]
    norm_high = [None] + [swap(sends[low + c - 1], "expert", masks[c] * low) for c in (1, 2, 3)]
    halves = [range(low)[: low // 2], range(low)[low // 2 :]]
    early = line.move(
        *[[(cap, [(norm_zero[m], 0)]) for m in part] for part in halves],
        *[[(cap, [(cot_low[m], c * cap)]) for m in range(low)] for c in range(4)], hold=(weight_in, weight_down), name="pack_zero")
    early, cot_high = early[:2], [swap(x, "expert", masks[c] * low) if masks[c] else x for c, x in enumerate(early[2:])]
    early_far = [swap(x, "dp", far) for x in early]

    whole = lambda *arrays: [(x.shape[0], [(x, 0)]) for x in arrays]
    norm_far, *lows = line.move(
        whole(*early_far),
        *[[(cap, [(norm_high[c], m * cap)]) for c in (1, 2, 3)] for m in range(1, low)], name="pack_norm_y")
    lows = [swap(x, "expert", m + 1) for m, x in enumerate(lows)]
    rest = [(cap, [piece]) for c in (1, 2, 3) for piece in [(norm_high[c], 0)] + [(x, (c - 1) * cap) for x in lows]]
    norm_own, norm_rest = line.move(whole(*early) + rest, rest, name="pack_norm_x")
    norm_far = [norm_far, swap(norm_rest, "dp", far)]
    norm_core = swap(norm_own, "dp", 1)
    block = 256 if hidden % 256 == 0 else hidden

    def forward(parts, pieces):
        rows = sum(x.shape[0] for x in parts)
        piece = rows // pieces

        def body(*refs):
            ins = refs[: len(parts)]
            router_ref, in_ref, down_ref, rows_hbm, act_hbm, der_ref, gate_ref = refs[len(parts) : len(parts) + 7]
            sums, (rows_ref, act_ref, total, sems) = refs[len(parts) + 7 : -4], refs[-4:]
            at = 0
            for ref in ins:
                rows_ref[at : at + ref.shape[0], :] = ref[...]
                at += ref.shape[0]
            stores = [pltpu.make_async_copy(rows_ref, rows_hbm, sems.at[0]), pltpu.make_async_copy(act_ref, act_hbm, sems.at[1])]
            stores[0].start()
            for j in range(hidden // block):
                at = slice(j * block, (j + 1) * block)
                value, derivative = gelu_pair(mm(rows_ref[...], in_ref[:, at]))
                act = value.astype(BF)
                act_ref[:, at] = act
                der_ref[:, at] = derivative.astype(BF)
                term = mm(act, down_ref[at, :])
                total[...] = term if j == 0 else total[...] + term
            stores[1].start()
            for i in range(pieces):
                sums[i][...] = total[i * piece : (i + 1) * piece, :].astype(BF)
            logits = mm(rows_ref[...], router_ref[...], NT)
            lanes = lax.broadcasted_iota(jnp.int32, logits.shape, 1)
            picked = jnp.sum(jnp.where(lanes == lax.axis_index("expert"), logits, 0.0), axis=1, keepdims=True)
            gate_ref[...] = jax.nn.sigmoid(picked)
            for store in stores:
                store.wait()

        *results, = line.call(
            body,
            [shape((rows, width)), shape((rows, hidden)), shape((rows, hidden)), shape((rows, 1), F32)]
            + [shape((piece, width))] * pieces,
            (*parts, router_t, weight_in, weight_down),
            out_specs=[HBM] * 2 + [VMEM] * (2 + pieces),
            scratch=[pltpu.VMEM((rows, width), BF), pltpu.VMEM((rows, hidden), BF), pltpu.VMEM((rows, width), F32), DMA((2,))],
            vmem=20 * MIB, name="forward")
        return (*results[:4], results[4:])

    def backward(parts, gate, der, pieces):
        rows = sum(x.shape[0] for x in parts)
        piece = rows // pieces

        def body(*refs):
            ins, refs = refs[: len(parts)], refs[len(parts) :]
            gate_ref, der_ref, in_ref, down_ref, grads_hbm, pre_hbm = refs[:6]
            sums, (grads_ref, pre_ref, total, sems) = refs[6 : 6 + pieces], refs[6 + pieces :]
            first = 0
            for ref in ins:
                at = slice(first, first + ref.shape[0])
                first += ref.shape[0]
                grads_ref[at, :] = (gate_ref[at, :] * ref[...].astype(F32)).astype(BF)
            stores = [pltpu.make_async_copy(grads_ref, grads_hbm, sems.at[0]), pltpu.make_async_copy(pre_ref, pre_hbm, sems.at[1])]
            stores[0].start()
            for j in range(hidden // block):
                at = slice(j * block, (j + 1) * block)
                act_grad = mm(grads_ref[...], down_ref[at, :], NT)
                pre = (act_grad * der_ref[:, at].astype(F32)).astype(BF)
                pre_ref[:, at] = pre
                term = mm(pre, in_ref[:, at], NT)
                total[...] = term if j == 0 else total[...] + term
            stores[1].start()
            for i in range(pieces):
                sums[i][...] = total[i * piece : (i + 1) * piece, :].astype(BF)
            for store in stores:
                store.wait()

        grads, pre, *sums = line.call(
            body,
            [shape((rows, width)), shape((rows, hidden))] + [shape((piece, width))] * pieces,
            (*parts, gate, der, weight_in, weight_down),
            out_specs=[HBM] * 2 + [VMEM] * pieces,
            scratch=[pltpu.VMEM((rows, width), BF), pltpu.VMEM((rows, hidden), BF), pltpu.VMEM((rows, width), F32), DMA((2,))],
            vmem=20 * MIB, name="backward")
        return grads, pre, sums

    half = slots // 2

    def relay(x, pieces):
        each = slots // pieces
        first, second = x[0], x[-1]
        cut = first.shape[0]
        spans = [[(lo, hi) for lo, hi in ((i * each, min((i + 1) * each, cut)), (max(i * each, cut), (i + 1) * each)) if lo < hi]
                 for i in range(pieces)]
        taken = [[(hi - lo, [(first, lo) if hi <= cut else (second, lo - cut)]) for lo, hi in span] for span in spans]
        joined, *parts = line.move(whole(*x), *taken, name="relay")
        return [joined] + [swap(part, "dp", 1) for part in parts]

    own = forward([norm_own], 1)
    cot_own = line.move(whole(*cot_high), flops=WAIT, name="pack_cot_x")[0]
    cot_far = [swap(cot_own, "dp", far)]
    cot_core = swap(cot_own, "dp", 1)
    near = forward([norm_core], 1)
    near_out = swap(near[4][0], "dp", 1)
    whole_far, *pieces_far = relay(norm_far, PIECES)
    away = forward([whole_far], 1)
    cross = forward(pieces_far, PIECES)
    core_out = [swap(x, "dp", 1) for x in cross[4]]
    own_in = backward([cot_own], gate=own[3], der=own[2], pieces=1)
    far_out = line.move([(x.shape[0], [(away[4][0], i * x.shape[0]), (x, 0)]) for i, x in enumerate(core_out)], name="sum_core_out")[0]
    far_out = swap(far_out, "dp", far)
    whole_far, *pieces_far = relay(cot_far, 2)
    near_back = backward([cot_core], gate=near[3], der=near[2], pieces=1)
    near_in = swap(near_back[2][0], "dp", 1)
    away_in = backward([whole_far], gate=away[3], der=away[2], pieces=1)
    cross_back = backward(pieces_far, gate=cross[3], der=cross[2], pieces=2)
    core_in = [swap(x, "dp", 1) for x in cross_back[2]]
    fronts, backs = (own, near, away, cross), (own_in, near_back, away_in, cross_back)
    keep_n, ikeep_n, ikeep_f = own[4][0], own_in[2][0], away_in[2][0]
    far_in = [swap(line.move([(half, [(ikeep_f, 0), (core_in[0], 0)])], name="sum_core_in")[0], "dp", far)]

    def weight_grad(lefts, rights):
        left, right = lefts[0].shape[1], rights[0].shape[1]
        tile = 256 if left % 256 == 0 else left

        def body(*refs):
            count = len(lefts) + len(rights)
            out_hbm, left_ref, right_ref, result, sems = refs[count:]
            loads = []
            for group, ref in ((refs[: len(lefts)], left_ref), (refs[len(lefts) : count], right_ref)):
                at = 0
                for src in group:
                    loads.append(pltpu.make_async_copy(src, ref.at[at : at + src.shape[0], :], sems.at[len(loads)]))
                    loads[-1].start()
                    at += src.shape[0]
            for load in loads:
                load.wait()
            stores = []
            for i in range(left // tile):
                at = slice(i * tile, (i + 1) * tile)
                result[at, :] = mm(left_ref[:, at], right_ref[...], TN).astype(BF)
                stores.append(pltpu.make_async_copy(result.at[at, :], out_hbm.at[at, :], sems.at[count + i]))
                stores[-1].start()
            for store in stores:
                store.wait()

        return line.call(
            body, [shape((left, right))], (*lefts, *rights), specs=[HBM] * (len(lefts) + len(rights)), out_specs=[HBM],
            scratch=[pltpu.VMEM((4 * slots, left), BF), pltpu.VMEM((4 * slots, right), BF), pltpu.VMEM((left, right), BF),
                     DMA((len(lefts) + len(rights) + left // tile,))],
            vmem=20 * MIB, name="weights")[0]

    tile = max(per, LANES)

    def turn_body(ctx_ref, out_ref):
        for i in range(width // tile):
            turned = ctx_ref[:, i * tile : (i + 1) * tile].astype(F32).T.astype(BF)
            for j in range(tile // per):
                spot, lower = order((i * (tile // per) + j) ^ lax.axis_index("expert"))
                at = pl.ds(pl.multiple_of((spot * low + lower) * per, TILE), per)
                out_ref[at, :] = turned[j * per : (j + 1) * per, :]

    context_t = line.call(turn_body, [shape((width, tok))], (context,), name="turn")[0]

    quarter = slots // 4
    sums = line.move(
        *[[(quarter, [(x, c * quarter) for x in (keep_n, near_out, far_out)])] for c in range(4)], name="sum_x_out")
    out_high = [swap(x, "expert", masks[c] * low) if masks[c] else x for c, x in enumerate(sums)]

    far_in.append(swap(line.move([(half, [(ikeep_f, half), (core_in[1], 0)])], name="sum_core_in")[0], "dp", far))

    def gather_in(i):
        terms = lambda at, rows: (rows, [(ikeep_n, i * half + at), (near_in, i * half + at), (far_in[i], at)])
        total, *lows = line.move(
            [terms(0, half)], *[[terms(j * size + m * cap, cap) for j in range(2)] for m in range(1, low)], name="sum_x_in")
        return total, [swap(x, "expert", m + 1) for m, x in enumerate(lows)]

    def send_back(i, total, lows):
        blocks = line.move(
            *[[(cap, [(total, j * size)])] + [(cap, [(x, j * cap)]) for x in lows] for j in range(2)], name="pack_back_z")
        return [swap(b, "expert", masks[c] * low) if masks[c] else b for c, b in zip(chunks[i], blocks)]

    total_a = gather_in(0)
    grad_w_down = weight_grad([f[1] for f in fronts], [b[0] for b in backs])
    total_b = gather_in(1)
    out_low = []
    if low > 1:
        out_low = line.move(*[[(cap, [(x, m * cap)]) for x in out_high] for m in range(1, low)], name="pack_out_y")
    back_in = send_back(0, *total_a)
    if low > 1:
        out_low = line.move(*[[(2 * cap, [(x, i * 2 * cap)])] for x in out_low for i in range(2)], name="pass_out_y")
        out_low = [swap(x, "expert", i // 2 + 1) for i, x in enumerate(out_low)]
    back_in += send_back(1, *total_b)
    back_a = line.move([(x.shape[0], [(x, 0)]) for x in back_in[:2]], name="pack_back")[0]
    back_out = line.move(
        [(cap, [piece]) for c in range(4) for piece in [(out_high[c], 0)] + [(out_low[2 * m + c // 2], c % 2 * cap) for m in range(low - 1)]],
        name="pack_out")

    spare = -(-experts // TILE) * TILE
    span = width + spare

    def combine_body(*refs):
        back_ref, placed_ref, ids_ref, router_ref, resid_ref, cot_ref, normed_ref, out_ref, table_ref, local_ref = refs
        logits = mm(router_ref[...], normed_ref[...], NT)
        gates = [jax.nn.sigmoid(jnp.sum(logits * h, axis=0, keepdims=True)) for h in hot_rows(ids_ref, 0, experts)]
        ids_f = ids_ref[...].astype(F32)
        cols = jnp.concatenate(gates + [ids_f] * 3, axis=0).T
        held = back_ref[...]
        cot_f = cot_ref[...].astype(F32)
        total = resid_ref[...].astype(F32)
        table = jnp.zeros((tok, LANES), F32)
        for k in range(2):
            gate = cols[:, k : k + 1]
            taken = mm(at_rows([placed_ref[k : k + 1, :]], slots), held, TN)
            total = total + gate * taken
            logit = jnp.sum(cot_f * taken, axis=1, keepdims=True) * gate * (1.0 - gate)
            table = table + onehot(cols[:, 2 + k : 3 + k].astype(jnp.int32), LANES) * logit
        out_ref[...] = total.astype(BF)
        table = table.astype(BF)
        table_ref[...] = table
        local_ref[...] = mm(table, normed_ref[...], TN)[:spare, :].astype(BF)

    output, table, local_router = line.call(
        combine_body, [shape((tok, width)), shape((tok, LANES)), shape((spare, width))],
        (*back_out, placed, ids_t, router_t, resid, cotangent, normed),
        name="combine")

    def products(odd, ctx_ref, grad_ref, local_ref, turned, out):
        mine = lax.axis_index("dp")
        for d in range(far):
            at = pl.ds(pl.multiple_of((mine ^ (2 * d + odd)) * part, LANES), part)
            turned[:, d * part : (d + 1) * part] = grad_ref[:, at]
            out[d * span + width : (d + 1) * span, :] = local_ref[:, at]
        for i in range(0, width, part):
            block = mm(ctx_ref[i : i + part, :], turned[...]).astype(BF)
            for d in range(far):
                out[d * span + i : d * span + i + part, :] = block[:, d * part : (d + 1) * part]

    def tail_body(*refs):
        backs = refs[:3]
        (placed_ref, table_ref, router_ref, resid_ref, inv_ref, local_ref, cot_ref, ctx_ref,
         grad_out, grad_ref, send_ref, turned) = refs[3:]
        held = jnp.concatenate([b[...] for b in backs], axis=0)
        where = at_rows([placed_ref[k : k + 1, :] for k in range(2)], slots)
        normed_grad = mm(where, held, TN) + mm(table_ref[:, :experts], router_ref[...])
        resid_f = resid_ref[...].astype(F32)
        inv_col = inv_ref[...]
        mean_term = jnp.mean(normed_grad * resid_f, axis=1, keepdims=True)
        grad_ref[...] = (cot_ref[...].astype(F32) + inv_col * normed_grad
                         - (inv_col * inv_col * inv_col * mean_term) * resid_f).astype(BF)
        grad_out[...] = grad_ref[...]
        products(1, ctx_ref, grad_ref, local_ref, turned, send_ref)

    grad_tokens, grad_near, send = line.call(
        tail_body, [shape((tok, width))] * 2 + [ shape((far * span, part))],
        (back_a, *back_in[2:], placed, table, router_t, resid, inv, local_router, cotangent, context_t),
        scratch=[pltpu.VMEM((tok, far * part), BF)],
        vmem=16 * MIB, name="tail")
    core = swap(send, "dp", 1)

    def keep_body(ctx_ref, grad_ref, local_ref, w_out_ref, grad_ctx_ref, keep_ref, turned):
        products(0, ctx_ref, grad_ref, local_ref, turned, keep_ref)
        grad_ctx_ref[...] = mm(grad_ref[...], w_out_ref[...], NT).astype(BF)

    grad_context, keep = line.call(
        keep_body, [shape((tok, width)), shape((far * span, part))], (context_t, grad_near, local_router, w_out),
        scratch=[pltpu.VMEM((tok, far * part), BF)], vmem=16 * MIB, name="keep")

    spot = lambda d, c, m: d * span + (c * low + m) * per
    two = lambda first: [(keep, first), (core, first)]
    group = [(spare, two(width))]
    sum_x = line.move(
        [(2 * low * per, two(span)), (spare, two(span + width))],
        *[[(per, two(spot(d, c, m))) for d in range(2) for c in (2, 3)] for m in range(1, low)], name="reduce_core")
    grad_w_in = weight_grad([f[0] for f in fronts], [b[1] for b in backs])
    first_x = swap(sum_x[0], "dp", far)
    second_low = [swap(x, "expert", m + 1) for m, x in enumerate(sum_x[1:])]
    first = line.move(
        *[[(per, two(spot(0, c, m)) + [(first_x, (c * low + m) * per)]) for c in (0, 1)]
          + [(spare, two(width) + [(first_x, 2 * low * per)])] for m in range(low)], name="reduce_x")
    first_low = [swap(x, "expert", m) for m, x in enumerate(first) if m]
    second = line.move(
        *[[(per, two(spot(d, c, 0)) + [(x, (d * 2 + i) * per) for x in second_low]) for i, c in enumerate((2, 3))]
          for d in (1, 0)], name="reduce_y")
    second_x = swap(second[0], "dp", far)
    router_terms = [(x, 2 * per) for x in [first[0], *first_low]]
    blocks = line.move(
        *[[(per, [(x, c * per) for x in [first[0], *first_low]]), (spare, router_terms)] for c in (0, 1)],
        *[[(per, [(second[1], c * per), (second_x, c * per)]), (spare, router_terms)] for c in (0, 1)], name="reduce_xy")
    blocks = [blocks[0]] + [swap(blocks[c], "expert", masks[c] * low) for c in (1, 2, 3)]
    own = line.move([(per + spare, [(b, 0) for b in blocks])], name="reduce_z")[0]
    quarters = [own] + [swap(own, "dp", m) for m in range(1, dp)]

    def final_body(*refs):
        me, mine = lax.axis_index("expert"), lax.axis_index("dp")
        out_ref, router_ref = refs[dp:]
        for m in range(dp):
            at = pl.ds(pl.multiple_of((mine ^ m) * part, LANES), part)
            out_ref[:, at] = refs[m][:per, :].astype(F32)
            table = refs[m][per:, :].astype(F32)
            rows = lax.broadcasted_iota(jnp.int32, table.shape, 0)
            router_ref[:, at] = jnp.sum(jnp.where(rows == me, table, 0.0), axis=0, keepdims=True)

    grad_w_out, grad_w_router = line.call(
        final_body, [shape((per, width), F32), shape((1, width), F32)], quarters, name="final")

    return (
        output,
        grad_tokens,
        grad_context,
        grad_w_out,
        grad_w_router.reshape(width, 1),
        grad_w_in.reshape(1, width, hidden),
        grad_w_down.reshape(1, hidden, width),
    )


def solution(mesh):
    split = P(("dp", "expert"), None)
    return jax.shard_map(
        on_device,
        mesh=mesh,
        in_specs=(split, split, P(), P(), split, P("expert", None, "dp"), P("expert", "dp", None), split),
        out_specs=(split, split, split, P("expert", None), P(None, "expert"), P("expert", None, "dp"),
                   P("expert", "dp", None)),
        check_vma=False,
    )
```

```python
import functools

import jax
import jax.numpy as jnp
from jax import lax
from jax.experimental import pallas as pl
from jax.experimental.pallas import tpu as pltpu
from jax.sharding import PartitionSpec as P

GELU_C = 0.7978845608028654
GELU_A = 0.044715
EPSILON = 1e-06
BF = jnp.bfloat16
F32 = jnp.float32
LANES = 128
TILE = 16
MIB = 1024 * 1024
WAIT = 20 * 10**9
PIECES = 4

NN = (((1,), (0,)), ((), ()))
NT = (((1,), (1,)), ((), ()))
TN = (((0,), (0,)), ((), ()))

VMEM = pl.BlockSpec(memory_space=pltpu.VMEM)
ANY = pl.BlockSpec(memory_space=pl.ANY)
HBM = pl.BlockSpec(memory_space=pltpu.HBM)
DMA = pltpu.SemaphoreType.DMA


def mm(a, b, dims=NN):
    return lax.dot_general(a, b, dims, preferred_element_type=F32)


def shape(dims, dtype=BF):
    return jax.ShapeDtypeStruct(dims, dtype)


def gelu_pair(preact):
    square = preact * preact
    tangent = jnp.tanh(GELU_C * (preact + GELU_A * (square * preact)))
    half = 0.5 * (1.0 + tangent)
    derivative = half + (0.5 * GELU_C) * preact * (1.0 - tangent * tangent) * (
        1.0 + 3.0 * GELU_A * square
    )
    return preact * half, derivative


class Line:
    def __init__(self):
        self.last = None

    def call(self, body, outs, args, specs=None, out_specs=None, scratch=(), flops=0, vmem=8 * MIB, name=None):
        args, specs = list(args), list(specs) if specs is not None else [VMEM] * len(args)
        out_specs = list(out_specs) if out_specs is not None else [VMEM] * len(outs)
        count, given = len(args), len(outs)
        if self.last is not None:
            args.append(self.last)
            specs.append(ANY)

        def kernel(*refs):
            results = refs[len(args) :]
            results[given][...] = jnp.zeros((8, LANES), F32)
            body(*refs[:count], *results[:given], *results[given + 1 :])

        *results, self.last = pl.pallas_call(
            kernel,
            out_shape=[*outs, shape((8, LANES), F32)],
            in_specs=specs,
            out_specs=[*out_specs, VMEM],
            scratch_shapes=scratch,
            compiler_params=pltpu.CompilerParams(vmem_limit_bytes=vmem),
            cost_estimate=pl.CostEstimate(flops=flops, bytes_accessed=0, transcendentals=0),
            name=name,
        )(*args)
        return results

    def move(self, *outputs, flops=0, hold=(), name="move"):
        arrays, places = [], {}
        aligned = True
        for pieces in outputs:
            for rows, terms in pieces:
                aligned = aligned and rows % TILE == 0
                for array, first in terms:
                    aligned = aligned and first % TILE == 0
                    if id(array) not in places:
                        places[id(array)] = len(arrays)
                        arrays.append(array)
        width = arrays[0].shape[1]
        if not aligned:
            return [
                jnp.concatenate([
                    added(*[a[f : f + rows] for a, f in terms]) if len(terms) > 1 else terms[0][0][terms[0][1] : terms[0][1] + rows]
                    for rows, terms in pieces
                ])
                for pieces in outputs
            ]

        def body(*refs):
            for pieces, out in zip(outputs, refs[len(arrays) + len(hold) :]):
                at = 0
                for rows, terms in pieces:
                    parts = [refs[places[id(a)]][f : f + rows, :] for a, f in terms]
                    if len(parts) > 1:
                        parts = [functools.reduce(jnp.add, [p.astype(F32) for p in parts]).astype(BF)]
                    out[at : at + rows, :] = parts[0]
                    at += rows

        outs = [shape((sum(rows for rows, _ in pieces), width)) for pieces in outputs]
        return self.call(body, outs, arrays + list(hold), flops=flops, name=name)


def added(*terms):
    return functools.reduce(jnp.add, [t.astype(F32) for t in terms]).astype(BF)


def swap(x, axis, mask):
    return lax.ppermute(x, axis, [(i, i ^ mask) for i in range(lax.axis_size(axis))])


def hot_rows(ids_ref, rel_to, count):
    tok = ids_ref.shape[1]
    rows = lax.broadcasted_iota(jnp.int32, (count, tok), 0)
    return [(rows == (ids_ref[k : k + 1, :] ^ rel_to)).astype(F32) for k in range(2)]


def at_rows(places, total):
    tok = places[0].shape[1]
    rows = lax.broadcasted_iota(jnp.int32, (total, tok), 0)
    return functools.reduce(jnp.add, [(rows == p).astype(F32) for p in places]).astype(BF)


def onehot(column, width):
    lanes = lax.broadcasted_iota(jnp.int32, (column.shape[0], width), 1)
    return (lanes == column).astype(F32)


def on_device(tokens, context, w_out, w_router, expert_ids, w_in, w_down, cotangent):
    tok, width = tokens.shape
    experts = lax.axis_size("expert")
    dp = lax.axis_size("dp")
    far = dp // 2
    cap = 2 * tok // experts
    slots = 2 * tok
    hidden = w_in.shape[2]
    masks = [0, 2, 1, 3]
    low = experts // len(masks)
    shift = low.bit_length() - 1
    chunks = [[0, 1], [2, 3]]
    size = low * cap
    ids_t = expert_ids.T
    router_t = w_router.T
    weight_in, weight_down = w_in[0], w_down[0]
    per = width // experts
    part = width // dp
    line = Line()

    def order(rel):
        high = rel >> shift
        return (high >> 1) | ((high & 1) << 1), rel & (low - 1)

    def head_body(ids_hbm, cot_hbm, tok_hbm, ctx_hbm, w_out_hbm, *refs):
        outs, copies = refs[: 2 * low + 7], refs[2 * low + 7 :]
        lows, (placed_ref, resid_ref, inv_ref, normed_ref), sends = outs[:low], outs[low : low + 4], outs[low + 4 :]
        held, sems = copies[:5], copies[5]
        me = lax.axis_index("expert")
        ids_ref, ctx_ref, w_out_ref, tok_ref, cot_ref = held
        quarter = width // 4
        rows_of = [slice(i * quarter, (i + 1) * quarter) for i in range(4)]
        pairs = [(ids_hbm, ids_ref), (ctx_hbm, ctx_ref)] + [(w_out_hbm.at[r, :], w_out_ref.at[r, :]) for r in rows_of]
        pairs += [(tok_hbm, tok_ref), (cot_hbm, cot_ref)]
        loads = [pltpu.make_async_copy(src, dst, sems.at[i]) for i, (src, dst) in enumerate(pairs)]
        for load in loads:
            load.start()
        loads[0].wait()
        rows = lax.broadcasted_iota(jnp.int32, (tok, tok), 0)
        cols = lax.broadcasted_iota(jnp.int32, (tok, tok), 1)
        upper = (rows < cols).astype(BF)
        hot = hot_rows(ids_ref, me, experts)
        before = [mm(h.astype(BF), upper) for h in hot]
        first = jnp.sum(hot[0], axis=1, keepdims=True)
        rank = [jnp.sum(before[0] * hot[0], axis=0, keepdims=True),
                jnp.sum((before[1] + first) * hot[1], axis=0, keepdims=True)]
        places, spots = [], []
        for k in range(2):
            block, lower = order(ids_ref[k : k + 1, :] ^ me)
            places.append((block * low + lower) * cap + rank[k].astype(jnp.int32))
            placed_ref[k : k + 1, :] = places[k]
            spots.append((lower * len(masks) + block) * cap + rank[k].astype(jnp.int32))
        loads[1].wait()
        attn = None
        for i, r in enumerate(rows_of):
            loads[2 + i].wait()
            term = mm(ctx_ref[:, r], w_out_ref[r, :])
            attn = term if attn is None else attn + term
        loads[6].wait()
        resid = (tok_ref[...].astype(F32) + attn).astype(BF)
        resid_ref[...] = resid
        resid_f = resid.astype(F32)
        inv = lax.rsqrt(jnp.mean(resid_f * resid_f, axis=1, keepdims=True) + EPSILON)
        inv_ref[...] = inv
        normed = (resid_f * inv).astype(BF)
        normed_ref[...] = normed
        moved = mm(at_rows(places, slots), normed).astype(BF)
        for m in range(low):
            sends[m][...] = moved[m * cap : (m + 1) * cap, :]
        for c in range(1, 4):
            sends[low + c - 1][...] = moved[c * size : (c + 1) * size, :]
        loads[7].wait()
        moved = mm(at_rows(spots, slots), cot_ref[...]).astype(BF)
        each = slots // low
        for m in range(low):
            lows[m][...] = moved[m * each : (m + 1) * each, :]

    outs = line.call(
        head_body,
        [shape((slots // low, width))] * low + [shape((2, tok), jnp.int32)]
        + [shape((tok, width)), shape((tok, 1), F32), shape((tok, width))] + [shape((cap, width))] * low + [shape((size, width))] * 3,
        (ids_t, cotangent, tokens, context, w_out), specs=[HBM] * 5,
        scratch=[pltpu.VMEM((2, tok), jnp.int32), pltpu.VMEM((tok, width), BF), pltpu.VMEM((width, width), BF),
                 pltpu.VMEM((tok, width), BF), pltpu.VMEM((tok, width), BF), DMA((8,))],
        vmem=53 * MIB, name="head")
    cot_low, (placed, resid, inv, normed), sends = outs[:low], outs[low : low + 4], outs[low + 4 :]
    cot_low = [cot_low[0]] + [swap(cot_low[m], "expert", m) for m in range(1, low)]
    norm_zero = [sends[0]] + [swap(sends[m], "expert", m) for m in range(1, low)]
    norm_high = [None] + [swap(sends[low + c - 1], "expert", masks[c] * low) for c in (1, 2, 3)]
    halves = [range(low)[: low // 2], range(low)[low // 2 :]]
    early = line.move(
        *[[(cap, [(norm_zero[m], 0)]) for m in part] for part in halves],
        *[[(cap, [(cot_low[m], c * cap)]) for m in range(low)] for c in range(4)], hold=(weight_in, weight_down), name="pack_zero")
    early, cot_high = early[:2], [swap(x, "expert", masks[c] * low) if masks[c] else x for c, x in enumerate(early[2:])]
    early_far = [swap(x, "dp", far) for x in early]

    whole = lambda *arrays: [(x.shape[0], [(x, 0)]) for x in arrays]
    norm_far, *lows = line.move(
        whole(*early_far),
        *[[(cap, [(norm_high[c], m * cap)]) for c in (1, 2, 3)] for m in range(1, low)], name="pack_norm_y")
    lows = [swap(x, "expert", m + 1) for m, x in enumerate(lows)]
    rest = [(cap, [piece]) for c in (1, 2, 3) for piece in [(norm_high[c], 0)] + [(x, (c - 1) * cap) for x in lows]]
    norm_own, norm_rest = line.move(whole(*early) + rest, rest, name="pack_norm_x")
    norm_far = [norm_far, swap(norm_rest, "dp", far)]
    norm_core = swap(norm_own, "dp", 1)
    block = hidden

    def forward(parts, pieces):
        rows = sum(x.shape[0] for x in parts)
        piece = rows // pieces

        def body(*refs):
            ins = refs[: len(parts)]
            router_ref, in_ref, down_ref, rows_hbm, act_hbm, der_ref, gate_ref = refs[len(parts) : len(parts) + 7]
            sums, (rows_ref, act_ref, total, sems) = refs[len(parts) + 7 : -4], refs[-4:]
            at = 0
            for ref in ins:
                rows_ref[at : at + ref.shape[0], :] = ref[...]
                at += ref.shape[0]
            stores = [pltpu.make_async_copy(rows_ref, rows_hbm, sems.at[0]), pltpu.make_async_copy(act_ref, act_hbm, sems.at[1])]
            stores[0].start()
            for j in range(hidden // block):
                at = slice(j * block, (j + 1) * block)
                value, derivative = gelu_pair(mm(rows_ref[...], in_ref[:, at]))
                act = value.astype(BF)
                act_ref[:, at] = act
                der_ref[:, at] = derivative.astype(BF)
                term = mm(act, down_ref[at, :])
                total[...] = term if j == 0 else total[...] + term
            stores[1].start()
            for i in range(pieces):
                sums[i][...] = total[i * piece : (i + 1) * piece, :].astype(BF)
            logits = mm(rows_ref[...], router_ref[...], NT)
            lanes = lax.broadcasted_iota(jnp.int32, logits.shape, 1)
            picked = jnp.sum(jnp.where(lanes == lax.axis_index("expert"), logits, 0.0), axis=1, keepdims=True)
            gate_ref[...] = jax.nn.sigmoid(picked)
            for store in stores:
                store.wait()

        *results, = line.call(
            body,
            [shape((rows, width)), shape((rows, hidden)), shape((rows, hidden)), shape((rows, 1), F32)]
            + [shape((piece, width))] * pieces,
            (*parts, router_t, weight_in, weight_down),
            out_specs=[HBM] * 2 + [VMEM] * (2 + pieces),
            scratch=[pltpu.VMEM((rows, width), BF), pltpu.VMEM((rows, hidden), BF), pltpu.VMEM((rows, width), F32), DMA((2,))],
            vmem=20 * MIB, name="forward")
        return (*results[:4], results[4:])

    def backward(parts, gate, der, pieces):
        rows = sum(x.shape[0] for x in parts)
        piece = rows // pieces

        def body(*refs):
            ins, refs = refs[: len(parts)], refs[len(parts) :]
            gate_ref, der_ref, in_ref, down_ref, grads_hbm, pre_hbm = refs[:6]
            sums, (grads_ref, pre_ref, total, sems) = refs[6 : 6 + pieces], refs[6 + pieces :]
            first = 0
            for ref in ins:
                at = slice(first, first + ref.shape[0])
                first += ref.shape[0]
                grads_ref[at, :] = (gate_ref[at, :] * ref[...].astype(F32)).astype(BF)
            stores = [pltpu.make_async_copy(grads_ref, grads_hbm, sems.at[0]), pltpu.make_async_copy(pre_ref, pre_hbm, sems.at[1])]
            stores[0].start()
            for j in range(hidden // block):
                at = slice(j * block, (j + 1) * block)
                act_grad = mm(grads_ref[...], down_ref[at, :], NT)
                pre = (act_grad * der_ref[:, at].astype(F32)).astype(BF)
                pre_ref[:, at] = pre
                term = mm(pre, in_ref[:, at], NT)
                total[...] = term if j == 0 else total[...] + term
            stores[1].start()
            for i in range(pieces):
                sums[i][...] = total[i * piece : (i + 1) * piece, :].astype(BF)
            for store in stores:
                store.wait()

        grads, pre, *sums = line.call(
            body,
            [shape((rows, width)), shape((rows, hidden))] + [shape((piece, width))] * pieces,
            (*parts, gate, der, weight_in, weight_down),
            out_specs=[HBM] * 2 + [VMEM] * pieces,
            scratch=[pltpu.VMEM((rows, width), BF), pltpu.VMEM((rows, hidden), BF), pltpu.VMEM((rows, width), F32), DMA((2,))],
            vmem=20 * MIB, name="backward")
        return grads, pre, sums

    half = slots // 2

    def relay(x, pieces):
        each = slots // pieces
        first, second = x[0], x[-1]
        cut = first.shape[0]
        spans = [[(lo, hi) for lo, hi in ((i * each, min((i + 1) * each, cut)), (max(i * each, cut), (i + 1) * each)) if lo < hi]
                 for i in range(pieces)]
        taken = [[(hi - lo, [(first, lo) if hi <= cut else (second, lo - cut)]) for lo, hi in span] for span in spans]
        joined, *parts = line.move(whole(*x), *taken, name="relay")
        return [joined] + [swap(part, "dp", 1) for part in parts]

    own = forward([norm_own], 1)
    cot_own = line.move(whole(*cot_high), flops=WAIT, name="pack_cot_x")[0]
    cot_far = [swap(cot_own, "dp", far)]
    cot_core = swap(cot_own, "dp", 1)
    near = forward([norm_core], 1)
    near_out = swap(near[4][0], "dp", 1)
    whole_far, *pieces_far = relay(norm_far, PIECES)
    away = forward([whole_far], 1)
    cross = forward(pieces_far, PIECES)
    core_out = [swap(x, "dp", 1) for x in cross[4]]
    own_in = backward([cot_own], gate=own[3], der=own[2], pieces=1)
    far_out = line.move([(x.shape[0], [(away[4][0], i * x.shape[0]), (x, 0)]) for i, x in enumerate(core_out)], name="sum_core_out")[0]
    far_out = swap(far_out, "dp", far)
    whole_far, *pieces_far = relay(cot_far, 2)
    near_back = backward([cot_core], gate=near[3], der=near[2], pieces=1)
    near_in = swap(near_back[2][0], "dp", 1)
    away_in = backward([whole_far], gate=away[3], der=away[2], pieces=1)
    cross_back = backward(pieces_far, gate=cross[3], der=cross[2], pieces=2)
    core_in = [swap(x, "dp", 1) for x in cross_back[2]]
    fronts, backs = (own, near, away, cross), (own_in, near_back, away_in, cross_back)
    keep_n, ikeep_n, ikeep_f = own[4][0], own_in[2][0], away_in[2][0]
    far_in = [swap(line.move([(half, [(ikeep_f, 0), (core_in[0], 0)])], name="sum_core_in")[0], "dp", far)]

    def weight_grad(lefts, rights):
        left, right = lefts[0].shape[1], rights[0].shape[1]
        tile = 256 if left % 256 == 0 else left

        def body(*refs):
            count = len(lefts) + len(rights)
            out_hbm, left_ref, right_ref, result, sems = refs[count:]
            loads = []
            for group, ref in ((refs[: len(lefts)], left_ref), (refs[len(lefts) : count], right_ref)):
                at = 0
                for src in group:
                    loads.append(pltpu.make_async_copy(src, ref.at[at : at + src.shape[0], :], sems.at[len(loads)]))
                    loads[-1].start()
                    at += src.shape[0]
            for load in loads:
                load.wait()
            stores = []
            for i in range(left // tile):
                at = slice(i * tile, (i + 1) * tile)
                result[at, :] = mm(left_ref[:, at], right_ref[...], TN).astype(BF)
                stores.append(pltpu.make_async_copy(result.at[at, :], out_hbm.at[at, :], sems.at[count + i]))
                stores[-1].start()
            for store in stores:
                store.wait()

        return line.call(
            body, [shape((left, right))], (*lefts, *rights), specs=[HBM] * (len(lefts) + len(rights)), out_specs=[HBM],
            scratch=[pltpu.VMEM((4 * slots, left), BF), pltpu.VMEM((4 * slots, right), BF), pltpu.VMEM((left, right), BF),
                     DMA((len(lefts) + len(rights) + left // tile,))],
            vmem=20 * MIB, name="weights")[0]

    tile = max(per, LANES)

    def turn_body(ctx_ref, out_ref):
        for i in range(width // tile):
            turned = ctx_ref[:, i * tile : (i + 1) * tile].astype(F32).T.astype(BF)
            for j in range(tile // per):
                spot, lower = order((i * (tile // per) + j) ^ lax.axis_index("expert"))
                at = pl.ds(pl.multiple_of((spot * low + lower) * per, TILE), per)
                out_ref[at, :] = turned[j * per : (j + 1) * per, :]

    context_t = line.call(turn_body, [shape((width, tok))], (context,), name="turn")[0]

    quarter = slots // 4
    sums = line.move(
        *[[(quarter, [(x, c * quarter) for x in (keep_n, near_out, far_out)])] for c in range(4)], name="sum_x_out")
    out_high = [swap(x, "expert", masks[c] * low) if masks[c] else x for c, x in enumerate(sums)]

    far_in.append(swap(line.move([(half, [(ikeep_f, half), (core_in[1], 0)])], name="sum_core_in")[0], "dp", far))

    def gather_in(i):
        terms = lambda at, rows: (rows, [(ikeep_n, i * half + at), (near_in, i * half + at), (far_in[i], at)])
        total, *lows = line.move(
            [terms(0, half)], *[[terms(j * size + m * cap, cap) for j in range(2)] for m in range(1, low)], name="sum_x_in")
        return total, [swap(x, "expert", m + 1) for m, x in enumerate(lows)]

    def send_back(i, total, lows):
        blocks = line.move(
            *[[(cap, [(total, j * size)])] + [(cap, [(x, j * cap)]) for x in lows] for j in range(2)], name="pack_back_z")
        return [swap(b, "expert", masks[c] * low) if masks[c] else b for c, b in zip(chunks[i], blocks)]

    total_a = gather_in(0)
    grad_w_down = weight_grad([f[1] for f in fronts], [b[0] for b in backs])
    total_b = gather_in(1)
    out_low = []
    if low > 1:
        out_low = line.move(*[[(cap, [(x, m * cap)]) for x in out_high] for m in range(1, low)], name="pack_out_y")
    back_in = send_back(0, *total_a)
    if low > 1:
        out_low = line.move(*[[(2 * cap, [(x, i * 2 * cap)])] for x in out_low for i in range(2)], name="pass_out_y")
        out_low = [swap(x, "expert", i // 2 + 1) for i, x in enumerate(out_low)]
    back_in += send_back(1, *total_b)
    back_a = line.move([(x.shape[0], [(x, 0)]) for x in back_in[:2]], name="pack_back")[0]
    back_out = line.move(
        [(cap, [piece]) for c in range(4) for piece in [(out_high[c], 0)] + [(out_low[2 * m + c // 2], c % 2 * cap) for m in range(low - 1)]],
        name="pack_out")

    spare = -(-experts // TILE) * TILE
    span = width + spare

    def combine_body(*refs):
        back_ref, placed_ref, ids_ref, router_ref, resid_ref, cot_ref, normed_ref, out_ref, table_ref, local_ref = refs
        logits = mm(router_ref[...], normed_ref[...], NT)
        gates = [jax.nn.sigmoid(jnp.sum(logits * h, axis=0, keepdims=True)) for h in hot_rows(ids_ref, 0, experts)]
        ids_f = ids_ref[...].astype(F32)
        cols = jnp.concatenate(gates + [ids_f] * 3, axis=0).T
        held = back_ref[...]
        cot_f = cot_ref[...].astype(F32)
        total = resid_ref[...].astype(F32)
        table = jnp.zeros((tok, LANES), F32)
        for k in range(2):
            gate = cols[:, k : k + 1]
            taken = mm(at_rows([placed_ref[k : k + 1, :]], slots), held, TN)
            total = total + gate * taken
            logit = jnp.sum(cot_f * taken, axis=1, keepdims=True) * gate * (1.0 - gate)
            table = table + onehot(cols[:, 2 + k : 3 + k].astype(jnp.int32), LANES) * logit
        out_ref[...] = total.astype(BF)
        table = table.astype(BF)
        table_ref[...] = table
        local_ref[...] = mm(table, normed_ref[...], TN)[:spare, :].astype(BF)

    output, table, local_router = line.call(
        combine_body, [shape((tok, width)), shape((tok, LANES)), shape((spare, width))],
        (*back_out, placed, ids_t, router_t, resid, cotangent, normed),
        name="combine")

    def products(odd, ctx_ref, grad_ref, local_ref, turned, out):
        mine = lax.axis_index("dp")
        for d in range(far):
            at = pl.ds(pl.multiple_of((mine ^ (2 * d + odd)) * part, LANES), part)
            turned[:, d * part : (d + 1) * part] = grad_ref[:, at]
            out[d * span + width : (d + 1) * span, :] = local_ref[:, at]
        for i in range(0, width, part):
            block = mm(ctx_ref[i : i + part, :], turned[...]).astype(BF)
            for d in range(far):
                out[d * span + i : d * span + i + part, :] = block[:, d * part : (d + 1) * part]

    def tail_body(*refs):
        backs = refs[:3]
        (placed_ref, table_ref, router_ref, resid_ref, inv_ref, local_ref, cot_ref, ctx_ref,
         grad_out, grad_ref, send_ref, turned) = refs[3:]
        held = jnp.concatenate([b[...] for b in backs], axis=0)
        where = at_rows([placed_ref[k : k + 1, :] for k in range(2)], slots)
        normed_grad = mm(where, held, TN) + mm(table_ref[:, :experts], router_ref[...])
        resid_f = resid_ref[...].astype(F32)
        inv_col = inv_ref[...]
        mean_term = jnp.mean(normed_grad * resid_f, axis=1, keepdims=True)
        grad_ref[...] = (cot_ref[...].astype(F32) + inv_col * normed_grad
                         - (inv_col * inv_col * inv_col * mean_term) * resid_f).astype(BF)
        grad_out[...] = grad_ref[...]
        products(1, ctx_ref, grad_ref, local_ref, turned, send_ref)

    grad_tokens, grad_near, send = line.call(
        tail_body, [shape((tok, width))] * 2 + [ shape((far * span, part))],
        (back_a, *back_in[2:], placed, table, router_t, resid, inv, local_router, cotangent, context_t),
        scratch=[pltpu.VMEM((tok, far * part), BF)],
        vmem=16 * MIB, name="tail")
    core = swap(send, "dp", 1)

    def keep_body(ctx_ref, grad_ref, local_ref, w_out_ref, grad_ctx_ref, keep_ref, turned):
        products(0, ctx_ref, grad_ref, local_ref, turned, keep_ref)
        grad_ctx_ref[...] = mm(grad_ref[...], w_out_ref[...], NT).astype(BF)

    grad_context, keep = line.call(
        keep_body, [shape((tok, width)), shape((far * span, part))], (context_t, grad_near, local_router, w_out),
        scratch=[pltpu.VMEM((tok, far * part), BF)], vmem=16 * MIB, name="keep")

    spot = lambda d, c, m: d * span + (c * low + m) * per
    two = lambda first: [(keep, first), (core, first)]
    group = [(spare, two(width))]
    sum_x = line.move(
        [(2 * low * per, two(span)), (spare, two(span + width))],
        *[[(per, two(spot(d, c, m))) for d in range(2) for c in (2, 3)] for m in range(1, low)], name="reduce_core")
    grad_w_in = weight_grad([f[0] for f in fronts], [b[1] for b in backs])
    first_x = swap(sum_x[0], "dp", far)
    second_low = [swap(x, "expert", m + 1) for m, x in enumerate(sum_x[1:])]
    first = line.move(
        *[[(per, two(spot(0, c, m)) + [(first_x, (c * low + m) * per)]) for c in (0, 1)]
          + [(spare, two(width) + [(first_x, 2 * low * per)])] for m in range(low)], name="reduce_x")
    first_low = [swap(x, "expert", m) for m, x in enumerate(first) if m]
    second = line.move(
        *[[(per, two(spot(d, c, 0)) + [(x, (d * 2 + i) * per) for x in second_low]) for i, c in enumerate((2, 3))]
          for d in (1, 0)], name="reduce_y")
    second_x = swap(second[0], "dp", far)
    router_terms = [(x, 2 * per) for x in [first[0], *first_low]]
    blocks = line.move(
        *[[(per, [(x, c * per) for x in [first[0], *first_low]]), (spare, router_terms)] for c in (0, 1)],
        *[[(per, [(second[1], c * per), (second_x, c * per)]), (spare, router_terms)] for c in (0, 1)], name="reduce_xy")
    blocks = [blocks[0]] + [swap(blocks[c], "expert", masks[c] * low) for c in (1, 2, 3)]
    own = line.move([(per + spare, [(b, 0) for b in blocks])], name="reduce_z")[0]
    quarters = [own] + [swap(own, "dp", m) for m in range(1, dp)]

    def final_body(*refs):
        me, mine = lax.axis_index("expert"), lax.axis_index("dp")
        out_ref, router_ref = refs[dp:]
        for m in range(dp):
            at = pl.ds(pl.multiple_of((mine ^ m) * part, LANES), part)
            out_ref[:, at] = refs[m][:per, :].astype(F32)
            table = refs[m][per:, :].astype(F32)
            rows = lax.broadcasted_iota(jnp.int32, table.shape, 0)
            router_ref[:, at] = jnp.sum(jnp.where(rows == me, table, 0.0), axis=0, keepdims=True)

    grad_w_out, grad_w_router = line.call(
        final_body, [shape((per, width), F32), shape((1, width), F32)], quarters, name="final")

    return (
        output,
        grad_tokens,
        grad_context,
        grad_w_out,
        grad_w_router.reshape(width, 1),
        grad_w_in.reshape(1, width, hidden),
        grad_w_down.reshape(1, hidden, width),
    )


def solution(mesh):
    split = P(("dp", "expert"), None)
    return jax.shard_map(
        on_device,
        mesh=mesh,
        in_specs=(split, split, P(), P(), split, P("expert", None, "dp"), P("expert", "dp", None), split),
        out_specs=(split, split, split, P("expert", None), P(None, "expert"), P("expert", None, "dp"),
                   P("expert", "dp", None)),
        check_vma=False,
    )
```

```python
import functools

import jax
import jax.numpy as jnp
from jax import lax
from jax.experimental import pallas as pl
from jax.experimental.pallas import tpu as pltpu
from jax.sharding import PartitionSpec as P

GELU_C = 0.7978845608028654
GELU_A = 0.044715
EPSILON = 1e-06
BF = jnp.bfloat16
F32 = jnp.float32
LANES = 128
TILE = 16
MIB = 1024 * 1024
WAIT = 20 * 10**9
PIECES = 4

NN = (((1,), (0,)), ((), ()))
NT = (((1,), (1,)), ((), ()))
TN = (((0,), (0,)), ((), ()))

VMEM = pl.BlockSpec(memory_space=pltpu.VMEM)
ANY = pl.BlockSpec(memory_space=pl.ANY)
HBM = pl.BlockSpec(memory_space=pltpu.HBM)
DMA = pltpu.SemaphoreType.DMA


def mm(a, b, dims=NN):
    return lax.dot_general(a, b, dims, preferred_element_type=F32)


def shape(dims, dtype=BF):
    return jax.ShapeDtypeStruct(dims, dtype)


def gelu_pair(preact):
    square = preact * preact
    tangent = jnp.tanh(GELU_C * (preact + GELU_A * (square * preact)))
    half = 0.5 * (1.0 + tangent)
    derivative = half + (0.5 * GELU_C) * preact * (1.0 - tangent * tangent) * (
        1.0 + 3.0 * GELU_A * square
    )
    return preact * half, derivative


class Line:
    def __init__(self):
        self.last = None

    def call(self, body, outs, args, specs=None, out_specs=None, scratch=(), flops=0, vmem=8 * MIB, name=None):
        args, specs = list(args), list(specs) if specs is not None else [VMEM] * len(args)
        out_specs = list(out_specs) if out_specs is not None else [VMEM] * len(outs)
        count, given = len(args), len(outs)
        if self.last is not None:
            args.append(self.last)
            specs.append(ANY)

        def kernel(*refs):
            results = refs[len(args) :]
            results[given][...] = jnp.zeros((8, LANES), F32)
            body(*refs[:count], *results[:given], *results[given + 1 :])

        *results, self.last = pl.pallas_call(
            kernel,
            out_shape=[*outs, shape((8, LANES), F32)],
            in_specs=specs,
            out_specs=[*out_specs, VMEM],
            scratch_shapes=scratch,
            compiler_params=pltpu.CompilerParams(vmem_limit_bytes=vmem),
            cost_estimate=pl.CostEstimate(flops=flops, bytes_accessed=0, transcendentals=0),
            name=name,
        )(*args)
        return results

    def move(self, *outputs, flops=0, hold=(), name="move"):
        arrays, places = [], {}
        aligned = True
        for pieces in outputs:
            for rows, terms in pieces:
                aligned = aligned and rows % TILE == 0
                for array, first in terms:
                    aligned = aligned and first % TILE == 0
                    if id(array) not in places:
                        places[id(array)] = len(arrays)
                        arrays.append(array)
        width = arrays[0].shape[1]
        if not aligned:
            return [
                jnp.concatenate([
                    added(*[a[f : f + rows] for a, f in terms]) if len(terms) > 1 else terms[0][0][terms[0][1] : terms[0][1] + rows]
                    for rows, terms in pieces
                ])
                for pieces in outputs
            ]

        def body(*refs):
            for pieces, out in zip(outputs, refs[len(arrays) + len(hold) :]):
                at = 0
                for rows, terms in pieces:
                    parts = [refs[places[id(a)]][f : f + rows, :] for a, f in terms]
                    if len(parts) > 1:
                        parts = [functools.reduce(jnp.add, [p.astype(F32) for p in parts]).astype(BF)]
                    out[at : at + rows, :] = parts[0]
                    at += rows

        outs = [shape((sum(rows for rows, _ in pieces), width)) for pieces in outputs]
        return self.call(body, outs, arrays + list(hold), flops=flops, name=name)


def added(*terms):
    return functools.reduce(jnp.add, [t.astype(F32) for t in terms]).astype(BF)


def swap(x, axis, mask):
    return lax.ppermute(x, axis, [(i, i ^ mask) for i in range(lax.axis_size(axis))])


def hot_rows(ids_ref, rel_to, count):
    tok = ids_ref.shape[1]
    rows = lax.broadcasted_iota(jnp.int32, (count, tok), 0)
    return [(rows == (ids_ref[k : k + 1, :] ^ rel_to)).astype(F32) for k in range(2)]


def at_rows(places, total):
    tok = places[0].shape[1]
    rows = lax.broadcasted_iota(jnp.int32, (total, tok), 0)
    return functools.reduce(jnp.add, [(rows == p).astype(F32) for p in places]).astype(BF)


def onehot(column, width):
    lanes = lax.broadcasted_iota(jnp.int32, (column.shape[0], width), 1)
    return (lanes == column).astype(F32)


def on_device(tokens, context, w_out, w_router, expert_ids, w_in, w_down, cotangent):
    tok, width = tokens.shape
    experts = lax.axis_size("expert")
    dp = lax.axis_size("dp")
    far = dp // 2
    cap = 2 * tok // experts
    slots = 2 * tok
    hidden = w_in.shape[2]
    masks = [0, 2, 1, 3]
    low = experts // len(masks)
    shift = low.bit_length() - 1
    chunks = [[0, 1], [2, 3]]
    size = low * cap
    ids_t = expert_ids.T
    router_t = w_router.T
    weight_in, weight_down = w_in[0], w_down[0]
    per = width // experts
    part = width // dp
    line = Line()

    def order(rel):
        high = rel >> shift
        return (high >> 1) | ((high & 1) << 1), rel & (low - 1)

    def head_body(ids_hbm, cot_hbm, tok_hbm, ctx_hbm, w_out_hbm, *refs):
        outs, copies = refs[: 2 * low + 7], refs[2 * low + 7 :]
        lows, (placed_ref, resid_ref, inv_ref, normed_ref), sends = outs[:low], outs[low : low + 4], outs[low + 4 :]
        held, sems = copies[:5], copies[5]
        me = lax.axis_index("expert")
        ids_ref, ctx_ref, w_out_ref, tok_ref, cot_ref = held
        quarter = width // 4
        rows_of = [slice(i * quarter, (i + 1) * quarter) for i in range(4)]
        pairs = [(ids_hbm, ids_ref), (ctx_hbm, ctx_ref)] + [(w_out_hbm.at[r, :], w_out_ref.at[r, :]) for r in rows_of]
        pairs += [(tok_hbm, tok_ref), (cot_hbm, cot_ref)]
        loads = [pltpu.make_async_copy(src, dst, sems.at[i]) for i, (src, dst) in enumerate(pairs)]
        for load in loads:
            load.start()
        loads[0].wait()
        rows = lax.broadcasted_iota(jnp.int32, (tok, tok), 0)
        cols = lax.broadcasted_iota(jnp.int32, (tok, tok), 1)
        upper = (rows < cols).astype(BF)
        hot = hot_rows(ids_ref, me, experts)
        before = [mm(h.astype(BF), upper) for h in hot]
        first = jnp.sum(hot[0], axis=1, keepdims=True)
        rank = [jnp.sum(before[0] * hot[0], axis=0, keepdims=True),
                jnp.sum((before[1] + first) * hot[1], axis=0, keepdims=True)]
        places, spots = [], []
        for k in range(2):
            block, lower = order(ids_ref[k : k + 1, :] ^ me)
            places.append((block * low + lower) * cap + rank[k].astype(jnp.int32))
            placed_ref[k : k + 1, :] = places[k]
            spots.append((lower * len(masks) + block) * cap + rank[k].astype(jnp.int32))
        loads[1].wait()
        attn = None
        for i, r in enumerate(rows_of):
            loads[2 + i].wait()
            term = mm(ctx_ref[:, r], w_out_ref[r, :])
            attn = term if attn is None else attn + term
        loads[6].wait()
        resid = (tok_ref[...].astype(F32) + attn).astype(BF)
        resid_ref[...] = resid
        resid_f = resid.astype(F32)
        inv = lax.rsqrt(jnp.mean(resid_f * resid_f, axis=1, keepdims=True) + EPSILON)
        inv_ref[...] = inv
        normed = (resid_f * inv).astype(BF)
        normed_ref[...] = normed
        moved = mm(at_rows(places, slots), normed).astype(BF)
        for m in range(low):
            sends[m][...] = moved[m * cap : (m + 1) * cap, :]
        for c in range(1, 4):
            sends[low + c - 1][...] = moved[c * size : (c + 1) * size, :]
        loads[7].wait()
        moved = mm(at_rows(spots, slots), cot_ref[...]).astype(BF)
        each = slots // low
        for m in range(low):
            lows[m][...] = moved[m * each : (m + 1) * each, :]

    outs = line.call(
        head_body,
        [shape((slots // low, width))] * low + [shape((2, tok), jnp.int32)]
        + [shape((tok, width)), shape((tok, 1), F32), shape((tok, width))] + [shape((cap, width))] * low + [shape((size, width))] * 3,
        (ids_t, cotangent, tokens, context, w_out), specs=[HBM] * 5,
        scratch=[pltpu.VMEM((2, tok), jnp.int32), pltpu.VMEM((tok, width), BF), pltpu.VMEM((width, width), BF),
                 pltpu.VMEM((tok, width), BF), pltpu.VMEM((tok, width), BF), DMA((8,))],
        vmem=53 * MIB, name="head")
    cot_low, (placed, resid, inv, normed), sends = outs[:low], outs[low : low + 4], outs[low + 4 :]
    cot_low = [cot_low[0]] + [swap(cot_low[m], "expert", m) for m in range(1, low)]
    norm_zero = [sends[0]] + [swap(sends[m], "expert", m) for m in range(1, low)]
    norm_high = [None] + [swap(sends[low + c - 1], "expert", masks[c] * low) for c in (1, 2, 3)]
    halves = [range(low)[: low // 2], range(low)[low // 2 :]]
    early = line.move(
        *[[(cap, [(norm_zero[m], 0)]) for m in part] for part in halves],
        *[[(cap, [(cot_low[m], c * cap)]) for m in range(low)] for c in range(4)], hold=(weight_in, weight_down), name="pack_zero")
    early, cot_high = early[:2], [swap(x, "expert", masks[c] * low) if masks[c] else x for c, x in enumerate(early[2:])]
    early_far = [swap(x, "dp", far) for x in early]

    whole = lambda *arrays: [(x.shape[0], [(x, 0)]) for x in arrays]
    norm_far, *lows = line.move(
        whole(*early_far),
        *[[(cap, [(norm_high[c], m * cap)]) for c in (1, 2, 3)] for m in range(1, low)], name="pack_norm_y")
    lows = [swap(x, "expert", m + 1) for m, x in enumerate(lows)]
    rest = [(cap, [piece]) for c in (1, 2, 3) for piece in [(norm_high[c], 0)] + [(x, (c - 1) * cap) for x in lows]]
    norm_own, norm_rest = line.move(whole(*early) + rest, rest, name="pack_norm_x")
    norm_far = [norm_far, swap(norm_rest, "dp", far)]
    norm_core = swap(norm_own, "dp", 1)
    block = hidden

    def forward(parts, pieces):
        rows = sum(x.shape[0] for x in parts)
        piece = rows // pieces

        def body(*refs):
            ins = refs[: len(parts)]
            router_ref, in_ref, down_ref, rows_hbm, act_hbm, der_ref, gate_ref = refs[len(parts) : len(parts) + 7]
            sums, (rows_ref, act_ref, sems) = refs[len(parts) + 7 : -3], refs[-3:]
            at = 0
            for ref in ins:
                rows_ref[at : at + ref.shape[0], :] = ref[...]
                at += ref.shape[0]
            stores = [pltpu.make_async_copy(rows_ref, rows_hbm, sems.at[0]), pltpu.make_async_copy(act_ref, act_hbm, sems.at[1])]
            stores[0].start()
            for j in range(hidden // block):
                at = slice(j * block, (j + 1) * block)
                value, derivative = gelu_pair(mm(rows_ref[...], in_ref[:, at]))
                act = value.astype(BF)
                act_ref[:, at] = act
                der_ref[:, at] = derivative.astype(BF)
                term = mm(act, down_ref[at, :])
                total = term if j == 0 else total + term
            stores[1].start()
            for i in range(pieces):
                sums[i][...] = total[i * piece : (i + 1) * piece, :].astype(BF)
            logits = mm(rows_ref[...], router_ref[...], NT)
            lanes = lax.broadcasted_iota(jnp.int32, logits.shape, 1)
            picked = jnp.sum(jnp.where(lanes == lax.axis_index("expert"), logits, 0.0), axis=1, keepdims=True)
            gate_ref[...] = jax.nn.sigmoid(picked)
            for store in stores:
                store.wait()

        *results, = line.call(
            body,
            [shape((rows, width)), shape((rows, hidden)), shape((rows, hidden)), shape((rows, 1), F32)]
            + [shape((piece, width))] * pieces,
            (*parts, router_t, weight_in, weight_down),
            out_specs=[HBM] * 2 + [VMEM] * (2 + pieces),
            scratch=[pltpu.VMEM((rows, width), BF), pltpu.VMEM((rows, hidden), BF), DMA((2,))],
            vmem=20 * MIB, name="forward")
        return (*results[:4], results[4:])

    def backward(parts, gate, der, pieces):
        rows = sum(x.shape[0] for x in parts)
        piece = rows // pieces

        def body(*refs):
            ins, refs = refs[: len(parts)], refs[len(parts) :]
            gate_ref, der_ref, in_ref, down_ref, grads_hbm, pre_hbm = refs[:6]
            sums, (grads_ref, pre_ref, sems) = refs[6 : 6 + pieces], refs[6 + pieces :]
            first = 0
            for ref in ins:
                at = slice(first, first + ref.shape[0])
                first += ref.shape[0]
                grads_ref[at, :] = (gate_ref[at, :] * ref[...].astype(F32)).astype(BF)
            stores = [pltpu.make_async_copy(grads_ref, grads_hbm, sems.at[0]), pltpu.make_async_copy(pre_ref, pre_hbm, sems.at[1])]
            stores[0].start()
            for j in range(hidden // block):
                at = slice(j * block, (j + 1) * block)
                act_grad = mm(grads_ref[...], down_ref[at, :], NT)
                pre = (act_grad * der_ref[:, at].astype(F32)).astype(BF)
                pre_ref[:, at] = pre
                term = mm(pre, in_ref[:, at], NT)
                total = term if j == 0 else total + term
            stores[1].start()
            for i in range(pieces):
                sums[i][...] = total[i * piece : (i + 1) * piece, :].astype(BF)
            for store in stores:
                store.wait()

        grads, pre, *sums = line.call(
            body,
            [shape((rows, width)), shape((rows, hidden))] + [shape((piece, width))] * pieces,
            (*parts, gate, der, weight_in, weight_down),
            out_specs=[HBM] * 2 + [VMEM] * pieces,
            scratch=[pltpu.VMEM((rows, width), BF), pltpu.VMEM((rows, hidden), BF), DMA((2,))],
            vmem=20 * MIB, name="backward")
        return grads, pre, sums

    half = slots // 2

    def relay(x, pieces):
        each = slots // pieces
        first, second = x[0], x[-1]
        cut = first.shape[0]
        spans = [[(lo, hi) for lo, hi in ((i * each, min((i + 1) * each, cut)), (max(i * each, cut), (i + 1) * each)) if lo < hi]
                 for i in range(pieces)]
        taken = [[(hi - lo, [(first, lo) if hi <= cut else (second, lo - cut)]) for lo, hi in span] for span in spans]
        joined, *parts = line.move(whole(*x), *taken, name="relay")
        return [joined] + [swap(part, "dp", 1) for part in parts]

    own = forward([norm_own], 1)
    cot_own = line.move(whole(*cot_high), flops=WAIT, name="pack_cot_x")[0]
    cot_far = [swap(cot_own, "dp", far)]
    cot_core = swap(cot_own, "dp", 1)
    near = forward([norm_core], 1)
    near_out = swap(near[4][0], "dp", 1)
    whole_far, *pieces_far = relay(norm_far, PIECES)
    away = forward([whole_far], 1)
    cross = forward(pieces_far, PIECES)
    core_out = [swap(x, "dp", 1) for x in cross[4]]
    own_in = backward([cot_own], gate=own[3], der=own[2], pieces=1)
    far_out = line.move([(x.shape[0], [(away[4][0], i * x.shape[0]), (x, 0)]) for i, x in enumerate(core_out)], name="sum_core_out")[0]
    far_out = swap(far_out, "dp", far)
    whole_far, *pieces_far = relay(cot_far, 2)
    near_back = backward([cot_core], gate=near[3], der=near[2], pieces=1)
    near_in = swap(near_back[2][0], "dp", 1)
    away_in = backward([whole_far], gate=away[3], der=away[2], pieces=1)
    cross_back = backward(pieces_far, gate=cross[3], der=cross[2], pieces=2)
    core_in = [swap(x, "dp", 1) for x in cross_back[2]]
    fronts, backs = (own, near, away, cross), (own_in, near_back, away_in, cross_back)
    keep_n, ikeep_n, ikeep_f = own[4][0], own_in[2][0], away_in[2][0]
    far_in = [swap(line.move([(half, [(ikeep_f, 0), (core_in[0], 0)])], name="sum_core_in")[0], "dp", far)]

    def weight_grad(lefts, rights):
        left, right = lefts[0].shape[1], rights[0].shape[1]
        tile = 256 if left % 256 == 0 else left

        def body(*refs):
            count = len(lefts) + len(rights)
            out_hbm, left_ref, right_ref, result, sems = refs[count:]
            loads = []
            for group, ref in ((refs[: len(lefts)], left_ref), (refs[len(lefts) : count], right_ref)):
                at = 0
                for src in group:
                    loads.append(pltpu.make_async_copy(src, ref.at[at : at + src.shape[0], :], sems.at[len(loads)]))
                    loads[-1].start()
                    at += src.shape[0]
            for load in loads:
                load.wait()
            stores = []
            for i in range(left // tile):
                at = slice(i * tile, (i + 1) * tile)
                result[at, :] = mm(left_ref[:, at], right_ref[...], TN).astype(BF)
                stores.append(pltpu.make_async_copy(result.at[at, :], out_hbm.at[at, :], sems.at[count + i]))
                stores[-1].start()
            for store in stores:
                store.wait()

        return line.call(
            body, [shape((left, right))], (*lefts, *rights), specs=[HBM] * (len(lefts) + len(rights)), out_specs=[HBM],
            scratch=[pltpu.VMEM((4 * slots, left), BF), pltpu.VMEM((4 * slots, right), BF), pltpu.VMEM((left, right), BF),
                     DMA((len(lefts) + len(rights) + left // tile,))],
            vmem=20 * MIB, name="weights")[0]

    tile = max(per, LANES)

    def turn_body(ctx_ref, out_ref):
        for i in range(width // tile):
            turned = ctx_ref[:, i * tile : (i + 1) * tile].astype(F32).T.astype(BF)
            for j in range(tile // per):
                spot, lower = order((i * (tile // per) + j) ^ lax.axis_index("expert"))
                at = pl.ds(pl.multiple_of((spot * low + lower) * per, TILE), per)
                out_ref[at, :] = turned[j * per : (j + 1) * per, :]

    context_t = line.call(turn_body, [shape((width, tok))], (context,), name="turn")[0]

    quarter = slots // 4
    sums = line.move(
        *[[(quarter, [(x, c * quarter) for x in (keep_n, near_out, far_out)])] for c in range(4)], name="sum_x_out")
    out_high = [swap(x, "expert", masks[c] * low) if masks[c] else x for c, x in enumerate(sums)]

    far_in.append(swap(line.move([(half, [(ikeep_f, half), (core_in[1], 0)])], name="sum_core_in")[0], "dp", far))

    def gather_in(i):
        terms = lambda at, rows: (rows, [(ikeep_n, i * half + at), (near_in, i * half + at), (far_in[i], at)])
        total, *lows = line.move(
            [terms(0, half)], *[[terms(j * size + m * cap, cap) for j in range(2)] for m in range(1, low)], name="sum_x_in")
        return total, [swap(x, "expert", m + 1) for m, x in enumerate(lows)]

    def send_back(i, total, lows):
        blocks = line.move(
            *[[(cap, [(total, j * size)])] + [(cap, [(x, j * cap)]) for x in lows] for j in range(2)], name="pack_back_z")
        return [swap(b, "expert", masks[c] * low) if masks[c] else b for c, b in zip(chunks[i], blocks)]

    total_a = gather_in(0)
    grad_w_down = weight_grad([f[1] for f in fronts], [b[0] for b in backs])
    total_b = gather_in(1)
    out_low = []
    if low > 1:
        out_low = line.move(*[[(cap, [(x, m * cap)]) for x in out_high] for m in range(1, low)], name="pack_out_y")
    back_in = send_back(0, *total_a)
    if low > 1:
        out_low = line.move(*[[(2 * cap, [(x, i * 2 * cap)])] for x in out_low for i in range(2)], name="pass_out_y")
        out_low = [swap(x, "expert", i // 2 + 1) for i, x in enumerate(out_low)]
    back_in += send_back(1, *total_b)
    back_a = line.move([(x.shape[0], [(x, 0)]) for x in back_in[:2]], name="pack_back")[0]
    back_out = line.move(
        [(cap, [piece]) for c in range(4) for piece in [(out_high[c], 0)] + [(out_low[2 * m + c // 2], c % 2 * cap) for m in range(low - 1)]],
        name="pack_out")

    spare = -(-experts // TILE) * TILE
    span = width + spare

    def combine_body(*refs):
        back_ref, placed_ref, ids_ref, router_ref, resid_ref, cot_ref, normed_ref, out_ref, table_ref, local_ref = refs
        logits = mm(router_ref[...], normed_ref[...], NT)
        gates = [jax.nn.sigmoid(jnp.sum(logits * h, axis=0, keepdims=True)) for h in hot_rows(ids_ref, 0, experts)]
        ids_f = ids_ref[...].astype(F32)
        cols = jnp.concatenate(gates + [ids_f] * 3, axis=0).T
        held = back_ref[...]
        cot_f = cot_ref[...].astype(F32)
        total = resid_ref[...].astype(F32)
        table = jnp.zeros((tok, LANES), F32)
        for k in range(2):
            gate = cols[:, k : k + 1]
            taken = mm(at_rows([placed_ref[k : k + 1, :]], slots), held, TN)
            total = total + gate * taken
            logit = jnp.sum(cot_f * taken, axis=1, keepdims=True) * gate * (1.0 - gate)
            table = table + onehot(cols[:, 2 + k : 3 + k].astype(jnp.int32), LANES) * logit
        out_ref[...] = total.astype(BF)
        table = table.astype(BF)
        table_ref[...] = table
        local_ref[...] = mm(table, normed_ref[...], TN)[:spare, :].astype(BF)

    output, table, local_router = line.call(
        combine_body, [shape((tok, width)), shape((tok, LANES)), shape((spare, width))],
        (*back_out, placed, ids_t, router_t, resid, cotangent, normed),
        name="combine")

    def products(odd, ctx_ref, grad_ref, local_ref, turned, out):
        mine = lax.axis_index("dp")
        for d in range(far):
            at = pl.ds(pl.multiple_of((mine ^ (2 * d + odd)) * part, LANES), part)
            turned[:, d * part : (d + 1) * part] = grad_ref[:, at]
            out[d * span + width : (d + 1) * span, :] = local_ref[:, at]
        for i in range(0, width, part):
            block = mm(ctx_ref[i : i + part, :], turned[...]).astype(BF)
            for d in range(far):
                out[d * span + i : d * span + i + part, :] = block[:, d * part : (d + 1) * part]

    def tail_body(*refs):
        backs = refs[:3]
        (placed_ref, table_ref, router_ref, resid_ref, inv_ref, local_ref, cot_ref, ctx_ref,
         grad_out, grad_ref, send_ref, turned) = refs[3:]
        held = jnp.concatenate([b[...] for b in backs], axis=0)
        where = at_rows([placed_ref[k : k + 1, :] for k in range(2)], slots)
        normed_grad = mm(where, held, TN) + mm(table_ref[:, :experts], router_ref[...])
        resid_f = resid_ref[...].astype(F32)
        inv_col = inv_ref[...]
        mean_term = jnp.mean(normed_grad * resid_f, axis=1, keepdims=True)
        grad_ref[...] = (cot_ref[...].astype(F32) + inv_col * normed_grad
                         - (inv_col * inv_col * inv_col * mean_term) * resid_f).astype(BF)
        grad_out[...] = grad_ref[...]
        products(1, ctx_ref, grad_ref, local_ref, turned, send_ref)

    grad_tokens, grad_near, send = line.call(
        tail_body, [shape((tok, width))] * 2 + [ shape((far * span, part))],
        (back_a, *back_in[2:], placed, table, router_t, resid, inv, local_router, cotangent, context_t),
        scratch=[pltpu.VMEM((tok, far * part), BF)],
        vmem=16 * MIB, name="tail")
    core = swap(send, "dp", 1)

    def keep_body(ctx_ref, grad_ref, local_ref, w_out_ref, grad_ctx_ref, keep_ref, turned):
        products(0, ctx_ref, grad_ref, local_ref, turned, keep_ref)
        grad_ctx_ref[...] = mm(grad_ref[...], w_out_ref[...], NT).astype(BF)

    grad_context, keep = line.call(
        keep_body, [shape((tok, width)), shape((far * span, part))], (context_t, grad_near, local_router, w_out),
        scratch=[pltpu.VMEM((tok, far * part), BF)], vmem=16 * MIB, name="keep")

    spot = lambda d, c, m: d * span + (c * low + m) * per
    two = lambda first: [(keep, first), (core, first)]
    group = [(spare, two(width))]
    sum_x = line.move(
        [(2 * low * per, two(span)), (spare, two(span + width))],
        *[[(per, two(spot(d, c, m))) for d in range(2) for c in (2, 3)] for m in range(1, low)], name="reduce_core")
    grad_w_in = weight_grad([f[0] for f in fronts], [b[1] for b in backs])
    first_x = swap(sum_x[0], "dp", far)
    second_low = [swap(x, "expert", m + 1) for m, x in enumerate(sum_x[1:])]
    first = line.move(
        *[[(per, two(spot(0, c, m)) + [(first_x, (c * low + m) * per)]) for c in (0, 1)]
          + [(spare, two(width) + [(first_x, 2 * low * per)])] for m in range(low)], name="reduce_x")
    first_low = [swap(x, "expert", m) for m, x in enumerate(first) if m]
    second = line.move(
        *[[(per, two(spot(d, c, 0)) + [(x, (d * 2 + i) * per) for x in second_low]) for i, c in enumerate((2, 3))]
          for d in (1, 0)], name="reduce_y")
    second_x = swap(second[0], "dp", far)
    router_terms = [(x, 2 * per) for x in [first[0], *first_low]]
    blocks = line.move(
        *[[(per, [(x, c * per) for x in [first[0], *first_low]]), (spare, router_terms)] for c in (0, 1)],
        *[[(per, [(second[1], c * per), (second_x, c * per)]), (spare, router_terms)] for c in (0, 1)], name="reduce_xy")
    blocks = [blocks[0]] + [swap(blocks[c], "expert", masks[c] * low) for c in (1, 2, 3)]
    own = line.move([(per + spare, [(b, 0) for b in blocks])], name="reduce_z")[0]
    quarters = [own] + [swap(own, "dp", m) for m in range(1, dp)]

    def final_body(*refs):
        me, mine = lax.axis_index("expert"), lax.axis_index("dp")
        out_ref, router_ref = refs[dp:]
        for m in range(dp):
            at = pl.ds(pl.multiple_of((mine ^ m) * part, LANES), part)
            out_ref[:, at] = refs[m][:per, :].astype(F32)
            table = refs[m][per:, :].astype(F32)
            rows = lax.broadcasted_iota(jnp.int32, table.shape, 0)
            router_ref[:, at] = jnp.sum(jnp.where(rows == me, table, 0.0), axis=0, keepdims=True)

    grad_w_out, grad_w_router = line.call(
        final_body, [shape((per, width), F32), shape((1, width), F32)], quarters, name="final")

    return (
        output,
        grad_tokens,
        grad_context,
        grad_w_out,
        grad_w_router.reshape(width, 1),
        grad_w_in.reshape(1, width, hidden),
        grad_w_down.reshape(1, hidden, width),
    )


def solution(mesh):
    split = P(("dp", "expert"), None)
    return jax.shard_map(
        on_device,
        mesh=mesh,
        in_specs=(split, split, P(), P(), split, P("expert", None, "dp"), P("expert", "dp", None), split),
        out_specs=(split, split, split, P("expert", None), P(None, "expert"), P("expert", None, "dp"),
                   P("expert", "dp", None)),
        check_vma=False,
    )
```
